32 devices in a mesh: lon: 8 (over z, y), lat: 4 (over x, core).
Axes of the slice: x: 2, y: 2, z: 4, core: 2. Of those that a mesh axis runs over, the one named last changes fastest.
Arguments:
- inverse: float32 [16, 8, 128, 128], P('lon', 'lat'), may hold values from -0.1 to 0.2
- vert_diag: float32 [16, 8, 128], P('lon', 'lat'), may hold values from 0.1 to 1
- vert_coup: float32 [16, 8, 128], P('lon', 'lat'), may hold values from 0.5 to 4
- face_east: float32 [16, 8, 128], P('lon', 'lat'), may hold values from 0.3 to 3
- face_north: float32 [16, 8, 128], P('lon', 'lat'), may hold values from 0.3 to 3
- land_mask: int32 [16, 8], P('lon', 'lat'), may hold values 0 or 1
- aggregate: int32 [16, 8], P('lon', 'lat'), may hold values from -1 to 31, as said below
Outputs:
- coarse: float32 [8, 4, 13, 128, 128], P('lon', 'lat')
The draws below stay inside these ranges and needn't reach their ends.
Inputs may be any that keep to these rules, and one draw needn't show every extreme that they name: `aggregate`: each entry is -1 (the column belongs to no coarse column) or the index I * 4 + J of the coarse column (I, J) = (i // 2, j // 2) of its own 2 x 2 block; -1 may occur anywhere and is more frequent in the two fine latitudes nearest each end of the latitude range.
All inputs are finite; a program needn't handle non-finite values. No bound on the sum of `land_mask` on one device may be relied on, other than what follows from the above.
Results may differ from the reference program's by a relative error of at most 0.0002.
Values sent between devices are 32-bit elements; how exact they have to be, the bound alone decides.
No kernel may reach another device: no remote copies, remote signals or barrier semaphores. Data moves between devices by JAX's collectives and lax.ppermute only.
A program may use at most 64 MiB of HBM per device.

```python
import math
import jax
import jax.numpy as jnp
from jax import lax

NZ = 128
NX = 16
NY = 8
NXC = 8
NYC = 4


def draw_inverse(key, part):
    diag_key, entry_key = jax.random.split(jax.random.fold_in(key, 11), 2)
    diagonal = jnp.exp(jax.random.uniform(diag_key, (NX, NY, NZ), jnp.float32, math.log(0.05), math.log(0.2)))
    spread = 0.05 / math.sqrt(NZ)
    entries = jax.random.truncated_normal(entry_key, -4.0, 4.0, (NX, NY, NZ, NZ), jnp.float32) * spread
    identity = jnp.eye(NZ, dtype=jnp.float32)
    return (entries * (1.0 - identity) + diagonal[..., None] * identity).astype(jnp.float32)


def draw_aggregate(key, part):
    lon_index = lax.broadcasted_iota(jnp.int32, (NX, NY), 0)
    lat_index = lax.broadcasted_iota(jnp.int32, (NX, NY), 1)
    natural = lon_index // 2 * NYC + lat_index // 2
    polar = (lat_index < 2) | (lat_index >= NY - 2)
    rolled = jax.random.randint(jax.random.fold_in(key, 23), (NX, NY), 0, 8)
    dropped = jnp.where(polar, rolled < 4, rolled < 1)
    return jnp.where(dropped, -1, natural).astype(jnp.int32)


def set_ends(drawn, rng, least, high):
    extent = drawn.shape
    index_at = [jax.random.randint(jax.random.fold_in(rng, axis), (), 0, extent[axis]) for axis in range(len(extent))]
    drawn = drawn.at[tuple(index_at)].set(least)
    longest = extent.index(max(extent))
    index_at[longest] = (index_at[longest] + 1) % extent[longest]
    return drawn.at[tuple(index_at)].set(high)


def level_of(own_key, extent, cuts, low, high):
    level = 1.0
    for axis_at, parts in cuts:
        heights = jax.random.uniform(jax.random.fold_in(jax.random.fold_in(own_key, 6), axis_at), (parts,), jnp.float32, low / len(cuts), high / len(cuts))
        level = level * jnp.repeat(jnp.exp(heights), extent[axis_at] // parts).reshape((-1,) + (1,) * (len(extent) - 1 - axis_at))
    return level


def setup_inputs(seed: int = 0) -> dict:
    streams_of = jax.random.split(jax.random.key(seed), 8)
    inverse = draw_inverse(jax.random.fold_in(streams_of[7], 71), 0)
    vert_diag = jnp.clip(jnp.exp(math.log(1.0) - 2.3025851 * jax.random.uniform(streams_of[1], (NX, NY, NZ), jnp.float32) ** level_of(streams_of[1], (NX, NY, NZ), ((0, 8), (1, 4)), -0.2, 0.2)), 0.1, 1.0)
    vert_coup = jnp.clip(jnp.exp(math.log(4.0) - 2.0794415 * jax.random.uniform(streams_of[2], (NX, NY, NZ), jnp.float32) ** level_of(streams_of[2], (NX, NY, NZ), ((0, 8), (1, 4)), -0.2, 0.2)), 0.5, 4.0)
    face_east = jnp.clip(jnp.exp(math.log(3.0) - 2.3025851 * jax.random.uniform(streams_of[3], (NX, NY, NZ), jnp.float32) ** level_of(streams_of[3], (NX, NY, NZ), ((0, 8), (1, 4)), -0.2, 0.2)), 0.3, 3.0)
    face_north = jnp.clip(jnp.exp(math.log(3.0) - 2.3025851 * jax.random.uniform(streams_of[4], (NX, NY, NZ), jnp.float32) ** level_of(streams_of[4], (NX, NY, NZ), ((0, 8), (1, 4)), -0.2, 0.2)), 0.3, 3.0)
    land_mask = set_ends((jax.random.randint(streams_of[5], (NX, NY), 0, 8) < 7).astype(jnp.int32), jax.random.fold_in(streams_of[5], 1), 0, 1)
    aggregate = draw_aggregate(jax.random.fold_in(streams_of[7], 71), 0)
    return dict(inverse=inverse, vert_diag=vert_diag, vert_coup=vert_coup, face_east=face_east, face_north=face_north, land_mask=land_mask, aggregate=aggregate)


relax_weight = 0.6
stencil_offsets = [(-2, 0), (-1, -1), (-1, 0), (-1, 1), (0, -2), (0, -1), (0, 0), (0, 1), (0, 2), (1, -1), (1, 0), (1, 1), (2, 0)]

def shift_levels_down(values):
    return jnp.concatenate([jnp.zeros_like(values[..., :1]), values[..., :-1]], axis=-1)

def shift_levels_up(values):
    return jnp.concatenate([values[..., 1:], jnp.zeros_like(values[..., :1])], axis=-1)

def shift_rows_down(blocks):
    return jnp.concatenate([jnp.zeros_like(blocks[..., :1, :]), blocks[..., :-1, :]], axis=-2)

def shift_rows_up(blocks):
    return jnp.concatenate([blocks[..., 1:, :], jnp.zeros_like(blocks[..., :1, :])], axis=-2)

def block_steps(parity_lon, parity_lat):
    lon_step = -1 if parity_lon == 0 else 1
    lat_step = -1 if parity_lat == 0 else 1
    return [(0, 0), (lon_step, 0), (0, lat_step)]

def off_coupling(vertical):
    levels = vertical.shape[-1]
    level_index = lax.broadcasted_iota(jnp.int32, vertical.shape, vertical.ndim - 1)
    return jnp.where(level_index < levels - 1, vertical, jnp.zeros_like(vertical))

def prolong_rows(inverse_block, column_data, parity_lon, parity_lat):
    main_diag = column_data[..., 0, :]
    coupling = off_coupling(column_data[..., 1, :])
    east_weighted = column_data[..., 2, :]
    west_weighted = column_data[..., 3, :]
    north_weighted = column_data[..., 4, :]
    south_weighted = column_data[..., 5, :]
    weights = column_data[..., 8, :]
    same_lon = east_weighted if parity_lon == 0 else west_weighted
    cross_lon = west_weighted if parity_lon == 0 else east_weighted
    same_lat = north_weighted if parity_lat == 0 else south_weighted
    cross_lat = south_weighted if parity_lat == 0 else north_weighted
    diagonal_part = weights * main_diag - same_lon - same_lat
    coupling_below = shift_levels_down(coupling)
    left_cols = shift_levels_down(inverse_block)
    right_cols = shift_levels_up(inverse_block)
    smoothed = inverse_block * diagonal_part[..., None, :] - weights[..., None, :] * (left_cols * coupling_below[..., None, :] + right_cols * coupling[..., None, :])
    levels = inverse_block.shape[-1]
    identity = (lax.broadcasted_iota(jnp.int32, (levels, levels), 0) == lax.broadcasted_iota(jnp.int32, (levels, levels), 1)).astype(jnp.float32)
    own_block = weights[..., None, :] * identity - relax_weight * smoothed
    lon_block = relax_weight * inverse_block * cross_lon[..., None, :]
    lat_block = relax_weight * inverse_block * cross_lat[..., None, :]
    return jnp.stack([own_block, lon_block, lat_block], axis=-3)

def apply_column(column_data, blocks):
    main_diag = column_data[..., 0, :]
    coupling = off_coupling(column_data[..., 1, :])
    coupling_below = shift_levels_down(coupling)
    return main_diag[..., None, :, None] * blocks - coupling_below[..., None, :, None] * shift_rows_down(blocks) - coupling[..., None, :, None] * shift_rows_up(blocks)

def contract(left, right):
    return jnp.einsum('xyrk,xyrl->xykl', left, right, precision=lax.Precision.HIGHEST, preferred_element_type=jnp.float32)

def reference(inverse, vert_diag, vert_coup, face_east, face_north, land_mask, aggregate):
    live_cols = (aggregate >= 0).astype(jnp.float32)
    block_count = live_cols.reshape(NXC, 2, NYC, 2).sum(axis=(1, 3))
    block_count = jnp.repeat(jnp.repeat(block_count, 2, axis=0), 2, axis=1)
    weights = live_cols / jnp.sqrt(jnp.maximum(block_count, 1.0))
    land_open = land_mask.astype(jnp.float32)
    lat_index = lax.broadcasted_iota(jnp.int32, (NX, NY), 1)
    east_open = land_open * jnp.roll(land_open, -1, axis=0)
    north_open = land_open * jnp.roll(land_open, -1, axis=1) * (lat_index < NY - 1).astype(jnp.float32)
    east_face = face_east * east_open[:, :, None]
    north_face = face_north * north_open[:, :, None]
    west_face = jnp.roll(east_face, 1, axis=0)
    south_face = jnp.roll(north_face, 1, axis=1)
    weight_col = jnp.broadcast_to(weights[:, :, None], vert_diag.shape)
    east_weighted = east_face * jnp.roll(weight_col, -1, axis=0)
    west_weighted = west_face * jnp.roll(weight_col, 1, axis=0)
    north_weighted = north_face * jnp.roll(weight_col, -1, axis=1)
    south_weighted = south_face * jnp.roll(weight_col, 1, axis=1)
    main_diag = vert_diag + vert_coup + shift_levels_down(vert_coup) + east_face + west_face + north_face + south_face
    column_data = jnp.stack([main_diag, vert_coup, east_weighted, west_weighted, north_weighted, south_weighted, east_face, north_face, weight_col], axis=2)
    inverse_split = inverse.reshape(NXC, 2, NYC, 2, NZ, NZ)
    data_split = column_data.reshape(NXC, 2, NYC, 2, 9, NZ)
    classes = {}
    data_classes = {}
    for parity_lon in (0, 1):
        for parity_lat in (0, 1):
            class_data = data_split[:, parity_lon, :, parity_lat]
            data_classes[parity_lon, parity_lat] = class_data
            classes[parity_lon, parity_lat] = prolong_rows(inverse_split[:, parity_lon, :, parity_lat], class_data, parity_lon, parity_lat)
    offset_slot = {offset: place for place, offset in enumerate(stencil_offsets)}
    slots = [jnp.zeros((NXC, NYC, NZ, NZ), jnp.float32) for offset in stencil_offsets]

    def add_term(landing, target, term):
        place = offset_slot[target[0] - landing[0], target[1] - landing[1]]
        slots[place] = slots[place] + jnp.roll(term, landing, axis=(0, 1))
    for parity_lon in (0, 1):
        for parity_lat in (0, 1):
            own_rows = classes[parity_lon, parity_lat]
            own_data = data_classes[parity_lon, parity_lat]
            own_applied = apply_column(own_data, own_rows)
            own_steps = block_steps(parity_lon, parity_lat)
            for left_index in range(3):
                for right_index in range(left_index, 3):
                    term = contract(own_rows[:, :, left_index], own_applied[:, :, right_index])
                    add_term(own_steps[left_index], own_steps[right_index], term)
                    if right_index != left_index:
                        add_term(own_steps[right_index], own_steps[left_index], jnp.swapaxes(term, -1, -2))
            for face_dir in (0, 1):
                if face_dir == 0:
                    partner_key = (1 - parity_lon, parity_lat)
                    shift = (parity_lon, 0)
                    face = own_data[:, :, 6]
                else:
                    partner_key = (parity_lon, 1 - parity_lat)
                    shift = (0, parity_lat)
                    face = own_data[:, :, 7]
                partner_rows = classes[partner_key]
                if shift[0] == 1:
                    partner_rows = jnp.roll(partner_rows, -1, axis=0)
                if shift[1] == 1:
                    partner_rows = jnp.roll(partner_rows, -1, axis=1)
                partner_steps = block_steps(partner_key[0], partner_key[1])
                for left_index in range(3):
                    for right_index in range(3):
                        target = (shift[0] + partner_steps[right_index][0], shift[1] + partner_steps[right_index][1])
                        term = -contract(own_rows[:, :, left_index], face[:, :, :, None] * partner_rows[:, :, right_index])
                        add_term(own_steps[left_index], target, term)
                        add_term(target, own_steps[left_index], jnp.swapaxes(term, -1, -2))
    return jnp.stack(slots, axis=2)
```

```python
import functools

import jax
import jax.numpy as jnp
from jax import lax
from jax.experimental import pallas as pl
from jax.experimental.pallas import tpu as pltpu
from jax.sharding import PartitionSpec as P

relax_weight = 0.6
stencil_offsets = [
    (-2, 0),
    (-1, -1),
    (-1, 0),
    (-1, 1),
    (0, -2),
    (0, -1),
    (0, 0),
    (0, 1),
    (0, 2),
    (1, -1),
    (1, 0),
    (1, 1),
    (2, 0),
]
DIAG, UP, DOWN, EAST, NORTH, OPEN, WEIGHT = range(7)
COEF_ROWS = 8


def pair_near(axis):
    count = lax.axis_size(axis)
    return [(i, i ^ 1) for i in range(count) if i ^ 1 < count]


def pair_far(axis, closed):
    count = lax.axis_size(axis)
    pairs = [(i, i - 1 if i % 2 == 0 else i + 1) for i in range(count)]
    if closed:
        return [(i, j % count) for i, j in pairs]
    return [(i, j) for i, j in pairs if 0 <= j < count]


def second(axis, outward):
    count = lax.axis_size(axis)
    return [(i, (i + (2 if (i % 2 == 0) == outward else -2)) % count) for i in range(count)]


def pack_kernel(inverse, vert_diag, vert_coup, face_east, face_north, land, aggregate, payload, coefs):
    levels = inverse.shape[-1]
    lane = lax.broadcasted_iota(jnp.int32, (1, levels), 1)
    live = [
        jnp.where(jnp.full((1, levels), aggregate[q // 2, q % 2]) >= 0, 1.0, 0.0) for q in range(4)
    ]
    count = live[0] + live[1] + live[2] + live[3]
    scale = jnp.sqrt(jnp.maximum(count, 1.0))
    for q in range(4):
        x, y = q // 2, q % 2
        payload[q * levels : (q + 1) * levels, :] = inverse[x, y]
        coupling = vert_coup[x, y : y + 1, :]
        up = jnp.where(lane < levels - 1, coupling, 0.0)
        down = jnp.where(lane > 0, pltpu.roll(coupling, 1, axis=1), 0.0)
        is_open = jnp.full((1, levels), land[x, y]).astype(jnp.float32)
        rows = [
            vert_diag[x, y : y + 1, :] + coupling + down,
            up,
            down,
            face_east[x, y : y + 1, :] * is_open,
            face_north[x, y : y + 1, :] * is_open,
            is_open,
            live[q] / scale,
            jnp.zeros((1, levels), jnp.float32),
        ]
        block = jnp.concatenate(rows, axis=0)
        base = 4 * levels + q * COEF_ROWS
        payload[base : base + COEF_ROWS, :] = block
        coefs[q * COEF_ROWS : (q + 1) * COEF_ROWS, :] = block


def parities():
    even_lon = lax.rem(lax.axis_index("lon"), 2) == 0
    even_lat = lax.rem(lax.axis_index("lat"), 2) == 0
    return even_lon, even_lat


def corner_kernel(lon_near, lon_far, lat_near, lat_far, to_near, to_far):
    even_lon, even_lat = parities()
    rows = lon_near.shape[0]
    levels = lon_near.shape[1]
    coef = slice(4 * levels, rows)
    west = lambda q: jnp.where(
        even_lon,
        lon_far[q * levels : (q + 1) * levels, :],
        lon_near[q * levels : (q + 1) * levels, :],
    )
    east = lambda q: jnp.where(
        even_lon,
        lon_near[q * levels : (q + 1) * levels, :],
        lon_far[q * levels : (q + 1) * levels, :],
    )
    west_low, west_high, east_low, east_high = west(2), west(3), east(0), east(1)
    west_coef = jnp.where(even_lon, lon_far[coef, :], lon_near[coef, :])
    east_coef = jnp.where(even_lon, lon_near[coef, :], lon_far[coef, :])
    size = rows - 4 * levels
    base = 2 * levels
    for out, low, other in ((to_near, jnp.logical_not(even_lat), lat_far), (to_far, even_lat, lat_near)):
        out[:levels, :] = jnp.where(low, west_low, west_high)
        out[levels:base, :] = jnp.where(low, east_low, east_high)
        out[base : base + size, :] = west_coef
        out[base + size : base + 2 * size, :] = east_coef
        out[base + 2 * size : base + 3 * size, :] = other[coef, :]


def split(values):
    high = values.astype(jnp.bfloat16)
    return high, (values - high.astype(jnp.float32)).astype(jnp.bfloat16)


def product(left, right):
    left_high, left_low = split(left)
    right_high, right_low = split(right)
    return jnp.dot(
        jnp.concatenate([left_high, left_high, left_low], axis=1),
        jnp.concatenate([right_high, right_low, right_high], axis=0),
        preferred_element_type=jnp.float32,
    )


def coarse_kernel(own, lon_near, lon_far, lat_near, lat_far, corner_near, corner_far, ring_near, ring_far, out):
    even_lon, even_lat = parities()
    levels = own.shape[1]
    size = 4 * COEF_ROWS
    full = 4 * levels
    half = 2 * levels
    sources = {
        (0, 0): (None, own, own, full),
        (1, 0): (even_lon, lon_near, lon_far, full),
        (-1, 0): (even_lon, lon_far, lon_near, full),
        (0, 1): (even_lat, lat_near, lat_far, full),
        (0, -1): (even_lat, lat_far, lat_near, full),
        (-1, 1): (even_lat, corner_near, corner_far, half),
        (-1, -1): (even_lat, corner_far, corner_near, half),
        (1, 1): (even_lat, corner_near, corner_far, half + size),
        (1, -1): (even_lat, corner_far, corner_near, half + size),
        (0, 2): (even_lat, corner_near, corner_far, half + 2 * size),
        (0, -2): (even_lat, corner_far, corner_near, half + 2 * size),
        (2, 0): (even_lon, ring_near, ring_far, 0),
        (-2, 0): (even_lon, ring_far, ring_near, 0),
    }

    def fetch(device, start, count):
        flag, first, other, _ = sources[device]
        if flag is None:
            return first[start : start + count, :]
        return jnp.where(flag, first[start : start + count, :], other[start : start + count, :])

    coefs = {}
    for device in sources:
        base = sources[device][3]
        coefs[device] = fetch(device, base, size)

    def coef(x, y, row):
        at = (2 * (x % 2) + y % 2) * COEF_ROWS + row
        return coefs[x // 2, y // 2][at : at + 1, :]

    @functools.cache
    def east(x, y):
        return coef(x, y, EAST) * coef(x + 1, y, OPEN)

    @functools.cache
    def north(x, y):
        return coef(x, y, NORTH) * coef(x, y + 1, OPEN)

    @functools.cache
    def main(x, y):
        return coef(x, y, DIAG) + east(x, y) + east(x - 1, y) + north(x, y) + north(x, y - 1)

    def lon_faces(x, y):
        right = east(x, y) * coef(x + 1, y, WEIGHT)
        left = east(x - 1, y) * coef(x - 1, y, WEIGHT)
        return (right, left) if x % 2 == 0 else (left, right)

    def lat_faces(x, y):
        above = north(x, y) * coef(x, y + 1, WEIGHT)
        below = north(x, y - 1) * coef(x, y - 1, WEIGHT)
        return (above, below) if y % 2 == 0 else (below, above)

    def inverse(x, y):
        device = (x // 2, y // 2)
        if device[0] != 0 and device[1] != 0:
            start = 0 if device[0] < 0 else levels
        else:
            start = (2 * (x % 2) + y % 2) * levels
        return fetch(device, start, levels)

    row = lax.broadcasted_iota(jnp.int32, (levels, levels), 0)
    lane = lax.broadcasted_iota(jnp.int32, (levels, levels), 1)

    def own_diag(x, y):
        return coef(x, y, WEIGHT) * main(x, y) - lon_faces(x, y)[0] - lat_faces(x, y)[0]

    def left(values):
        return pltpu.roll(values, 1, axis=1)

    def right(values):
        return pltpu.roll(values, levels - 1, axis=1)

    own_cells = [(x, y) for x in (0, 1) for y in (0, 1)]
    lon_cells = [(x, y) for x in (-1, 2) for y in (0, 1)]
    lat_cells = [(x, y) for x in (0, 1) for y in (-1, 2)]
    rows_t = {}
    for x, y in own_cells:
        block = inverse(x, y)
        weight = coef(x, y, WEIGHT)
        smoothed = (
            block * own_diag(x, y)
            - left(block * (weight * coef(x, y, UP)))
            - right(block * (weight * coef(x, y, DOWN)))
        )
        rows_t[x, y] = (jnp.where(row == lane, weight, 0.0) - relax_weight * smoothed).T
    for x, y in lon_cells:
        rows_t[x, y] = (inverse(x, y) * (relax_weight * lon_faces(x, y)[1])).T
    for x, y in lat_cells:
        rows_t[x, y] = (inverse(x, y) * (relax_weight * lat_faces(x, y)[1])).T

    def residual(x, y):
        total = None
        if (x, y) in rows_t:
            block = rows_t[x, y]
            total = block * main(x, y) - left(block * coef(x, y, UP)) - right(block * coef(x, y, DOWN))
        for near, face in (
            ((x + 1, y), east(x, y)),
            ((x - 1, y), east(x - 1, y)),
            ((x, y + 1), north(x, y)),
            ((x, y - 1), north(x, y - 1)),
        ):
            if near in rows_t:
                term = rows_t[near] * face
                total = -term if total is None else total - term
        return total

    slot_of = {offset: place for place, offset in enumerate(stencil_offsets)}
    started = set()

    def add(target, term):
        place = slot_of[target]
        if target in started:
            out[place] += term
        else:
            out[place] = term
            started.add(target)

    groups = [
        ((0, 0), own_cells),
        ((0, 1), [(x, y) for x in (0, 1) for y in (2, 3)]),
        ((0, -1), [(x, y) for x in (0, 1) for y in (-1, -2)]),
        ((1, 0), [(x, y) for x in (2, 3) for y in (0, 1)]),
        ((-1, 0), [(x, y) for x in (-1, -2) for y in (0, 1)]),
        ((1, 1), [(2, 2)]),
        ((1, -1), [(2, -1)]),
        ((-1, 1), [(-1, 2)]),
        ((-1, -1), [(-1, -1)]),
    ]
    for device, cells in groups:
        straight = down = up = None
        for x, y in cells:
            rest = residual(x, y)
            weight = coef(x, y, WEIGHT)
            smooth = product(rest, inverse(x, y)) * relax_weight
            terms = (
                rest * weight - smooth * own_diag(x, y),
                smooth * (weight * coef(x, y, UP)),
                smooth * (weight * coef(x, y, DOWN)),
            )
            if straight is None:
                straight, up, down = terms
            else:
                straight, up, down = straight + terms[0], up + terms[1], down + terms[2]
            lon_target = (device[0] + (-1 if x % 2 == 0 else 1), device[1])
            lat_target = (device[0], device[1] + (-1 if y % 2 == 0 else 1))
            add(lon_target, smooth * lon_faces(x, y)[1])
            add(lat_target, smooth * lat_faces(x, y)[1])
        add(device, straight + left(up) + right(down))


def local(inverse, vert_diag, vert_coup, face_east, face_north, land_mask, aggregate):
    levels = inverse.shape[-1]
    rows = 4 * (levels + COEF_ROWS)
    vmem = pl.BlockSpec(memory_space=pltpu.VMEM)
    smem = pl.BlockSpec(memory_space=pltpu.SMEM)
    array = lambda count: jax.ShapeDtypeStruct((count, levels), jnp.float32)
    payload, coefs = pl.pallas_call(
        pack_kernel,
        out_shape=(array(rows), array(4 * COEF_ROWS)),
        in_specs=[vmem] * 5 + [smem] * 2,
        out_specs=(vmem, vmem),
    )(inverse, vert_diag, vert_coup, face_east, face_north, land_mask, aggregate)
    lon_near = lax.ppermute(payload, "lon", pair_near("lon"))
    lon_far = lax.ppermute(payload, "lon", pair_far("lon", True))
    lat_near = lax.ppermute(payload, "lat", pair_near("lat"))
    lat_far = lax.ppermute(payload, "lat", pair_far("lat", False))
    ring_near = lax.ppermute(coefs, "lon", second("lon", False))
    ring_far = lax.ppermute(coefs, "lon", second("lon", True))
    corner_rows = 2 * levels + 3 * 4 * COEF_ROWS
    to_near, to_far = pl.pallas_call(
        corner_kernel,
        out_shape=(array(corner_rows), array(corner_rows)),
        in_specs=[vmem] * 4,
        out_specs=(vmem, vmem),
    )(lon_near, lon_far, lat_near, lat_far)
    corner_near = lax.ppermute(to_near, "lat", pair_near("lat"))
    corner_far = lax.ppermute(to_far, "lat", pair_far("lat", False))
    out = pl.pallas_call(
        coarse_kernel,
        out_shape=jax.ShapeDtypeStruct((len(stencil_offsets), levels, levels), jnp.float32),
        in_specs=[vmem] * 9,
        out_specs=vmem,
        compiler_params=pltpu.CompilerParams(vmem_limit_bytes=32 * 1024 * 1024),
    )(payload, lon_near, lon_far, lat_near, lat_far, corner_near, corner_far, ring_near, ring_far)
    return out[None, None]


def solution(mesh):
    return jax.shard_map(
        local,
        mesh=mesh,
        in_specs=(
            P("lon", "lat", None, None),
            P("lon", "lat", None),
            P("lon", "lat", None),
            P("lon", "lat", None),
            P("lon", "lat", None),
            P("lon", "lat"),
            P("lon", "lat"),
        ),
        out_specs=P("lon", "lat", None, None, None),
        check_vma=False,
    )
```

```python
import functools

import jax
import jax.numpy as jnp
from jax import lax
from jax.experimental import pallas as pl
from jax.experimental.pallas import tpu as pltpu
from jax.sharding import PartitionSpec as P

relax_weight = 0.6
stencil_offsets = [
    (-2, 0),
    (-1, -1),
    (-1, 0),
    (-1, 1),
    (0, -2),
    (0, -1),
    (0, 0),
    (0, 1),
    (0, 2),
    (1, -1),
    (1, 0),
    (1, 1),
    (2, 0),
]
DIAG, UP, DOWN, EAST, NORTH, OPEN, WEIGHT = range(7)
COEF_ROWS = 8


def pair_near(axis):
    count = lax.axis_size(axis)
    return [(i, i ^ 1) for i in range(count) if i ^ 1 < count]


def pair_far(axis, closed):
    count = lax.axis_size(axis)
    pairs = [(i, i - 1 if i % 2 == 0 else i + 1) for i in range(count)]
    if closed:
        return [(i, j % count) for i, j in pairs]
    return [(i, j) for i, j in pairs if 0 <= j < count]


def second(axis, outward):
    count = lax.axis_size(axis)
    return [(i, (i + (2 if (i % 2 == 0) == outward else -2)) % count) for i in range(count)]


def pack_kernel(
    inverse_hbm,
    diag_hbm,
    coup_hbm,
    east_hbm,
    north_hbm,
    land_hbm,
    aggregate_hbm,
    both,
    to_near,
    to_far,
    inverse,
    vert_diag,
    vert_coup,
    face_east,
    face_north,
    land,
    aggregate,
    block,
    small_sems,
    sems,
):
    lon = lax.rem(lax.axis_index("lon"), 2)
    levels = inverse.shape[-1]
    whole = pltpu.make_async_copy(inverse_hbm, inverse, small_sems.at[6])
    whole.start()
    small = [
        pltpu.make_async_copy(source, target, small_sems.at[place])
        for place, (source, target) in enumerate(
            (
                (land_hbm, land),
                (aggregate_hbm, aggregate),
                (coup_hbm, vert_coup),
                (diag_hbm, vert_diag),
                (east_hbm, face_east),
                (north_hbm, face_north),
            )
        )
    ]
    for copy in small:
        copy.start()
    copies = []
    for y in range(2):
        rows = pl.ds(y * levels, levels)
        copies.append((inverse.at[1 - lon, y], to_near.at[rows]))
        copies.append((inverse.at[lon, y], to_far.at[rows]))
        for x in range(2):
            copies.append((inverse.at[x, y], both.at[pl.ds((2 * x + y) * levels, levels)]))
    copies = [
        pltpu.make_async_copy(source, target, sems.at[place])
        for place, (source, target) in enumerate(copies)
    ]
    whole.wait()
    for copy in copies:
        copy.start()
    for copy in small:
        copy.wait()
    lane = lax.broadcasted_iota(jnp.int32, (1, levels), 1)
    live = [
        jnp.where(jnp.full((1, levels), aggregate[q // 2, q % 2]) >= 0, 1.0, 0.0) for q in range(4)
    ]
    count = live[0] + live[1] + live[2] + live[3]
    scale = jnp.sqrt(jnp.maximum(count, 1.0))
    for q in range(4):
        x, y = q // 2, q % 2
        coupling = vert_coup[x, y : y + 1, :]
        up = jnp.where(lane < levels - 1, coupling, 0.0)
        down = jnp.where(lane > 0, pltpu.roll(coupling, 1, axis=1), 0.0)
        is_open = jnp.full((1, levels), land[x, y]).astype(jnp.float32)
        rows = [
            vert_diag[x, y : y + 1, :] + coupling + down,
            up,
            down,
            face_east[x, y : y + 1, :] * is_open,
            face_north[x, y : y + 1, :] * is_open,
            is_open,
            live[q] / scale,
            jnp.zeros((1, levels), jnp.float32),
        ]
        block[q * COEF_ROWS : (q + 1) * COEF_ROWS, :] = jnp.concatenate(rows, axis=0)
    size = 4 * COEF_ROWS
    last = [
        pltpu.make_async_copy(block, target.at[pl.ds(base, size)], small_sems.at[place])
        for place, (target, base) in enumerate(
            ((to_near, 2 * levels), (to_far, 2 * levels), (both, 4 * levels))
        )
    ]
    for copy in last:
        copy.start()
    for copy in copies + last:
        copy.wait()


def parities():
    even_lon = lax.rem(lax.axis_index("lon"), 2) == 0
    even_lat = lax.rem(lax.axis_index("lat"), 2) == 0
    return even_lon, even_lat


def wide_kernel(block, ring, wide):
    levels = block.shape[1]
    wide[: 2 * levels, :] = block[: 2 * levels, :]
    wide[2 * levels : block.shape[0], :] = ring[2 * levels :, :]


def corner_kernel(lon_near, lon_far, lat_near, lat_far, to_near, to_far):
    even_lon, even_lat = parities()
    levels = lon_near.shape[1]
    size = 4 * COEF_ROWS
    lon = slice(2 * levels, 2 * levels + size)
    lat = slice(4 * levels, 4 * levels + size)

    def west(rows):
        return jnp.where(even_lon, lon_far[rows, :], lon_near[rows, :])

    def east(rows):
        return jnp.where(even_lon, lon_near[rows, :], lon_far[rows, :])

    low, high = slice(0, levels), slice(levels, 2 * levels)
    base = 2 * levels
    for out, lower, other in ((to_near, jnp.logical_not(even_lat), lat_far), (to_far, even_lat, lat_near)):
        out[:levels, :] = jnp.where(lower, west(low), west(high))
        out[levels:base, :] = jnp.where(lower, east(low), east(high))
        out[base : base + size, :] = west(lon)
        out[base + size : base + 2 * size, :] = east(lon)
        out[base + 2 * size : base + 3 * size, :] = other[lat, :]


def split(values):
    high = values.astype(jnp.bfloat16)
    return high, (values - high.astype(jnp.float32)).astype(jnp.bfloat16)


def product(left, right):
    left_high, left_low = split(left)
    right_high, right_low = split(right)
    return jnp.dot(
        jnp.concatenate([left_high, left_high, left_low], axis=1),
        jnp.concatenate([right_high, right_low, right_high], axis=0),
        preferred_element_type=jnp.float32,
    )


def left(values):
    return pltpu.roll(values, 1, axis=1)


def right(values):
    return pltpu.roll(values, values.shape[1] - 1, axis=1)


class Stencil:
    def __init__(self, own, lon_near, lon_far, wide_near, wide_far, lat_near, lat_far, corner_near=None, corner_far=None):
        even_lon, even_lat = parities()
        levels = own.shape[1]
        size = 4 * COEF_ROWS
        full = 4 * levels
        half = 2 * levels
        self.levels = levels
        self.wide = {3: (even_lon, wide_near, wide_far), -2: (even_lon, wide_far, wide_near)}
        sources = {
            (0, 0): (None, own, own, full),
            (1, 0): (even_lon, lon_near, lon_far, half),
            (-1, 0): (even_lon, lon_far, lon_near, half),
            (0, 1): (even_lat, lat_near, lat_far, full),
            (0, -1): (even_lat, lat_far, lat_near, full),
            (2, 0): (even_lon, wide_near, wide_far, half),
            (-2, 0): (even_lon, wide_far, wide_near, half),
        }
        if corner_near is not None:
            sources |= {
                (-1, 1): (even_lat, corner_near, corner_far, half),
                (-1, -1): (even_lat, corner_far, corner_near, half),
                (1, 1): (even_lat, corner_near, corner_far, half + size),
                (1, -1): (even_lat, corner_far, corner_near, half + size),
                (0, 2): (even_lat, corner_near, corner_far, half + 2 * size),
                (0, -2): (even_lat, corner_far, corner_near, half + 2 * size),
            }
        self.sources = sources
        self.coefs = {place: self.fetch(*source, size) for place, source in sources.items()}
        self.east = functools.cache(self.east)
        self.north = functools.cache(self.north)
        self.main = functools.cache(self.main)

    def fetch(self, flag, first, other, start, count):
        if flag is None:
            return first[start : start + count, :]
        return jnp.where(flag, first[start : start + count, :], other[start : start + count, :])

    def coef(self, x, y, row):
        at = (2 * (x % 2) + y % 2) * COEF_ROWS + row
        return self.coefs[x // 2, y // 2][at : at + 1, :]

    def weight(self, x, y):
        return self.coef(x, y, WEIGHT)

    def east(self, x, y):
        return self.coef(x, y, EAST) * self.coef(x + 1, y, OPEN)

    def north(self, x, y):
        return self.coef(x, y, NORTH) * self.coef(x, y + 1, OPEN)

    def main(self, x, y):
        lon = self.east(x, y) + self.east(x - 1, y)
        return self.coef(x, y, DIAG) + lon + self.north(x, y) + self.north(x, y - 1)

    def lon_faces(self, x, y):
        above = self.east(x, y) * self.weight(x + 1, y)
        below = self.east(x - 1, y) * self.weight(x - 1, y)
        return (above, below) if x % 2 == 0 else (below, above)

    def lat_faces(self, x, y):
        above = self.north(x, y) * self.weight(x, y + 1)
        below = self.north(x, y - 1) * self.weight(x, y - 1)
        return (above, below) if y % 2 == 0 else (below, above)

    def own_diag(self, x, y):
        return (
            self.weight(x, y) * self.main(x, y) - self.lon_faces(x, y)[0] - self.lat_faces(x, y)[0]
        )

    def inverse(self, x, y):
        lon, lat = x // 2, y // 2
        levels = self.levels
        if x in self.wide:
            return self.fetch(*self.wide[x], y % 2 * levels, levels)
        if lon != 0 and lat != 0:
            start = 0 if lon < 0 else levels
        elif lon != 0:
            start = y % 2 * levels
        else:
            start = (2 * (x % 2) + y % 2) * levels
        return self.fetch(*self.sources[lon, lat][:3], start, levels)

    def residual(self, rows_t, x, y):
        total = None
        if (x, y) in rows_t:
            block = rows_t[x, y]
            total = (
                block * self.main(x, y)
                - left(block * self.coef(x, y, UP))
                - right(block * self.coef(x, y, DOWN))
            )
        for near, face in (
            ((x + 1, y), lambda: self.east(x, y)),
            ((x - 1, y), lambda: self.east(x - 1, y)),
            ((x, y + 1), lambda: self.north(x, y)),
            ((x, y - 1), lambda: self.north(x, y - 1)),
        ):
            if near in rows_t:
                term = rows_t[near] * face()
                total = -term if total is None else total - term
        return total


own_cells = [(x, y) for x in (0, 1) for y in (0, 1)]
lon_cells = [(x, y) for x in (-1, 2) for y in (0, 1)]
lat_cells = [(x, y) for x in (0, 1) for y in (-1, 2)]
reach_cells = own_cells + lon_cells + lat_cells
far_cells = [(x, y) for x in (-2, 3) for y in (0, 1)] + [(x, y) for x in (0, 1) for y in (-2, 3)]
groups = {}
for cell in lon_cells + lat_cells + far_cells + [(2, 2), (2, -1), (-1, 2), (-1, -1)]:
    groups.setdefault((cell[0] // 2, cell[1] // 2), []).append(cell)
first_targets = [(0, 0), (1, 0), (-1, 0), (0, 1), (0, -1)]


class Sums:
    def __init__(self, out, targets, started=()):
        self.out = out
        self.slots = {target: place for place, target in enumerate(targets)}
        self.started = set(started)

    def add(self, target, term):
        place = self.slots[target]
        if target in self.started:
            self.out[place] += term
        else:
            self.out[place] = term
            self.started.add(target)


def lateral_targets(x, y):
    lon, lat = x // 2, y // 2
    return (lon + (-1 if x % 2 == 0 else 1), lat), (lon, lat + (-1 if y % 2 == 0 else 1))


def apply_columns(cells, sums, x, y, smooth):
    lon_target, lat_target = lateral_targets(x, y)
    sums.add(lon_target, smooth * cells.lon_faces(x, y)[1])
    sums.add(lat_target, smooth * cells.lat_faces(x, y)[1])
    weight = cells.weight(x, y)
    return (
        smooth * cells.own_diag(x, y),
        smooth * (weight * cells.coef(x, y, UP)),
        smooth * (weight * cells.coef(x, y, DOWN)),
    )


def plus(parts, more):
    return more if parts is None else tuple(a + b for a, b in zip(parts, more))


def close_kernel(*refs):
    cells = Stencil(*refs[:7])
    rows_out, smooth_out, partial = refs[7:]
    levels = cells.levels
    row = lax.broadcasted_iota(jnp.int32, (levels, levels), 0)
    lane = lax.broadcasted_iota(jnp.int32, (levels, levels), 1)
    rows_t = {}
    for x, y in own_cells:
        block = cells.inverse(x, y)
        weight = cells.weight(x, y)
        smoothed = (
            block * cells.own_diag(x, y)
            - left(block * (weight * cells.coef(x, y, UP)))
            - right(block * (weight * cells.coef(x, y, DOWN)))
        )
        rows_t[x, y] = (jnp.where(row == lane, weight, 0.0) - relax_weight * smoothed).T
    for x, y in lon_cells:
        rows_t[x, y] = (cells.inverse(x, y) * (relax_weight * cells.lon_faces(x, y)[1])).T
    for x, y in lat_cells:
        rows_t[x, y] = (cells.inverse(x, y) * (relax_weight * cells.lat_faces(x, y)[1])).T
    for place, cell in enumerate(reach_cells):
        rows_out[place] = rows_t[cell]
    sums = Sums(partial, first_targets)
    parts = None
    for x, y in own_cells:
        rest = cells.residual(rows_t, x, y)
        smooth = product(rest, cells.inverse(x, y)) * relax_weight
        terms = apply_columns(cells, sums, x, y, smooth)
        parts = plus(parts, (rest * cells.weight(x, y) - terms[0],) + terms[1:])
    sums.add((0, 0), parts[0] + left(parts[1]) + right(parts[2]))
    for place, (x, y) in enumerate(far_cells):
        rest = cells.residual(rows_t, x, y)
        smooth_out[place] = product(rest, cells.inverse(x, y)) * relax_weight
        sums.add((x // 2, y // 2), rest * cells.weight(x, y))


def coarse_kernel(*refs):
    cells = Stencil(*refs[:9])
    rows_in, smooth_in, partial, out = refs[9:]
    rows_t = {cell: rows_in[place] for place, cell in enumerate(reach_cells)}
    sums = Sums(out, stencil_offsets)
    for place, target in enumerate(first_targets):
        sums.add(target, partial[place])
    for device, members in groups.items():
        straight = parts = None
        for x, y in members:
            if (x, y) in far_cells:
                smooth = smooth_in[far_cells.index((x, y))]
            else:
                rest = cells.residual(rows_t, x, y)
                smooth = product(rest, cells.inverse(x, y)) * relax_weight
                term = rest * cells.weight(x, y)
                straight = term if straight is None else straight + term
            parts = plus(parts, apply_columns(cells, sums, x, y, smooth))
        sums.add(device, straight - parts[0] + left(parts[1]) + right(parts[2]))


def local(inverse, vert_diag, vert_coup, face_east, face_north, land_mask, aggregate):
    levels = inverse.shape[-1]
    size = 4 * COEF_ROWS
    args = (inverse, vert_diag, vert_coup, face_east, face_north, land_mask, aggregate)
    vmem = pl.BlockSpec(memory_space=pltpu.VMEM)
    params = pltpu.CompilerParams(vmem_limit_bytes=8 * 1024 * 1024)
    array = lambda count: jax.ShapeDtypeStruct((count, levels), jnp.float32)
    cost = lambda size: pl.CostEstimate(flops=size * 10**6, bytes_accessed=size * 10**3, transcendentals=0)
    shapes = [4 * levels + size] + [2 * levels + size] * 2
    both, to_near, to_far = pl.pallas_call(
        pack_kernel,
        out_shape=tuple(array(rows) for rows in shapes),
        in_specs=[pl.BlockSpec(memory_space=pltpu.HBM)] * 7,
        out_specs=(pl.BlockSpec(memory_space=pltpu.HBM),) * 3,
        scratch_shapes=[pltpu.VMEM(arg.shape, arg.dtype) for arg in args[:5]]
        + [pltpu.SMEM(arg.shape, arg.dtype) for arg in args[5:]]
        + [pltpu.VMEM((size, levels), jnp.float32)]
        + [pltpu.SemaphoreType.DMA((7,)), pltpu.SemaphoreType.DMA((8,))],
    )(*args)
    lon_near = lax.ppermute(to_near, "lon", pair_near("lon"))
    lon_far = lax.ppermute(to_far, "lon", pair_far("lon", True))
    lat_near = lax.ppermute(both, "lat", pair_near("lat"))
    lat_far = lax.ppermute(both, "lat", pair_far("lat", False))

    def widened(block, ring, rows):
        return pl.pallas_call(
            wide_kernel,
            out_shape=array(rows),
            in_specs=[vmem] * 2,
            out_specs=vmem,
            compiler_params=params,
        )(block, ring)

    wide_far = lax.ppermute(
        widened(to_near, lon_near, 2 * levels + size + 8), "lon", pair_far("lon", True)
    )
    wide_near = lax.ppermute(widened(to_far, lon_far, 2 * levels + size), "lon", pair_near("lon"))
    corner_rows = 2 * levels + 3 * size
    corner_to_near, corner_to_far = pl.pallas_call(
        corner_kernel,
        out_shape=(array(corner_rows), array(corner_rows)),
        in_specs=[vmem] * 4,
        out_specs=(vmem, vmem),
        compiler_params=params,
    )(lon_near, lon_far, lat_near, lat_far)
    corner_near = lax.ppermute(corner_to_near, "lat", pair_near("lat"))
    corner_far = lax.ppermute(corner_to_far, "lat", pair_far("lat", False))
    blocks = lambda count: jax.ShapeDtypeStruct((count, levels, levels), jnp.float32)
    near_args = (both, lon_near, lon_far, wide_near, wide_far, lat_near, lat_far)
    close = pl.pallas_call(
        close_kernel,
        out_shape=(blocks(len(reach_cells)), blocks(len(far_cells)), blocks(len(first_targets))),
        in_specs=[vmem] * 7,
        out_specs=(vmem,) * 3,
        cost_estimate=cost(50000),
        compiler_params=params,
    )(*near_args)
    out = pl.pallas_call(
        coarse_kernel,
        out_shape=blocks(len(stencil_offsets)),
        in_specs=[vmem] * 12,
        out_specs=vmem,
        compiler_params=params,
    )(*near_args, corner_near, corner_far, *close)
    return out[None, None]


def solution(mesh):
    return jax.shard_map(
        local,
        mesh=mesh,
        in_specs=(
            P("lon", "lat", None, None),
            P("lon", "lat", None),
            P("lon", "lat", None),
            P("lon", "lat", None),
            P("lon", "lat", None),
            P("lon", "lat"),
            P("lon", "lat"),
        ),
        out_specs=P("lon", "lat", None, None, None),
        check_vma=False,
    )
```

```python
import functools

import jax
import jax.numpy as jnp
from jax import lax
from jax.experimental import pallas as pl
from jax.experimental.pallas import tpu as pltpu
from jax.sharding import PartitionSpec as P

relax_weight = 0.6
stencil_offsets = [
    (-2, 0),
    (-1, -1),
    (-1, 0),
    (-1, 1),
    (0, -2),
    (0, -1),
    (0, 0),
    (0, 1),
    (0, 2),
    (1, -1),
    (1, 0),
    (1, 1),
    (2, 0),
]
DIAG, UP, DOWN, EAST, NORTH, OPEN, WEIGHT = range(7)
COEF_ROWS = 8


def pair_near(axis):
    count = lax.axis_size(axis)
    return [(i, i ^ 1) for i in range(count) if i ^ 1 < count]


def pair_far(axis, closed):
    count = lax.axis_size(axis)
    pairs = [(i, i - 1 if i % 2 == 0 else i + 1) for i in range(count)]
    if closed:
        return [(i, j % count) for i, j in pairs]
    return [(i, j) for i, j in pairs if 0 <= j < count]


def second(axis, outward):
    count = lax.axis_size(axis)
    return [(i, (i + (2 if (i % 2 == 0) == outward else -2)) % count) for i in range(count)]


def pack_kernel(
    inverse_hbm,
    diag_hbm,
    coup_hbm,
    east_hbm,
    north_hbm,
    land_hbm,
    aggregate_hbm,
    both,
    to_near,
    to_far,
    inverse,
    vert_diag,
    vert_coup,
    face_east,
    face_north,
    land,
    aggregate,
    small_sems,
):
    lon = lax.rem(lax.axis_index("lon"), 2)
    levels = inverse.shape[-1]
    whole = pltpu.make_async_copy(inverse_hbm, inverse, small_sems.at[6])
    whole.start()
    small = [
        pltpu.make_async_copy(source, target, small_sems.at[place])
        for place, (source, target) in enumerate(
            (
                (land_hbm, land),
                (aggregate_hbm, aggregate),
                (coup_hbm, vert_coup),
                (diag_hbm, vert_diag),
                (east_hbm, face_east),
                (north_hbm, face_north),
            )
        )
    ]
    for copy in small:
        copy.start()
    for copy in small:
        copy.wait()
    lane = lax.broadcasted_iota(jnp.int32, (1, levels), 1)
    live = [
        jnp.where(jnp.full((1, levels), aggregate[q // 2, q % 2]) >= 0, 1.0, 0.0) for q in range(4)
    ]
    count = live[0] + live[1] + live[2] + live[3]
    scale = jnp.sqrt(jnp.maximum(count, 1.0))
    for q in range(4):
        x, y = q // 2, q % 2
        coupling = vert_coup[x, y : y + 1, :]
        up = jnp.where(lane < levels - 1, coupling, 0.0)
        down = jnp.where(lane > 0, pltpu.roll(coupling, 1, axis=1), 0.0)
        is_open = jnp.full((1, levels), land[x, y]).astype(jnp.float32)
        rows = [
            vert_diag[x, y : y + 1, :] + coupling + down,
            up,
            down,
            face_east[x, y : y + 1, :] * is_open,
            face_north[x, y : y + 1, :] * is_open,
            is_open,
            live[q] / scale,
            jnp.zeros((1, levels), jnp.float32),
        ]
        block = jnp.concatenate(rows, axis=0)
        for ref, base in ((both, 4 * levels), (to_near, 2 * levels), (to_far, 2 * levels)):
            ref[base + q * COEF_ROWS : base + (q + 1) * COEF_ROWS, :] = block
    whole.wait()
    even_lon = lon == 0
    for y in range(2):
        low, high = inverse[0, y], inverse[1, y]
        both[y * levels : (y + 1) * levels, :] = low
        both[(2 + y) * levels : (3 + y) * levels, :] = high
        to_near[y * levels : (y + 1) * levels, :] = jnp.where(even_lon, high, low)
        to_far[y * levels : (y + 1) * levels, :] = jnp.where(even_lon, low, high)


def parities():
    even_lon = lax.rem(lax.axis_index("lon"), 2) == 0
    even_lat = lax.rem(lax.axis_index("lat"), 2) == 0
    return even_lon, even_lat


def wide_kernel(facing_far, own, ring, wide):
    even_lon, _ = parities()
    levels = own.shape[1]
    high = jnp.logical_not(even_lon) if facing_far else even_lon
    for y in range(2):
        low_rows = own[y * levels : (y + 1) * levels, :]
        high_rows = own[(2 + y) * levels : (3 + y) * levels, :]
        wide[y * levels : (y + 1) * levels, :] = jnp.where(high, high_rows, low_rows)
    base = 2 * levels
    coef = [ring[base + q * COEF_ROWS : base + (q + 1) * COEF_ROWS, :] for q in range(4)]
    for y in range(2):
        beyond = jnp.where(high, coef[y], coef[2 + y])
        wide[base + y * COEF_ROWS : base + (y + 1) * COEF_ROWS, :] = beyond


def corner_kernel(lon_near, lon_far, lat_near, lat_far, to_near, to_far):
    even_lon, even_lat = parities()
    levels = lon_near.shape[1]
    size = 4 * COEF_ROWS
    lon = slice(2 * levels, 2 * levels + size)
    lat = slice(4 * levels, 4 * levels + size)

    def west(rows):
        return jnp.where(even_lon, lon_far[rows, :], lon_near[rows, :])

    def east(rows):
        return jnp.where(even_lon, lon_near[rows, :], lon_far[rows, :])

    low, high = slice(0, levels), slice(levels, 2 * levels)
    base = 2 * levels
    for out, lower, other in ((to_near, jnp.logical_not(even_lat), lat_far), (to_far, even_lat, lat_near)):
        out[:levels, :] = jnp.where(lower, west(low), west(high))
        out[levels:base, :] = jnp.where(lower, east(low), east(high))
        out[base : base + size, :] = west(lon)
        out[base + size : base + 2 * size, :] = east(lon)
        out[base + 2 * size : base + 3 * size, :] = other[lat, :]


def split(values):
    high = values.astype(jnp.bfloat16)
    return high, (values - high.astype(jnp.float32)).astype(jnp.bfloat16)


def product(left, right):
    left_high, left_low = split(left)
    right_high, right_low = split(right)
    return jnp.dot(
        jnp.concatenate([left_high, left_high, left_low], axis=1),
        jnp.concatenate([right_high, right_low, right_high], axis=0),
        preferred_element_type=jnp.float32,
    )


def left(values):
    return pltpu.roll(values, 1, axis=1)


def right(values):
    return pltpu.roll(values, values.shape[1] - 1, axis=1)


class Stencil:
    def __init__(self, own, lon_near, lon_far, wide_near, wide_far, lat_near, lat_far, corner_near=None, corner_far=None):
        even_lon, even_lat = parities()
        levels = own.shape[1]
        size = 4 * COEF_ROWS
        full = 4 * levels
        half = 2 * levels
        self.levels = levels
        self.wide = {3: (even_lon, wide_near, wide_far), -2: (even_lon, wide_far, wide_near)}
        sources = {
            (0, 0): (None, own, own, full),
            (1, 0): (even_lon, lon_near, lon_far, half),
            (-1, 0): (even_lon, lon_far, lon_near, half),
            (0, 1): (even_lat, lat_near, lat_far, full),
            (0, -1): (even_lat, lat_far, lat_near, full),
        }
        if corner_near is not None:
            sources |= {
                (-1, 1): (even_lat, corner_near, corner_far, half),
                (-1, -1): (even_lat, corner_far, corner_near, half),
                (1, 1): (even_lat, corner_near, corner_far, half + size),
                (1, -1): (even_lat, corner_far, corner_near, half + size),
                (0, 2): (even_lat, corner_near, corner_far, half + 2 * size),
                (0, -2): (even_lat, corner_far, corner_near, half + 2 * size),
            }
        self.sources = sources
        self.coefs = {place: self.fetch(*source, size) for place, source in sources.items()}
        pair = 2 * COEF_ROWS
        for x, source in self.wide.items() if wide_near is not None else ():
            beyond = self.fetch(*source, half, pair)
            self.coefs[2 if x > 0 else -2, 0] = jnp.concatenate([beyond, beyond], axis=0)
        self.east = functools.cache(self.east)
        self.north = functools.cache(self.north)
        self.main = functools.cache(self.main)

    def fetch(self, flag, first, other, start, count):
        if flag is None:
            return first[start : start + count, :]
        return jnp.where(flag, first[start : start + count, :], other[start : start + count, :])

    def coef(self, x, y, row):
        at = (2 * (x % 2) + y % 2) * COEF_ROWS + row
        return self.coefs[x // 2, y // 2][at : at + 1, :]

    def weight(self, x, y):
        return self.coef(x, y, WEIGHT)

    def east(self, x, y):
        return self.coef(x, y, EAST) * self.coef(x + 1, y, OPEN)

    def north(self, x, y):
        return self.coef(x, y, NORTH) * self.coef(x, y + 1, OPEN)

    def main(self, x, y):
        lon = self.east(x, y) + self.east(x - 1, y)
        return self.coef(x, y, DIAG) + lon + self.north(x, y) + self.north(x, y - 1)

    def lon_faces(self, x, y):
        above = self.east(x, y) * self.weight(x + 1, y)
        below = self.east(x - 1, y) * self.weight(x - 1, y)
        return (above, below) if x % 2 == 0 else (below, above)

    def lat_faces(self, x, y):
        above = self.north(x, y) * self.weight(x, y + 1)
        below = self.north(x, y - 1) * self.weight(x, y - 1)
        return (above, below) if y % 2 == 0 else (below, above)

    def own_diag(self, x, y):
        return (
            self.weight(x, y) * self.main(x, y) - self.lon_faces(x, y)[0] - self.lat_faces(x, y)[0]
        )

    def inverse(self, x, y):
        lon, lat = x // 2, y // 2
        levels = self.levels
        if x in self.wide:
            return self.fetch(*self.wide[x], y % 2 * levels, levels)
        if lon != 0 and lat != 0:
            start = 0 if lon < 0 else levels
        elif lon != 0:
            start = y % 2 * levels
        else:
            start = (2 * (x % 2) + y % 2) * levels
        return self.fetch(*self.sources[lon, lat][:3], start, levels)

    def residual(self, rows_t, x, y):
        total = None
        if (x, y) in rows_t:
            block = rows_t[x, y]
            total = (
                block * self.main(x, y)
                - left(block * self.coef(x, y, UP))
                - right(block * self.coef(x, y, DOWN))
            )
        for near, face in (
            ((x + 1, y), lambda: self.east(x, y)),
            ((x - 1, y), lambda: self.east(x - 1, y)),
            ((x, y + 1), lambda: self.north(x, y)),
            ((x, y - 1), lambda: self.north(x, y - 1)),
        ):
            if near in rows_t:
                term = rows_t[near] * face()
                total = -term if total is None else total - term
        return total


own_cells = [(x, y) for x in (0, 1) for y in (0, 1)]
lon_cells = [(x, y) for x in (-1, 2) for y in (0, 1)]
lat_cells = [(x, y) for x in (0, 1) for y in (-1, 2)]
reach_cells = own_cells + lon_cells + lat_cells
lon_far_cells = [(x, y) for x in (-2, 3) for y in (0, 1)]
lat_far_cells = [(x, y) for x in (0, 1) for y in (-2, 3)]
far_cells = lon_far_cells + lat_far_cells
groups = {}
for cell in lon_cells + lat_cells + far_cells + [(2, 2), (2, -1), (-1, 2), (-1, -1)]:
    groups.setdefault((cell[0] // 2, cell[1] // 2), []).append(cell)
first_targets = [(0, 0), (1, 0), (-1, 0), (0, 1), (0, -1)]


class Sums:
    def __init__(self, out, targets, started=()):
        self.out = out
        self.slots = {target: place for place, target in enumerate(targets)}
        self.started = set(started)

    def add(self, target, term):
        place = self.slots[target]
        if target in self.started:
            self.out[place] += term
        else:
            self.out[place] = term
            self.started.add(target)


def lateral_targets(x, y):
    lon, lat = x // 2, y // 2
    return (lon + (-1 if x % 2 == 0 else 1), lat), (lon, lat + (-1 if y % 2 == 0 else 1))


def apply_columns(cells, sums, x, y, smooth):
    lon_target, lat_target = lateral_targets(x, y)
    sums.add(lon_target, smooth * cells.lon_faces(x, y)[1])
    sums.add(lat_target, smooth * cells.lat_faces(x, y)[1])
    weight = cells.weight(x, y)
    return (
        smooth * cells.own_diag(x, y),
        smooth * (weight * cells.coef(x, y, UP)),
        smooth * (weight * cells.coef(x, y, DOWN)),
    )


def plus(parts, more):
    return more if parts is None else tuple(a + b for a, b in zip(parts, more))


def close_kernel(own, lon_near, lon_far, lat_near, lat_far, rows_out, smooth_out, partial):
    cells = Stencil(own, lon_near, lon_far, None, None, lat_near, lat_far)
    levels = cells.levels
    row = lax.broadcasted_iota(jnp.int32, (levels, levels), 0)
    lane = lax.broadcasted_iota(jnp.int32, (levels, levels), 1)
    rows_t = {}
    for x, y in own_cells:
        block = cells.inverse(x, y)
        weight = cells.weight(x, y)
        smoothed = (
            block * cells.own_diag(x, y)
            - left(block * (weight * cells.coef(x, y, UP)))
            - right(block * (weight * cells.coef(x, y, DOWN)))
        )
        rows_t[x, y] = (jnp.where(row == lane, weight, 0.0) - relax_weight * smoothed).T
    for x, y in lon_cells:
        rows_t[x, y] = (cells.inverse(x, y) * (relax_weight * cells.lon_faces(x, y)[1])).T
    for x, y in lat_cells:
        rows_t[x, y] = (cells.inverse(x, y) * (relax_weight * cells.lat_faces(x, y)[1])).T
    for place, cell in enumerate(reach_cells):
        rows_out[place] = rows_t[cell]
    sums = Sums(partial, first_targets)
    parts = None
    for x, y in own_cells:
        rest = cells.residual(rows_t, x, y)
        smooth = product(rest, cells.inverse(x, y)) * relax_weight
        terms = apply_columns(cells, sums, x, y, smooth)
        parts = plus(parts, (rest * cells.weight(x, y) - terms[0],) + terms[1:])
    sums.add((0, 0), parts[0] + left(parts[1]) + right(parts[2]))
    for x, y in far_cells:
        rest = cells.residual(rows_t, x, y)
        sums.add((x // 2, y // 2), rest * cells.weight(x, y))
        if (x, y) in lat_far_cells:
            smooth = product(rest, cells.inverse(x, y)) * relax_weight
            smooth_out[lat_far_cells.index((x, y))] = smooth


def wide_products_kernel(own, lon_near, lon_far, wide_near, wide_far, lat_near, lat_far, rows_in, smooth_out):
    cells = Stencil(own, lon_near, lon_far, wide_near, wide_far, lat_near, lat_far)
    rows_t = {cell: rows_in[place] for place, cell in enumerate(reach_cells) if cell in lon_cells}
    for place, (x, y) in enumerate(lon_far_cells):
        rest = cells.residual(rows_t, x, y)
        smooth_out[place] = product(rest, cells.inverse(x, y)) * relax_weight


def coarse_kernel(*refs):
    cells = Stencil(*refs[:9])
    rows_in, lat_smooth, partial, lon_smooth, out = refs[9:]
    rows_t = {cell: rows_in[place] for place, cell in enumerate(reach_cells)}
    sums = Sums(out, stencil_offsets)
    for place, target in enumerate(first_targets):
        sums.add(target, partial[place])
    for device, members in groups.items():
        straight = parts = None
        for x, y in members:
            if (x, y) in lon_far_cells:
                smooth = lon_smooth[lon_far_cells.index((x, y))]
            elif (x, y) in lat_far_cells:
                smooth = lat_smooth[lat_far_cells.index((x, y))]
            else:
                rest = cells.residual(rows_t, x, y)
                smooth = product(rest, cells.inverse(x, y)) * relax_weight
                term = rest * cells.weight(x, y)
                straight = term if straight is None else straight + term
            parts = plus(parts, apply_columns(cells, sums, x, y, smooth))
        sums.add(device, straight - parts[0] + left(parts[1]) + right(parts[2]))


def local(inverse, vert_diag, vert_coup, face_east, face_north, land_mask, aggregate):
    levels = inverse.shape[-1]
    size = 4 * COEF_ROWS
    args = (inverse, vert_diag, vert_coup, face_east, face_north, land_mask, aggregate)
    vmem = pl.BlockSpec(memory_space=pltpu.VMEM)
    params = pltpu.CompilerParams(vmem_limit_bytes=8 * 1024 * 1024)
    array = lambda count: jax.ShapeDtypeStruct((count, levels), jnp.float32)
    cost = lambda size: pl.CostEstimate(flops=size * 10**6, bytes_accessed=size * 10**3, transcendentals=0)
    shapes = [4 * levels + size] + [2 * levels + size] * 2
    both, to_near, to_far = pl.pallas_call(
        pack_kernel,
        out_shape=tuple(pltpu.VMEM((rows, levels), jnp.float32) for rows in shapes),
        in_specs=[pl.BlockSpec(memory_space=pltpu.HBM)] * 7,
        out_specs=(vmem,) * 3,
        scratch_shapes=[pltpu.VMEM(arg.shape, arg.dtype) for arg in args[:5]]
        + [pltpu.SMEM(arg.shape, arg.dtype) for arg in args[5:]]
        + [pltpu.SemaphoreType.DMA((7,))],
        compiler_params=pltpu.CompilerParams(vmem_limit_bytes=8 * 1024 * 1024),
    )(*(pltpu.with_memory_space_constraint(arg, pltpu.HBM) for arg in args))
    lon_near = lax.ppermute(to_near, "lon", pair_near("lon"))
    lon_far = lax.ppermute(to_far, "lon", pair_far("lon", True))
    lat_near = lax.ppermute(both, "lat", pair_near("lat"))
    lat_far = lax.ppermute(both, "lat", pair_far("lat", False))

    def widened(facing_far, ring, spare, weight):
        return pl.pallas_call(
            functools.partial(wide_kernel, facing_far),
            out_shape=array(2 * (levels + COEF_ROWS) + spare),
            in_specs=[vmem] * 2,
            out_specs=vmem,
            cost_estimate=cost(weight),
            compiler_params=params,
        )(both, ring)

    wide_far = lax.ppermute(widened(False, lon_near, 8, 1000), "lon", pair_far("lon", True))
    wide_near = lax.ppermute(widened(True, lon_far, 0, 8000), "lon", pair_near("lon"))
    corner_rows = 2 * levels + 3 * size
    corner_to_near, corner_to_far = pl.pallas_call(
        corner_kernel,
        out_shape=(array(corner_rows), array(corner_rows)),
        in_specs=[vmem] * 4,
        out_specs=(vmem, vmem),
        compiler_params=params,
    )(lon_near, lon_far, lat_near, lat_far)
    corner_near = lax.ppermute(corner_to_near, "lat", pair_near("lat"))
    corner_far = lax.ppermute(corner_to_far, "lat", pair_far("lat", False))
    blocks = lambda count: jax.ShapeDtypeStruct((count, levels, levels), jnp.float32)
    close = pl.pallas_call(
        close_kernel,
        out_shape=(blocks(len(reach_cells)), blocks(len(lat_far_cells)), blocks(len(first_targets))),
        in_specs=[vmem] * 5,
        out_specs=(vmem,) * 3,
        cost_estimate=cost(1),
        compiler_params=params,
    )(both, lon_near, lon_far, lat_near, lat_far)
    near_args = (both, lon_near, lon_far, wide_near, wide_far, lat_near, lat_far)
    lon_smooth = pl.pallas_call(
        wide_products_kernel,
        out_shape=blocks(len(lon_far_cells)),
        in_specs=[vmem] * 8,
        out_specs=vmem,
        cost_estimate=cost(50000),
        compiler_params=params,
    )(*near_args, close[0])
    out = pl.pallas_call(
        coarse_kernel,
        out_shape=blocks(len(stencil_offsets)),
        in_specs=[vmem] * 13,
        out_specs=vmem,
        compiler_params=params,
    )(*near_args, corner_near, corner_far, *close, lon_smooth)
    return out[None, None]


def solution(mesh):
    return jax.shard_map(
        local,
        mesh=mesh,
        in_specs=(
            P("lon", "lat", None, None),
            P("lon", "lat", None),
            P("lon", "lat", None),
            P("lon", "lat", None),
            P("lon", "lat", None),
            P("lon", "lat"),
            P("lon", "lat"),
        ),
        out_specs=P("lon", "lat", None, None, None),
        check_vma=False,
    )
```

```python
import functools

import jax
import jax.numpy as jnp
from jax import lax
from jax.experimental import pallas as pl
from jax.experimental.pallas import tpu as pltpu
from jax.sharding import PartitionSpec as P

relax_weight = 0.6
stencil_offsets = [
    (-2, 0),
    (-1, -1),
    (-1, 0),
    (-1, 1),
    (0, -2),
    (0, -1),
    (0, 0),
    (0, 1),
    (0, 2),
    (1, -1),
    (1, 0),
    (1, 1),
    (2, 0),
]
DIAG, UP, DOWN, EAST, NORTH, OPEN, WEIGHT = range(7)
COEF_ROWS = 8


def pair_near(axis):
    count = lax.axis_size(axis)
    return [(i, i ^ 1) for i in range(count) if i ^ 1 < count]


def pair_far_closed(axis):
    count = lax.axis_size(axis)
    return [(i, (i - 1 if i % 2 == 0 else i + 1) % count) for i in range(count)]


def exchange_lat_far(values):
    lon_count, lat_count = lax.axis_size("lon"), lax.axis_size("lat")
    pairs = []
    for i in range(lon_count):
        for j in range(lat_count):
            partner = j - 1 if j % 2 == 0 else j + 1
            if 0 <= partner < lat_count:
                pairs.append((i * lat_count + j, i * lat_count + partner))
            elif i ^ 2 < lon_count:
                pairs.append((i * lat_count + j, (i ^ 2) * lat_count + j))
    return lax.ppermute(values, ("lon", "lat"), pairs)


def pack_kernel(
    inverse_hbm,
    diag_hbm,
    coup_hbm,
    east_hbm,
    north_hbm,
    land_hbm,
    aggregate_hbm,
    both,
    to_near,
    to_far,
    inverse,
    vert_diag,
    vert_coup,
    face_east,
    face_north,
    land,
    aggregate,
    small_sems,
):
    lon = lax.rem(lax.axis_index("lon"), 2)
    levels = inverse.shape[-1]
    whole = pltpu.make_async_copy(inverse_hbm, inverse, small_sems.at[6])
    whole.start()
    small = [
        pltpu.make_async_copy(source, target, small_sems.at[place])
        for place, (source, target) in enumerate(
            (
                (land_hbm, land),
                (aggregate_hbm, aggregate),
                (coup_hbm, vert_coup),
                (diag_hbm, vert_diag),
                (east_hbm, face_east),
                (north_hbm, face_north),
            )
        )
    ]
    for copy in small:
        copy.start()
    for copy in small:
        copy.wait()
    lane = lax.broadcasted_iota(jnp.int32, (1, levels), 1)
    live = [
        jnp.where(jnp.full((1, levels), aggregate[q // 2, q % 2]) >= 0, 1.0, 0.0) for q in range(4)
    ]
    count = live[0] + live[1] + live[2] + live[3]
    scale = jnp.sqrt(jnp.maximum(count, 1.0))
    for q in range(4):
        x, y = q // 2, q % 2
        coupling = vert_coup[x, y : y + 1, :]
        up = jnp.where(lane < levels - 1, coupling, 0.0)
        down = jnp.where(lane > 0, pltpu.roll(coupling, 1, axis=1), 0.0)
        is_open = jnp.full((1, levels), land[x, y]).astype(jnp.float32)
        rows = [
            vert_diag[x, y : y + 1, :] + coupling + down,
            up,
            down,
            face_east[x, y : y + 1, :] * is_open,
            face_north[x, y : y + 1, :] * is_open,
            is_open,
            live[q] / scale,
            jnp.zeros((1, levels), jnp.float32),
        ]
        block = jnp.concatenate(rows, axis=0)
        for ref, base in ((both, 4 * levels), (to_near, 2 * levels), (to_far, 2 * levels)):
            ref[base + q * COEF_ROWS : base + (q + 1) * COEF_ROWS, :] = block
    whole.wait()
    even_lon = lon == 0
    for y in range(2):
        low, high = inverse[0, y], inverse[1, y]
        both[y * levels : (y + 1) * levels, :] = low
        both[(2 + y) * levels : (3 + y) * levels, :] = high
        to_near[y * levels : (y + 1) * levels, :] = jnp.where(even_lon, high, low)
        to_far[y * levels : (y + 1) * levels, :] = jnp.where(even_lon, low, high)


def parities():
    even_lon = lax.rem(lax.axis_index("lon"), 2) == 0
    even_lat = lax.rem(lax.axis_index("lat"), 2) == 0
    return even_lon, even_lat


def has_lat_far():
    index = lax.axis_index("lat")
    return index != jnp.where(lax.rem(index, 2) == 0, 0, lax.axis_size("lat") - 1)


def wide_kernel(facing_far, own, ring, wide):
    even_lon, _ = parities()
    levels = own.shape[1]
    high = jnp.logical_not(even_lon) if facing_far else even_lon
    for y in range(2):
        low_rows = own[y * levels : (y + 1) * levels, :]
        high_rows = own[(2 + y) * levels : (3 + y) * levels, :]
        wide[y * levels : (y + 1) * levels, :] = jnp.where(high, high_rows, low_rows)
    base = 2 * levels
    coef = [ring[base + q * COEF_ROWS : base + (q + 1) * COEF_ROWS, :] for q in range(4)]
    for y in range(2):
        beyond = jnp.where(high, coef[y], coef[2 + y])
        wide[base + y * COEF_ROWS : base + (y + 1) * COEF_ROWS, :] = beyond


def corner_kernel(lon_near, lon_far, lat_near, lat_far, to_near, to_far):
    even_lon, even_lat = parities()
    levels = lon_near.shape[1]
    size = 4 * COEF_ROWS
    lon = slice(2 * levels, 2 * levels + size)
    lat = slice(4 * levels, 4 * levels + size)

    def west(rows):
        return jnp.where(even_lon, lon_far[rows, :], lon_near[rows, :])

    def east(rows):
        return jnp.where(even_lon, lon_near[rows, :], lon_far[rows, :])

    low, high = slice(0, levels), slice(levels, 2 * levels)
    base = 2 * levels
    beyond = jnp.where(has_lat_far(), lat_far[lat, :], 0.0)
    for out, lower, other in (
        (to_near, jnp.logical_not(even_lat), beyond),
        (to_far, even_lat, lat_near[lat, :]),
    ):
        out[:levels, :] = jnp.where(lower, west(low), west(high))
        out[levels:base, :] = jnp.where(lower, east(low), east(high))
        out[base : base + size, :] = west(lon)
        out[base + size : base + 2 * size, :] = east(lon)
        out[base + 2 * size : base + 3 * size, :] = other


def split(values):
    high = values.astype(jnp.bfloat16)
    return high, (values - high.astype(jnp.float32)).astype(jnp.bfloat16)


def product(left, right):
    left_high, left_low = split(left)
    right_high, right_low = split(right)
    return jnp.dot(
        jnp.concatenate([left_high, left_high, left_low], axis=1),
        jnp.concatenate([right_high, right_low, right_high], axis=0),
        preferred_element_type=jnp.float32,
    )


def left(values):
    return pltpu.roll(values, 1, axis=1)


def right(values):
    return pltpu.roll(values, values.shape[1] - 1, axis=1)


class Stencil:
    def __init__(self, own, lon_near, lon_far, wide_near, wide_far, lat_near, lat_far, corner_near=None, corner_far=None):
        even_lon, even_lat = parities()
        levels = own.shape[1]
        size = 4 * COEF_ROWS
        full = 4 * levels
        half = 2 * levels
        self.levels = levels
        self.wide = {3: (even_lon, wide_near, wide_far), -2: (even_lon, wide_far, wide_near)}
        sources = {
            (0, 0): (None, own, own, full),
            (1, 0): (even_lon, lon_near, lon_far, half),
            (-1, 0): (even_lon, lon_far, lon_near, half),
            (0, 1): (even_lat, lat_near, lat_far, full),
            (0, -1): (even_lat, lat_far, lat_near, full),
        }
        if corner_near is not None:
            sources |= {
                (-1, 1): (even_lat, corner_near, corner_far, half),
                (-1, -1): (even_lat, corner_far, corner_near, half),
                (1, 1): (even_lat, corner_near, corner_far, half + size),
                (1, -1): (even_lat, corner_far, corner_near, half + size),
                (0, 2): (even_lat, corner_near, corner_far, half + 2 * size),
                (0, -2): (even_lat, corner_far, corner_near, half + 2 * size),
            }
        self.sources = sources
        self.coefs = {place: self.fetch(*source, size) for place, source in sources.items()}
        far = has_lat_far()
        keep = {1: jnp.logical_or(even_lat, far), -1: jnp.logical_or(jnp.logical_not(even_lat), far)}
        for place in sources:
            if place[1] != 0:
                inside = keep[1 if place[1] > 0 else -1]
                self.coefs[place] = jnp.where(inside, self.coefs[place], 0.0)
        pair = 2 * COEF_ROWS
        for x, source in self.wide.items() if wide_near is not None else ():
            beyond = self.fetch(*source, half, pair)
            self.coefs[2 if x > 0 else -2, 0] = jnp.concatenate([beyond, beyond], axis=0)
        self.east = functools.cache(self.east)
        self.north = functools.cache(self.north)
        self.main = functools.cache(self.main)

    def fetch(self, flag, first, other, start, count):
        if flag is None:
            return first[start : start + count, :]
        return jnp.where(flag, first[start : start + count, :], other[start : start + count, :])

    def coef(self, x, y, row):
        at = (2 * (x % 2) + y % 2) * COEF_ROWS + row
        return self.coefs[x // 2, y // 2][at : at + 1, :]

    def weight(self, x, y):
        return self.coef(x, y, WEIGHT)

    def east(self, x, y):
        return self.coef(x, y, EAST) * self.coef(x + 1, y, OPEN)

    def north(self, x, y):
        return self.coef(x, y, NORTH) * self.coef(x, y + 1, OPEN)

    def main(self, x, y):
        lon = self.east(x, y) + self.east(x - 1, y)
        return self.coef(x, y, DIAG) + lon + self.north(x, y) + self.north(x, y - 1)

    def lon_faces(self, x, y):
        above = self.east(x, y) * self.weight(x + 1, y)
        below = self.east(x - 1, y) * self.weight(x - 1, y)
        return (above, below) if x % 2 == 0 else (below, above)

    def lat_faces(self, x, y):
        above = self.north(x, y) * self.weight(x, y + 1)
        below = self.north(x, y - 1) * self.weight(x, y - 1)
        return (above, below) if y % 2 == 0 else (below, above)

    def own_diag(self, x, y):
        return (
            self.weight(x, y) * self.main(x, y) - self.lon_faces(x, y)[0] - self.lat_faces(x, y)[0]
        )

    def inverse(self, x, y):
        lon, lat = x // 2, y // 2
        levels = self.levels
        if x in self.wide:
            return self.fetch(*self.wide[x], y % 2 * levels, levels)
        if lon != 0 and lat != 0:
            start = 0 if lon < 0 else levels
        elif lon != 0:
            start = y % 2 * levels
        else:
            start = (2 * (x % 2) + y % 2) * levels
        return self.fetch(*self.sources[lon, lat][:3], start, levels)

    def residual(self, rows_t, x, y):
        total = None
        if (x, y) in rows_t:
            block = rows_t[x, y]
            total = (
                block * self.main(x, y)
                - left(block * self.coef(x, y, UP))
                - right(block * self.coef(x, y, DOWN))
            )
        for near, face in (
            ((x + 1, y), lambda: self.east(x, y)),
            ((x - 1, y), lambda: self.east(x - 1, y)),
            ((x, y + 1), lambda: self.north(x, y)),
            ((x, y - 1), lambda: self.north(x, y - 1)),
        ):
            if near in rows_t:
                term = rows_t[near] * face()
                total = -term if total is None else total - term
        return total


own_cells = [(x, y) for x in (0, 1) for y in (0, 1)]
lon_cells = [(x, y) for x in (-1, 2) for y in (0, 1)]
lat_cells = [(x, y) for x in (0, 1) for y in (-1, 2)]
reach_cells = own_cells + lon_cells + lat_cells
lon_far_cells = [(x, y) for x in (-2, 3) for y in (0, 1)]
lat_far_cells = [(x, y) for x in (0, 1) for y in (-2, 3)]
far_cells = lon_far_cells + lat_far_cells
groups = {}
for cell in lon_cells + lat_cells + far_cells + [(2, 2), (2, -1), (-1, 2), (-1, -1)]:
    groups.setdefault((cell[0] // 2, cell[1] // 2), []).append(cell)
first_targets = [(0, 0), (1, 0), (-1, 0), (0, 1), (0, -1)]


class Sums:
    def __init__(self, out, targets, started=()):
        self.out = out
        self.slots = {target: place for place, target in enumerate(targets)}
        self.started = set(started)

    def add(self, target, term):
        place = self.slots[target]
        if target in self.started:
            self.out[place] += term
        else:
            self.out[place] = term
            self.started.add(target)


def lateral_targets(x, y):
    lon, lat = x // 2, y // 2
    return (lon + (-1 if x % 2 == 0 else 1), lat), (lon, lat + (-1 if y % 2 == 0 else 1))


def apply_columns(cells, sums, x, y, smooth):
    lon_target, lat_target = lateral_targets(x, y)
    sums.add(lon_target, smooth * cells.lon_faces(x, y)[1])
    sums.add(lat_target, smooth * cells.lat_faces(x, y)[1])
    weight = cells.weight(x, y)
    return (
        smooth * cells.own_diag(x, y),
        smooth * (weight * cells.coef(x, y, UP)),
        smooth * (weight * cells.coef(x, y, DOWN)),
    )


def plus(parts, more):
    return more if parts is None else tuple(a + b for a, b in zip(parts, more))


def close_kernel(own, lon_near, lon_far, lat_near, lat_far, rows_out, smooth_out, partial):
    cells = Stencil(own, lon_near, lon_far, None, None, lat_near, lat_far)
    levels = cells.levels
    row = lax.broadcasted_iota(jnp.int32, (levels, levels), 0)
    lane = lax.broadcasted_iota(jnp.int32, (levels, levels), 1)
    rows_t = {}
    for x, y in own_cells:
        block = cells.inverse(x, y)
        weight = cells.weight(x, y)
        smoothed = (
            block * cells.own_diag(x, y)
            - left(block * (weight * cells.coef(x, y, UP)))
            - right(block * (weight * cells.coef(x, y, DOWN)))
        )
        rows_t[x, y] = (jnp.where(row == lane, weight, 0.0) - relax_weight * smoothed).T
    for x, y in lon_cells:
        rows_t[x, y] = (cells.inverse(x, y) * (relax_weight * cells.lon_faces(x, y)[1])).T
    for x, y in lat_cells:
        rows_t[x, y] = (cells.inverse(x, y) * (relax_weight * cells.lat_faces(x, y)[1])).T
    for place, cell in enumerate(reach_cells):
        rows_out[place] = rows_t[cell]
    sums = Sums(partial, first_targets)
    parts = None
    for x, y in own_cells:
        rest = cells.residual(rows_t, x, y)
        smooth = product(rest, cells.inverse(x, y)) * relax_weight
        terms = apply_columns(cells, sums, x, y, smooth)
        parts = plus(parts, (rest * cells.weight(x, y) - terms[0],) + terms[1:])
    sums.add((0, 0), parts[0] + left(parts[1]) + right(parts[2]))
    for x, y in far_cells:
        rest = cells.residual(rows_t, x, y)
        sums.add((x // 2, y // 2), rest * cells.weight(x, y))
        if (x, y) in lat_far_cells:
            smooth = product(rest, cells.inverse(x, y)) * relax_weight
            smooth_out[lat_far_cells.index((x, y))] = smooth


def wide_products_kernel(own, lon_near, lon_far, wide_near, wide_far, lat_near, lat_far, rows_in, smooth_out):
    cells = Stencil(own, lon_near, lon_far, wide_near, wide_far, lat_near, lat_far)
    rows_t = {cell: rows_in[place] for place, cell in enumerate(reach_cells) if cell in lon_cells}
    for place, (x, y) in enumerate(lon_far_cells):
        rest = cells.residual(rows_t, x, y)
        smooth_out[place] = product(rest, cells.inverse(x, y)) * relax_weight


def coarse_kernel(*refs):
    cells = Stencil(*refs[:9])
    rows_in, lat_smooth, partial, lon_smooth, out = refs[9:]
    rows_t = {cell: rows_in[place] for place, cell in enumerate(reach_cells)}
    sums = Sums(out, stencil_offsets)
    for place, target in enumerate(first_targets):
        sums.add(target, partial[place])
    for device, members in groups.items():
        straight = parts = None
        for x, y in members:
            if (x, y) in lon_far_cells:
                smooth = lon_smooth[lon_far_cells.index((x, y))]
            elif (x, y) in lat_far_cells:
                smooth = lat_smooth[lat_far_cells.index((x, y))]
            else:
                rest = cells.residual(rows_t, x, y)
                smooth = product(rest, cells.inverse(x, y)) * relax_weight
                term = rest * cells.weight(x, y)
                straight = term if straight is None else straight + term
            parts = plus(parts, apply_columns(cells, sums, x, y, smooth))
        sums.add(device, straight - parts[0] + left(parts[1]) + right(parts[2]))


def local(inverse, vert_diag, vert_coup, face_east, face_north, land_mask, aggregate):
    levels = inverse.shape[-1]
    size = 4 * COEF_ROWS
    args = (inverse, vert_diag, vert_coup, face_east, face_north, land_mask, aggregate)
    vmem = pl.BlockSpec(memory_space=pltpu.VMEM)
    params = pltpu.CompilerParams(vmem_limit_bytes=8 * 1024 * 1024)
    array = lambda count: jax.ShapeDtypeStruct((count, levels), jnp.float32)
    cost = lambda size: pl.CostEstimate(flops=size * 10**6, bytes_accessed=size * 10**3, transcendentals=0)
    shapes = [4 * levels + size] + [2 * levels + size] * 2
    both, to_near, to_far = pl.pallas_call(
        pack_kernel,
        out_shape=tuple(pltpu.VMEM((rows, levels), jnp.float32) for rows in shapes),
        in_specs=[pl.BlockSpec(memory_space=pltpu.HBM)] * 7,
        out_specs=(vmem,) * 3,
        scratch_shapes=[pltpu.VMEM(arg.shape, arg.dtype) for arg in args[:5]]
        + [pltpu.SMEM(arg.shape, arg.dtype) for arg in args[5:]]
        + [pltpu.SemaphoreType.DMA((7,))],
        compiler_params=pltpu.CompilerParams(vmem_limit_bytes=8 * 1024 * 1024),
    )(*(pltpu.with_memory_space_constraint(arg, pltpu.HBM) for arg in args))
    lon_near = lax.ppermute(to_near, "lon", pair_near("lon"))
    lon_far = lax.ppermute(to_far, "lon", pair_far_closed("lon"))
    lat_near = lax.ppermute(both, "lat", pair_near("lat"))
    lat_far = exchange_lat_far(both)

    def widened(facing_far, ring, spare, weight):
        return pl.pallas_call(
            functools.partial(wide_kernel, facing_far),
            out_shape=array(2 * (levels + COEF_ROWS) + spare),
            in_specs=[vmem] * 2,
            out_specs=vmem,
            cost_estimate=cost(weight),
            compiler_params=params,
        )(both, ring)

    wide_far = lax.ppermute(widened(False, lon_near, 8, 1000), "lon", pair_far_closed("lon"))
    wide_near = lax.ppermute(widened(True, lon_far, 0, 8000), "lon", pair_near("lon"))
    corner_rows = 2 * levels + 3 * size
    corner_to_near, corner_to_far = pl.pallas_call(
        corner_kernel,
        out_shape=(array(corner_rows), array(corner_rows)),
        in_specs=[vmem] * 4,
        out_specs=(vmem, vmem),
        compiler_params=params,
    )(lon_near, lon_far, lat_near, lat_far)
    corner_near = lax.ppermute(corner_to_near, "lat", pair_near("lat"))
    corner_far = exchange_lat_far(corner_to_far)
    blocks = lambda count: jax.ShapeDtypeStruct((count, levels, levels), jnp.float32)
    close = pl.pallas_call(
        close_kernel,
        out_shape=(blocks(len(reach_cells)), blocks(len(lat_far_cells)), blocks(len(first_targets))),
        in_specs=[vmem] * 5,
        out_specs=(vmem,) * 3,
        cost_estimate=cost(1),
        compiler_params=params,
    )(both, lon_near, lon_far, lat_near, lat_far)
    near_args = (both, lon_near, lon_far, wide_near, wide_far, lat_near, lat_far)
    lon_smooth = pl.pallas_call(
        wide_products_kernel,
        out_shape=blocks(len(lon_far_cells)),
        in_specs=[vmem] * 8,
        out_specs=vmem,
        cost_estimate=cost(50000),
        compiler_params=params,
    )(*near_args, close[0])
    out = pl.pallas_call(
        coarse_kernel,
        out_shape=blocks(len(stencil_offsets)),
        in_specs=[vmem] * 13,
        out_specs=vmem,
        compiler_params=params,
    )(*near_args, corner_near, corner_far, *close, lon_smooth)
    return out[None, None]


def solution(mesh):
    return jax.shard_map(
        local,
        mesh=mesh,
        in_specs=(
            P("lon", "lat", None, None),
            P("lon", "lat", None),
            P("lon", "lat", None),
            P("lon", "lat", None),
            P("lon", "lat", None),
            P("lon", "lat"),
            P("lon", "lat"),
        ),
        out_specs=P("lon", "lat", None, None, None),
        check_vma=False,
    )
```

```python
import functools

import jax
import jax.numpy as jnp
from jax import lax
from jax.experimental import pallas as pl
from jax.experimental.pallas import tpu as pltpu
from jax.sharding import PartitionSpec as P

relax_weight = 0.6
stencil_offsets = [
    (-2, 0),
    (-1, -1),
    (-1, 0),
    (-1, 1),
    (0, -2),
    (0, -1),
    (0, 0),
    (0, 1),
    (0, 2),
    (1, -1),
    (1, 0),
    (1, 1),
    (2, 0),
]
DIAG, UP, DOWN, EAST, NORTH, OPEN, WEIGHT = range(7)
COEF_ROWS = 8


def pair_near(axis):
    count = lax.axis_size(axis)
    return [(i, i ^ 1) for i in range(count) if i ^ 1 < count]


def pair_far_closed(axis):
    count = lax.axis_size(axis)
    return [(i, (i - 1 if i % 2 == 0 else i + 1) % count) for i in range(count)]


def exchange_lat_far(values):
    lon_count, lat_count = lax.axis_size("lon"), lax.axis_size("lat")
    pairs = []
    for i in range(lon_count):
        for j in range(lat_count):
            partner = j - 1 if j % 2 == 0 else j + 1
            if 0 <= partner < lat_count:
                pairs.append((i * lat_count + j, i * lat_count + partner))
            elif i ^ 2 < lon_count:
                pairs.append((i * lat_count + j, (i ^ 2) * lat_count + j))
    return lax.ppermute(values, ("lon", "lat"), pairs)


def pack_kernel(
    inverse_hbm,
    diag_hbm,
    coup_hbm,
    east_hbm,
    north_hbm,
    land_hbm,
    aggregate_hbm,
    both,
    to_near,
    to_far,
    inverse,
    vert_diag,
    vert_coup,
    face_east,
    face_north,
    land,
    aggregate,
    small_sems,
):
    lon = lax.rem(lax.axis_index("lon"), 2)
    levels = inverse.shape[-1]
    whole = pltpu.make_async_copy(inverse_hbm, inverse, small_sems.at[6])
    whole.start()
    small = [
        pltpu.make_async_copy(source, target, small_sems.at[place])
        for place, (source, target) in enumerate(
            (
                (land_hbm, land),
                (aggregate_hbm, aggregate),
                (coup_hbm, vert_coup),
                (diag_hbm, vert_diag),
                (east_hbm, face_east),
                (north_hbm, face_north),
            )
        )
    ]
    for copy in small:
        copy.start()
    for copy in small:
        copy.wait()
    lane = lax.broadcasted_iota(jnp.int32, (1, levels), 1)
    live = [
        jnp.where(jnp.full((1, levels), aggregate[q // 2, q % 2]) >= 0, 1.0, 0.0) for q in range(4)
    ]
    count = live[0] + live[1] + live[2] + live[3]
    scale = jnp.sqrt(jnp.maximum(count, 1.0))
    for q in range(4):
        x, y = q // 2, q % 2
        coupling = vert_coup[x, y : y + 1, :]
        up = jnp.where(lane < levels - 1, coupling, 0.0)
        down = jnp.where(lane > 0, pltpu.roll(coupling, 1, axis=1), 0.0)
        is_open = jnp.full((1, levels), land[x, y]).astype(jnp.float32)
        rows = [
            vert_diag[x, y : y + 1, :] + coupling + down,
            up,
            down,
            face_east[x, y : y + 1, :] * is_open,
            face_north[x, y : y + 1, :] * is_open,
            is_open,
            live[q] / scale,
            jnp.zeros((1, levels), jnp.float32),
        ]
        block = jnp.concatenate(rows, axis=0)
        for ref, base in ((both, 4 * levels), (to_near, 2 * levels), (to_far, 2 * levels)):
            ref[base + q * COEF_ROWS : base + (q + 1) * COEF_ROWS, :] = block
    whole.wait()
    even_lon = lon == 0
    for y in range(2):
        low, high = inverse[0, y], inverse[1, y]
        both[y * levels : (y + 1) * levels, :] = low
        both[(2 + y) * levels : (3 + y) * levels, :] = high
        to_near[y * levels : (y + 1) * levels, :] = jnp.where(even_lon, high, low)
        to_far[y * levels : (y + 1) * levels, :] = jnp.where(even_lon, low, high)


def parities():
    even_lon = lax.rem(lax.axis_index("lon"), 2) == 0
    even_lat = lax.rem(lax.axis_index("lat"), 2) == 0
    return even_lon, even_lat


def has_lat_far():
    index = lax.axis_index("lat")
    return index != jnp.where(lax.rem(index, 2) == 0, 0, lax.axis_size("lat") - 1)


def wide_kernel(facing_far, own, ring, wide):
    even_lon, _ = parities()
    levels = own.shape[1]
    high = jnp.logical_not(even_lon) if facing_far else even_lon
    for y in range(2):
        low_rows = own[y * levels : (y + 1) * levels, :]
        high_rows = own[(2 + y) * levels : (3 + y) * levels, :]
        wide[y * levels : (y + 1) * levels, :] = jnp.where(high, high_rows, low_rows)
    base = 2 * levels
    coef = [ring[base + q * COEF_ROWS : base + (q + 1) * COEF_ROWS, :] for q in range(4)]
    for y in range(2):
        beyond = jnp.where(high, coef[y], coef[2 + y])
        wide[base + y * COEF_ROWS : base + (y + 1) * COEF_ROWS, :] = beyond


def corner_kernel(lon_near, lon_far, lat_near, lat_far, to_near, to_far):
    even_lon, even_lat = parities()
    levels = lon_near.shape[1]
    size = 4 * COEF_ROWS
    lon = slice(2 * levels, 2 * levels + size)
    lat = slice(4 * levels, 4 * levels + size)

    def west(rows):
        return jnp.where(even_lon, lon_far[rows, :], lon_near[rows, :])

    def east(rows):
        return jnp.where(even_lon, lon_near[rows, :], lon_far[rows, :])

    low, high = slice(0, levels), slice(levels, 2 * levels)
    base = 2 * levels
    beyond = jnp.where(has_lat_far(), lat_far[lat, :], 0.0)
    for out, lower, other in (
        (to_near, jnp.logical_not(even_lat), beyond),
        (to_far, even_lat, lat_near[lat, :]),
    ):
        out[:levels, :] = jnp.where(lower, west(low), west(high))
        out[levels:base, :] = jnp.where(lower, east(low), east(high))
        out[base : base + size, :] = west(lon)
        out[base + size : base + 2 * size, :] = east(lon)
        out[base + 2 * size : base + 3 * size, :] = other


def split(values):
    high = values.astype(jnp.bfloat16)
    return high, (values - high.astype(jnp.float32)).astype(jnp.bfloat16)


def product(left, right):
    return product_of_parts(left, *split(right))


def product_of_parts(left, right_high, right_low):
    left_high, left_low = split(left)
    return jnp.dot(
        jnp.concatenate([left_high, left_high, left_low], axis=1),
        jnp.concatenate([right_high, right_low, right_high], axis=0),
        preferred_element_type=jnp.float32,
    )


def left(values):
    return pltpu.roll(values, 1, axis=1)


def right(values):
    return pltpu.roll(values, values.shape[1] - 1, axis=1)


class Stencil:
    def __init__(self, own, lon_near, lon_far, wide_near, wide_far, lat_near, lat_far, corner_near=None, corner_far=None):
        even_lon, even_lat = parities()
        levels = own.shape[1]
        size = 4 * COEF_ROWS
        full = 4 * levels
        half = 2 * levels
        self.levels = levels
        self.wide = {3: (even_lon, wide_near, wide_far), -2: (even_lon, wide_far, wide_near)}
        sources = {
            (0, 0): (None, own, own, full),
            (1, 0): (even_lon, lon_near, lon_far, half),
            (-1, 0): (even_lon, lon_far, lon_near, half),
            (0, 1): (even_lat, lat_near, lat_far, full),
            (0, -1): (even_lat, lat_far, lat_near, full),
        }
        if corner_near is not None:
            sources |= {
                (-1, 1): (even_lat, corner_near, corner_far, half),
                (-1, -1): (even_lat, corner_far, corner_near, half),
                (1, 1): (even_lat, corner_near, corner_far, half + size),
                (1, -1): (even_lat, corner_far, corner_near, half + size),
                (0, 2): (even_lat, corner_near, corner_far, half + 2 * size),
                (0, -2): (even_lat, corner_far, corner_near, half + 2 * size),
            }
        self.sources = sources
        self.coefs = {place: self.fetch(*source, size) for place, source in sources.items()}
        far = has_lat_far()
        keep = {1: jnp.logical_or(even_lat, far), -1: jnp.logical_or(jnp.logical_not(even_lat), far)}
        for place in sources:
            if place[1] != 0:
                inside = keep[1 if place[1] > 0 else -1]
                self.coefs[place] = jnp.where(inside, self.coefs[place], 0.0)
        pair = 2 * COEF_ROWS
        for x, source in self.wide.items() if wide_near is not None else ():
            beyond = self.fetch(*source, half, pair)
            self.coefs[2 if x > 0 else -2, 0] = jnp.concatenate([beyond, beyond], axis=0)
        self.east = functools.cache(self.east)
        self.north = functools.cache(self.north)
        self.main = functools.cache(self.main)

    def fetch(self, flag, first, other, start, count):
        if flag is None:
            return first[start : start + count, :]
        return jnp.where(flag, first[start : start + count, :], other[start : start + count, :])

    def coef(self, x, y, row):
        at = (2 * (x % 2) + y % 2) * COEF_ROWS + row
        return self.coefs[x // 2, y // 2][at : at + 1, :]

    def weight(self, x, y):
        return self.coef(x, y, WEIGHT)

    def east(self, x, y):
        return self.coef(x, y, EAST) * self.coef(x + 1, y, OPEN)

    def north(self, x, y):
        return self.coef(x, y, NORTH) * self.coef(x, y + 1, OPEN)

    def main(self, x, y):
        lon = self.east(x, y) + self.east(x - 1, y)
        return self.coef(x, y, DIAG) + lon + self.north(x, y) + self.north(x, y - 1)

    def outer_face(self, x, y):
        if x in (0, 1):
            return self.east(x - 1, y) if x == 0 else self.east(x, y)
        return self.north(x, y - 1) if y == 0 else self.north(x, y)

    def inner_main(self, x, y):
        if x in (0, 1):
            inner = self.east(0, y) + self.north(x, y) + self.north(x, y - 1)
        else:
            inner = self.north(x, 0) + self.east(x, y) + self.east(x - 1, y)
        return self.coef(x, y, DIAG) + inner

    def lon_faces(self, x, y):
        above = self.east(x, y) * self.weight(x + 1, y)
        below = self.east(x - 1, y) * self.weight(x - 1, y)
        return (above, below) if x % 2 == 0 else (below, above)

    def lat_faces(self, x, y):
        above = self.north(x, y) * self.weight(x, y + 1)
        below = self.north(x, y - 1) * self.weight(x, y - 1)
        return (above, below) if y % 2 == 0 else (below, above)

    def own_diag(self, x, y):
        return (
            self.weight(x, y) * self.main(x, y) - self.lon_faces(x, y)[0] - self.lat_faces(x, y)[0]
        )

    def inverse(self, x, y):
        lon, lat = x // 2, y // 2
        levels = self.levels
        if x in self.wide:
            return self.fetch(*self.wide[x], y % 2 * levels, levels)
        if lon != 0 and lat != 0:
            start = 0 if lon < 0 else levels
        elif lon != 0:
            start = y % 2 * levels
        else:
            start = (2 * (x % 2) + y % 2) * levels
        return self.fetch(*self.sources[lon, lat][:3], start, levels)

    def residual(self, rows_t, x, y, main=None):
        total = None
        if (x, y) in rows_t:
            block = rows_t[x, y]
            total = (
                block * (self.main if main is None else main)(x, y)
                - left(block * self.coef(x, y, UP))
                - right(block * self.coef(x, y, DOWN))
            )
        for near, face in (
            ((x + 1, y), lambda: self.east(x, y)),
            ((x - 1, y), lambda: self.east(x - 1, y)),
            ((x, y + 1), lambda: self.north(x, y)),
            ((x, y - 1), lambda: self.north(x, y - 1)),
        ):
            if near in rows_t:
                term = rows_t[near] * face()
                total = -term if total is None else total - term
        return total


own_cells = [(x, y) for x in (0, 1) for y in (0, 1)]
lon_cells = [(x, y) for x in (-1, 2) for y in (0, 1)]
lat_cells = [(x, y) for x in (0, 1) for y in (-1, 2)]
near_cells = lon_cells + lat_cells
reach_cells = own_cells + near_cells
lon_far_cells = [(x, y) for x in (-2, 3) for y in (0, 1)]
lat_far_cells = [(x, y) for x in (0, 1) for y in (-2, 3)]
far_cells = lon_far_cells + lat_far_cells
corner_cells = [(2, 2), (2, -1), (-1, 2), (-1, -1)]
groups = {}
for cell in corner_cells + lon_far_cells + lon_cells + lat_far_cells + lat_cells:
    groups.setdefault((cell[0] // 2, cell[1] // 2), []).append(cell)
first_targets = [(0, 0), (1, 0), (-1, 0), (0, 1), (0, -1)]


class Sums:
    def __init__(self, out, targets, started=()):
        self.out = out
        self.slots = {target: place for place, target in enumerate(targets)}
        self.started = set(started)

    def add(self, target, term):
        place = self.slots[target]
        if target in self.started:
            self.out[place] += term
        else:
            self.out[place] = term
            self.started.add(target)


def lateral_targets(x, y):
    lon, lat = x // 2, y // 2
    return (lon + (-1 if x % 2 == 0 else 1), lat), (lon, lat + (-1 if y % 2 == 0 else 1))


def apply_columns(cells, sums, x, y, smooth):
    lon_target, lat_target = lateral_targets(x, y)
    sums.add(lon_target, smooth * cells.lon_faces(x, y)[1])
    sums.add(lat_target, smooth * cells.lat_faces(x, y)[1])
    weight = cells.weight(x, y)
    return (
        smooth * cells.own_diag(x, y),
        smooth * (weight * cells.coef(x, y, UP)),
        smooth * (weight * cells.coef(x, y, DOWN)),
    )


def plus(parts, more):
    return more if parts is None else tuple(a + b for a, b in zip(parts, more))


def close_kernel(own, lon_near, lon_far, lat_near, lat_far, rows_out, smooth_out, partial, rest_out, high_out, low_out):
    cells = Stencil(own, lon_near, lon_far, None, None, lat_near, lat_far)
    levels = cells.levels
    row = lax.broadcasted_iota(jnp.int32, (levels, levels), 0)
    lane = lax.broadcasted_iota(jnp.int32, (levels, levels), 1)
    rows_t = {}
    for x, y in own_cells:
        block = cells.inverse(x, y)
        weight = cells.weight(x, y)
        smoothed = (
            block * cells.own_diag(x, y)
            - left(block * (weight * cells.coef(x, y, UP)))
            - right(block * (weight * cells.coef(x, y, DOWN)))
        )
        rows_t[x, y] = (jnp.where(row == lane, weight, 0.0) - relax_weight * smoothed).T
    for x, y in lon_cells:
        rows_t[x, y] = (cells.inverse(x, y) * (relax_weight * cells.lon_faces(x, y)[1])).T
    for x, y in lat_cells:
        rows_t[x, y] = (cells.inverse(x, y) * (relax_weight * cells.lat_faces(x, y)[1])).T
    for place, cell in enumerate(reach_cells):
        rows_out[place] = rows_t[cell]
    sums = Sums(partial, first_targets)
    parts = None
    for x, y in own_cells:
        rest = cells.residual(rows_t, x, y)
        smooth = product(rest, cells.inverse(x, y)) * relax_weight
        terms = apply_columns(cells, sums, x, y, smooth)
        parts = plus(parts, (rest * cells.weight(x, y) - terms[0],) + terms[1:])
    sums.add((0, 0), parts[0] + left(parts[1]) + right(parts[2]))
    for x, y in far_cells:
        rest = cells.residual(rows_t, x, y)
        sums.add((x // 2, y // 2), rest * cells.weight(x, y))
        if (x, y) in lat_far_cells:
            smooth = product(rest, cells.inverse(x, y)) * relax_weight
            smooth_out[lat_far_cells.index((x, y))] = smooth
    for place, (x, y) in enumerate(near_cells):
        rest_out[place] = cells.residual(rows_t, x, y, cells.inner_main)
        high_out[place], low_out[place] = split(cells.inverse(x, y))


def wide_products_kernel(own, lon_near, lon_far, wide_near, wide_far, lat_near, lat_far, rows_in, smooth_out):
    cells = Stencil(own, lon_near, lon_far, wide_near, wide_far, lat_near, lat_far)
    rows_t = {cell: rows_in[place] for place, cell in enumerate(reach_cells) if cell in lon_cells}
    for place, (x, y) in enumerate(lon_far_cells):
        rest = cells.residual(rows_t, x, y)
        smooth_out[place] = product(rest, cells.inverse(x, y)) * relax_weight


def targets_of(device, members):
    return {device}.union(*(lateral_targets(*cell) for cell in members))


last_group = {
    target: device for device, members in groups.items() for target in targets_of(device, members)
}


def coarse_kernel(*refs):
    cells = Stencil(*refs[:9])
    rows_in, lat_smooth, partial, rest_in, high_in, low_in, lon_smooth, out, blocks, sems = refs[9:]
    rows_t = {cell: rows_in[place] for place, cell in enumerate(reach_cells)}
    sums = Sums(blocks, stencil_offsets)
    for place, target in enumerate(first_targets):
        sums.add(target, partial[place])
    copies = []
    for device, members in groups.items():
        straight = parts = None
        for x, y in members:
            if (x, y) in lon_far_cells:
                smooth = lon_smooth[lon_far_cells.index((x, y))]
            elif (x, y) in lat_far_cells:
                smooth = lat_smooth[lat_far_cells.index((x, y))]
            else:
                if (x, y) in near_cells:
                    place = near_cells.index((x, y))
                    rest = rest_in[place] + rows_t[x, y] * cells.outer_face(x, y)
                    smooth = product_of_parts(rest, high_in[place], low_in[place])
                else:
                    rest = cells.residual(rows_t, x, y)
                    smooth = product(rest, cells.inverse(x, y))
                smooth = smooth * relax_weight
                term = rest * cells.weight(x, y)
                straight = term if straight is None else straight + term
            parts = plus(parts, apply_columns(cells, sums, x, y, smooth))
        sums.add(device, straight - parts[0] + left(parts[1]) + right(parts[2]))
        for target, last in last_group.items():
            if last == device:
                place = sums.slots[target]
                copies.append(pltpu.make_async_copy(blocks.at[place], out.at[place], sems.at[place]))
                copies[-1].start()
    for copy in copies:
        copy.wait()


def local(inverse, vert_diag, vert_coup, face_east, face_north, land_mask, aggregate):
    levels = inverse.shape[-1]
    size = 4 * COEF_ROWS
    args = (inverse, vert_diag, vert_coup, face_east, face_north, land_mask, aggregate)
    vmem = pl.BlockSpec(memory_space=pltpu.VMEM)
    params = pltpu.CompilerParams(vmem_limit_bytes=8 * 1024 * 1024)
    array = lambda count: jax.ShapeDtypeStruct((count, levels), jnp.float32)
    cost = lambda size: pl.CostEstimate(flops=size * 10**6, bytes_accessed=size * 10**3, transcendentals=0)
    shapes = [4 * levels + size] + [2 * levels + size] * 2
    both, to_near, to_far = pl.pallas_call(
        pack_kernel,
        out_shape=tuple(pltpu.VMEM((rows, levels), jnp.float32) for rows in shapes),
        in_specs=[pl.BlockSpec(memory_space=pltpu.HBM)] * 7,
        out_specs=(vmem,) * 3,
        scratch_shapes=[pltpu.VMEM(arg.shape, arg.dtype) for arg in args[:5]]
        + [pltpu.SMEM(arg.shape, arg.dtype) for arg in args[5:]]
        + [pltpu.SemaphoreType.DMA((7,))],
        compiler_params=pltpu.CompilerParams(vmem_limit_bytes=8 * 1024 * 1024),
    )(*(pltpu.with_memory_space_constraint(arg, pltpu.HBM) for arg in args))
    lon_near = lax.ppermute(to_near, "lon", pair_near("lon"))
    lon_far = lax.ppermute(to_far, "lon", pair_far_closed("lon"))
    lat_near = lax.ppermute(both, "lat", pair_near("lat"))
    lat_far = exchange_lat_far(both)

    def widened(facing_far, ring, spare, weight):
        return pl.pallas_call(
            functools.partial(wide_kernel, facing_far),
            out_shape=array(2 * (levels + COEF_ROWS) + spare),
            in_specs=[vmem] * 2,
            out_specs=vmem,
            cost_estimate=cost(weight),
            compiler_params=params,
        )(both, ring)

    wide_far = lax.ppermute(widened(False, lon_near, 8, 1000), "lon", pair_far_closed("lon"))
    wide_near = lax.ppermute(widened(True, lon_far, 0, 8000), "lon", pair_near("lon"))
    corner_rows = 2 * levels + 3 * size
    corner_to_near, corner_to_far = pl.pallas_call(
        corner_kernel,
        out_shape=(array(corner_rows), array(corner_rows)),
        in_specs=[vmem] * 4,
        out_specs=(vmem, vmem),
        compiler_params=params,
    )(lon_near, lon_far, lat_near, lat_far)
    corner_near = lax.ppermute(corner_to_near, "lat", pair_near("lat"))
    corner_far = exchange_lat_far(corner_to_far)
    blocks = lambda count: jax.ShapeDtypeStruct((count, levels, levels), jnp.float32)
    close = pl.pallas_call(
        close_kernel,
        out_shape=(
            *(blocks(len(cells)) for cells in (reach_cells, lat_far_cells, first_targets, near_cells)),
            *(jax.ShapeDtypeStruct((len(near_cells), levels, levels), jnp.bfloat16),) * 2,
        ),
        in_specs=[vmem] * 5,
        out_specs=(vmem,) * 6,
        cost_estimate=cost(1),
        compiler_params=params,
    )(both, lon_near, lon_far, lat_near, lat_far)
    near_args = (both, lon_near, lon_far, wide_near, wide_far, lat_near, lat_far)
    lon_smooth = pl.pallas_call(
        wide_products_kernel,
        out_shape=blocks(len(lon_far_cells)),
        in_specs=[vmem] * 8,
        out_specs=vmem,
        cost_estimate=cost(50000),
        compiler_params=params,
    )(*near_args, close[0])
    out = pl.pallas_call(
        coarse_kernel,
        out_shape=blocks(len(stencil_offsets)),
        in_specs=[vmem] * 16,
        out_specs=pl.BlockSpec(memory_space=pltpu.HBM),
        scratch_shapes=[
            pltpu.VMEM((len(stencil_offsets), levels, levels), jnp.float32),
            pltpu.SemaphoreType.DMA((len(stencil_offsets),)),
        ],
        compiler_params=params,
    )(*near_args, corner_near, corner_far, *close, lon_smooth)
    return out[None, None]


def solution(mesh):
    return jax.shard_map(
        local,
        mesh=mesh,
        in_specs=(
            P("lon", "lat", None, None),
            P("lon", "lat", None),
            P("lon", "lat", None),
            P("lon", "lat", None),
            P("lon", "lat", None),
            P("lon", "lat"),
            P("lon", "lat"),
        ),
        out_specs=P("lon", "lat", None, None, None),
        check_vma=False,
    )
```

```python
import functools

import jax
import jax.numpy as jnp
from jax import lax
from jax.experimental import pallas as pl
from jax.experimental.pallas import tpu as pltpu
from jax.sharding import PartitionSpec as P

relax_weight = 0.6
stencil_offsets = [
    (-2, 0),
    (-1, -1),
    (-1, 0),
    (-1, 1),
    (0, -2),
    (0, -1),
    (0, 0),
    (0, 1),
    (0, 2),
    (1, -1),
    (1, 0),
    (1, 1),
    (2, 0),
]
DIAG, UP, DOWN, EAST, NORTH, OPEN, WEIGHT = range(7)
COEF_ROWS = 8
CORNER_ROWS = 2 * (COEF_ROWS + 2 * 4) + 2 * 4


def pair_near(axis):
    count = lax.axis_size(axis)
    return [(i, i ^ 1) for i in range(count) if i ^ 1 < count]


def pair_far_closed(axis):
    count = lax.axis_size(axis)
    return [(i, (i - 1 if i % 2 == 0 else i + 1) % count) for i in range(count)]


def exchange_lat_far(values):
    lon_count, lat_count = lax.axis_size("lon"), lax.axis_size("lat")
    pairs = []
    for i in range(lon_count):
        for j in range(lat_count):
            partner = j - 1 if j % 2 == 0 else j + 1
            if 0 <= partner < lat_count:
                pairs.append((i * lat_count + j, i * lat_count + partner))
            elif i ^ 2 < lon_count:
                pairs.append((i * lat_count + j, (i ^ 2) * lat_count + j))
    return lax.ppermute(values, ("lon", "lat"), pairs)


def pack_kernel(
    inverse_hbm,
    diag_hbm,
    coup_hbm,
    east_hbm,
    north_hbm,
    land_hbm,
    aggregate_hbm,
    both,
    to_near,
    to_far,
    inverse,
    vert_diag,
    vert_coup,
    face_east,
    face_north,
    land,
    aggregate,
    small_sems,
):
    lon = lax.rem(lax.axis_index("lon"), 2)
    levels = inverse.shape[-1]
    whole = pltpu.make_async_copy(inverse_hbm, inverse, small_sems.at[6])
    whole.start()
    small = [
        pltpu.make_async_copy(source, target, small_sems.at[place])
        for place, (source, target) in enumerate(
            (
                (land_hbm, land),
                (aggregate_hbm, aggregate),
                (coup_hbm, vert_coup),
                (diag_hbm, vert_diag),
                (east_hbm, face_east),
                (north_hbm, face_north),
            )
        )
    ]
    for copy in small:
        copy.start()
    for copy in small:
        copy.wait()
    lane = lax.broadcasted_iota(jnp.int32, (1, levels), 1)
    live = [
        jnp.where(jnp.full((1, levels), aggregate[q // 2, q % 2]) >= 0, 1.0, 0.0) for q in range(4)
    ]
    count = live[0] + live[1] + live[2] + live[3]
    scale = jnp.sqrt(jnp.maximum(count, 1.0))
    for q in range(4):
        x, y = q // 2, q % 2
        coupling = vert_coup[x, y : y + 1, :]
        up = jnp.where(lane < levels - 1, coupling, 0.0)
        down = jnp.where(lane > 0, pltpu.roll(coupling, 1, axis=1), 0.0)
        is_open = jnp.full((1, levels), land[x, y]).astype(jnp.float32)
        rows = [
            vert_diag[x, y : y + 1, :] + coupling + down,
            up,
            down,
            face_east[x, y : y + 1, :] * is_open,
            face_north[x, y : y + 1, :] * is_open,
            is_open,
            live[q] / scale,
            jnp.zeros((1, levels), jnp.float32),
        ]
        block = jnp.concatenate(rows, axis=0)
        for ref, base in ((both, 4 * levels), (to_near, 2 * levels), (to_far, 2 * levels)):
            ref[base + q * COEF_ROWS : base + (q + 1) * COEF_ROWS, :] = block
    whole.wait()
    even_lon = lon == 0
    for y in range(2):
        low, high = inverse[0, y], inverse[1, y]
        both[y * levels : (y + 1) * levels, :] = low
        both[(2 + y) * levels : (3 + y) * levels, :] = high
        to_near[y * levels : (y + 1) * levels, :] = jnp.where(even_lon, high, low)
        to_far[y * levels : (y + 1) * levels, :] = jnp.where(even_lon, low, high)


def parities():
    even_lon = lax.rem(lax.axis_index("lon"), 2) == 0
    even_lat = lax.rem(lax.axis_index("lat"), 2) == 0
    return even_lon, even_lat


def has_lat_far():
    index = lax.axis_index("lat")
    return index != jnp.where(lax.rem(index, 2) == 0, 0, lax.axis_size("lat") - 1)


def wide_kernel(facing_far, own, ring, wide):
    even_lon, _ = parities()
    levels = own.shape[1]
    high = jnp.logical_not(even_lon) if facing_far else even_lon
    for y in range(2):
        low_rows = own[y * levels : (y + 1) * levels, :]
        high_rows = own[(2 + y) * levels : (3 + y) * levels, :]
        wide[y * levels : (y + 1) * levels, :] = jnp.where(high, high_rows, low_rows)
    base = 2 * levels
    coef = [ring[base + q * COEF_ROWS : base + (q + 1) * COEF_ROWS, :] for q in range(4)]
    for y in range(2):
        beyond = jnp.where(high, coef[y], coef[2 + y])
        wide[base + y * COEF_ROWS : base + (y + 1) * COEF_ROWS, :] = beyond


def corner_kernel(lon_near, lon_far, lat_near, lat_far, to_near, to_far):
    even_lon, even_lat = parities()
    levels = lon_near.shape[1]
    base = 2 * levels

    def block(values, q, first=0):
        return values[q * COEF_ROWS + first : q * COEF_ROWS + (WEIGHT + 1 if first else COEF_ROWS), :]

    def sides(rows):
        near, far = lon_near[rows, :], lon_far[rows, :]
        return jnp.where(even_lon, far, near), jnp.where(even_lon, near, far)

    low = sides(slice(0, levels))
    high = sides(slice(levels, base))
    coefs = sides(slice(base, lon_near.shape[0]))
    lat = slice(2 * base, lat_near.shape[0])
    beyond = jnp.where(has_lat_far(), lat_far[lat, :], 0.0)
    for out, lower, other in (
        (to_near, jnp.logical_not(even_lat), beyond),
        (to_far, even_lat, lat_near[lat, :]),
    ):
        rows = []
        for place, facing in enumerate((1, 0)):
            out[place * levels : (place + 1) * levels, :] = jnp.where(lower, low[place], high[place])
            choices = []
            for y in (0, 1):
                corner, beside, behind = 2 * facing + y, 2 * (1 - facing) + y, 2 * facing + 1 - y
                choices.append(
                    [block(coefs[place], corner)]
                    + [block(coefs[place], q, EAST) for q in (beside, behind)]
                )
            rows += [jnp.where(lower, *pair) for pair in zip(*choices)]
        for x in (0, 1):
            choices = (block(other, 2 * x + y, EAST) for y in (0, 1))
            rows.append(jnp.where(lower, *choices))
        out[base : base + CORNER_ROWS, :] = jnp.concatenate(rows, axis=0)


def split(values):
    high = values.astype(jnp.bfloat16)
    return high, (values - high.astype(jnp.float32)).astype(jnp.bfloat16)


def product(left, right):
    return product_of_parts(left, *split(right))


def product_of_parts(left, right_high, right_low):
    left_high, left_low = split(left)
    return jnp.dot(
        jnp.concatenate([left_high, left_high, left_low], axis=1),
        jnp.concatenate([right_high, right_low, right_high], axis=0),
        preferred_element_type=jnp.float32,
    )


def left(values):
    return pltpu.roll(values, 1, axis=1)


def right(values):
    return pltpu.roll(values, values.shape[1] - 1, axis=1)


class Stencil:
    def __init__(self, own, lon_near, lon_far, wide_near, wide_far, lat_near, lat_far, corner_near=None, corner_far=None):
        even_lon, even_lat = parities()
        levels = own.shape[1]
        size = 4 * COEF_ROWS
        full = 4 * levels
        half = 2 * levels
        self.levels = levels
        self.wide = {3: (even_lon, wide_near, wide_far), -2: (even_lon, wide_far, wide_near)}
        sources = {
            (0, 0): (None, own, own, full),
            (1, 0): (even_lon, lon_near, lon_far, half),
            (-1, 0): (even_lon, lon_far, lon_near, half),
            (0, 1): (even_lat, lat_near, lat_far, full),
            (0, -1): (even_lat, lat_far, lat_near, full),
        }
        self.sources = sources
        self.coefs = {place: self.fetch(*source, size) for place, source in sources.items()}
        far = has_lat_far()
        keep = {1: jnp.logical_or(even_lat, far), -1: jnp.logical_or(jnp.logical_not(even_lat), far)}
        for place in sources:
            if place[1] != 0:
                inside = keep[1 if place[1] > 0 else -1]
                self.coefs[place] = jnp.where(inside, self.coefs[place], 0.0)
        self.parts = {}
        if corner_near is not None:
            self.corners = {1: (even_lat, corner_near, corner_far), -1: (even_lat, corner_far, corner_near)}
            for side, source in self.corners.items():
                rows = jnp.where(keep[side], self.fetch(*source, half, CORNER_ROWS), 0.0)
                facing, behind, beyond = (2, 3, 4) if side > 0 else (-1, -2, -3)
                start = 0
                for x, beside in ((-1, -2), (2, 3)):
                    self.parts[x, facing] = (rows, start)
                    self.parts[beside, facing] = (rows, start + COEF_ROWS - EAST)
                    self.parts[x, behind] = (rows, start + COEF_ROWS + 4 - EAST)
                    start += COEF_ROWS + 8
                for x in (0, 1):
                    self.parts[x, beyond] = (rows, start + 4 * x - EAST)
        pair = 2 * COEF_ROWS
        for x, source in self.wide.items() if wide_near is not None else ():
            beyond = self.fetch(*source, half, pair)
            self.coefs[2 if x > 0 else -2, 0] = jnp.concatenate([beyond, beyond], axis=0)
        self.east = functools.cache(self.east)
        self.north = functools.cache(self.north)
        self.main = functools.cache(self.main)

    def fetch(self, flag, first, other, start, count):
        if flag is None:
            return first[start : start + count, :]
        return jnp.where(flag, first[start : start + count, :], other[start : start + count, :])

    def coef(self, x, y, row):
        if (x, y) in self.parts:
            rows, start = self.parts[x, y]
            return rows[start + row : start + row + 1, :]
        at = (2 * (x % 2) + y % 2) * COEF_ROWS + row
        return self.coefs[x // 2, y // 2][at : at + 1, :]

    def weight(self, x, y):
        return self.coef(x, y, WEIGHT)

    def east(self, x, y):
        return self.coef(x, y, EAST) * self.coef(x + 1, y, OPEN)

    def north(self, x, y):
        return self.coef(x, y, NORTH) * self.coef(x, y + 1, OPEN)

    def main(self, x, y):
        lon = self.east(x, y) + self.east(x - 1, y)
        return self.coef(x, y, DIAG) + lon + self.north(x, y) + self.north(x, y - 1)

    def outer_face(self, x, y):
        if x in (0, 1):
            return self.east(x - 1, y) if x == 0 else self.east(x, y)
        return self.north(x, y - 1) if y == 0 else self.north(x, y)

    def inner_main(self, x, y):
        if x in (0, 1):
            inner = self.east(0, y) + self.north(x, y) + self.north(x, y - 1)
        else:
            inner = self.north(x, 0) + self.east(x, y) + self.east(x - 1, y)
        return self.coef(x, y, DIAG) + inner

    def lon_faces(self, x, y):
        above = self.east(x, y) * self.weight(x + 1, y)
        below = self.east(x - 1, y) * self.weight(x - 1, y)
        return (above, below) if x % 2 == 0 else (below, above)

    def lat_faces(self, x, y):
        above = self.north(x, y) * self.weight(x, y + 1)
        below = self.north(x, y - 1) * self.weight(x, y - 1)
        return (above, below) if y % 2 == 0 else (below, above)

    def own_diag(self, x, y):
        return (
            self.weight(x, y) * self.main(x, y) - self.lon_faces(x, y)[0] - self.lat_faces(x, y)[0]
        )

    def inverse(self, x, y):
        lon, lat = x // 2, y // 2
        levels = self.levels
        if x in self.wide:
            return self.fetch(*self.wide[x], y % 2 * levels, levels)
        if lon != 0 and lat != 0:
            return self.fetch(*self.corners[lat], 0 if lon < 0 else levels, levels)
        elif lon != 0:
            start = y % 2 * levels
        else:
            start = (2 * (x % 2) + y % 2) * levels
        return self.fetch(*self.sources[lon, lat][:3], start, levels)

    def residual(self, rows_t, x, y, main=None):
        total = None
        if (x, y) in rows_t:
            block = rows_t[x, y]
            total = (
                block * (self.main if main is None else main)(x, y)
                - left(block * self.coef(x, y, UP))
                - right(block * self.coef(x, y, DOWN))
            )
        for near, face in (
            ((x + 1, y), lambda: self.east(x, y)),
            ((x - 1, y), lambda: self.east(x - 1, y)),
            ((x, y + 1), lambda: self.north(x, y)),
            ((x, y - 1), lambda: self.north(x, y - 1)),
        ):
            if near in rows_t:
                term = rows_t[near] * face()
                total = -term if total is None else total - term
        return total


own_cells = [(x, y) for x in (0, 1) for y in (0, 1)]
lon_cells = [(x, y) for x in (-1, 2) for y in (0, 1)]
lat_cells = [(x, y) for x in (0, 1) for y in (-1, 2)]
near_cells = lon_cells + lat_cells
reach_cells = own_cells + near_cells
lon_far_cells = [(x, y) for x in (-2, 3) for y in (0, 1)]
lat_far_cells = [(x, y) for x in (0, 1) for y in (-2, 3)]
far_cells = lon_far_cells + lat_far_cells
corner_cells = [(2, 2), (2, -1), (-1, 2), (-1, -1)]
groups = {}
for cell in corner_cells + lon_far_cells + lon_cells + lat_far_cells + lat_cells:
    groups.setdefault((cell[0] // 2, cell[1] // 2), []).append(cell)
first_targets = [(0, 0), (1, 0), (-1, 0), (0, 1), (0, -1)]


class Sums:
    def __init__(self, out, targets, started=()):
        self.out = out
        self.slots = {target: place for place, target in enumerate(targets)}
        self.started = set(started)

    def add(self, target, term):
        place = self.slots[target]
        if target in self.started:
            self.out[place] += term
        else:
            self.out[place] = term
            self.started.add(target)


def lateral_targets(x, y):
    lon, lat = x // 2, y // 2
    return (lon + (-1 if x % 2 == 0 else 1), lat), (lon, lat + (-1 if y % 2 == 0 else 1))


def apply_columns(cells, sums, x, y, smooth):
    lon_target, lat_target = lateral_targets(x, y)
    sums.add(lon_target, smooth * cells.lon_faces(x, y)[1])
    sums.add(lat_target, smooth * cells.lat_faces(x, y)[1])
    weight = cells.weight(x, y)
    return (
        smooth * cells.own_diag(x, y),
        smooth * (weight * cells.coef(x, y, UP)),
        smooth * (weight * cells.coef(x, y, DOWN)),
    )


def plus(parts, more):
    return more if parts is None else tuple(a + b for a, b in zip(parts, more))


def close_kernel(own, lon_near, lon_far, lat_near, lat_far, rows_out, smooth_out, partial, rest_out, high_out, low_out):
    cells = Stencil(own, lon_near, lon_far, None, None, lat_near, lat_far)
    levels = cells.levels
    row = lax.broadcasted_iota(jnp.int32, (levels, levels), 0)
    lane = lax.broadcasted_iota(jnp.int32, (levels, levels), 1)
    rows_t = {}
    for x, y in own_cells:
        block = cells.inverse(x, y)
        weight = cells.weight(x, y)
        smoothed = (
            block * cells.own_diag(x, y)
            - left(block * (weight * cells.coef(x, y, UP)))
            - right(block * (weight * cells.coef(x, y, DOWN)))
        )
        rows_t[x, y] = (jnp.where(row == lane, weight, 0.0) - relax_weight * smoothed).T
    for x, y in lon_cells:
        rows_t[x, y] = (cells.inverse(x, y) * (relax_weight * cells.lon_faces(x, y)[1])).T
    for x, y in lat_cells:
        rows_t[x, y] = (cells.inverse(x, y) * (relax_weight * cells.lat_faces(x, y)[1])).T
    for place, cell in enumerate(reach_cells):
        rows_out[place] = rows_t[cell]
    sums = Sums(partial, first_targets)
    parts = None
    for x, y in own_cells:
        rest = cells.residual(rows_t, x, y)
        smooth = product(rest, cells.inverse(x, y)) * relax_weight
        terms = apply_columns(cells, sums, x, y, smooth)
        parts = plus(parts, (rest * cells.weight(x, y) - terms[0],) + terms[1:])
    sums.add((0, 0), parts[0] + left(parts[1]) + right(parts[2]))
    for x, y in far_cells:
        rest = cells.residual(rows_t, x, y)
        sums.add((x // 2, y // 2), rest * cells.weight(x, y))
        if (x, y) in lat_far_cells:
            smooth = product(rest, cells.inverse(x, y))
            smooth_out[lat_far_cells.index((x, y))] = smooth
    for place, (x, y) in enumerate(near_cells):
        rest_out[place] = cells.residual(rows_t, x, y, cells.inner_main)
        high_out[place], low_out[place] = split(cells.inverse(x, y))


def wide_products_kernel(own, lon_near, lon_far, wide_near, wide_far, lat_near, lat_far, rows_in, smooth_out):
    cells = Stencil(own, lon_near, lon_far, wide_near, wide_far, lat_near, lat_far)
    rows_t = {cell: rows_in[place] for place, cell in enumerate(reach_cells) if cell in lon_cells}
    for place, (x, y) in enumerate(lon_far_cells):
        rest = cells.residual(rows_t, x, y)
        smooth_out[place] = product(rest, cells.inverse(x, y))


product_cells = corner_cells + near_cells


target_order = [(-2, 0), (2, 0), (0, -2), (0, 2)] + [
    target for target in stencil_offsets if 2 not in target and -2 not in target
]


def coarse_kernel(*refs):
    cells = Stencil(*refs[:9])
    rows_in, lat_smooth, partial, rest_in, high_in, low_in, lon_smooth = refs[9:16]
    out, blocks, rests, smooths, sems = refs[16:]
    levels = cells.levels
    rows_t = {cell: rows_in[place] for place, cell in enumerate(reach_cells)}
    smooth_of, rest_of = {}, {}
    for place, cell in enumerate(lon_far_cells):
        smooth_of[cell] = lon_smooth.at[place]
    for place, cell in enumerate(lat_far_cells):
        smooth_of[cell] = lat_smooth.at[place]
    for place, (x, y) in enumerate(product_cells):
        if (x, y) in near_cells:
            known = near_cells.index((x, y))
            rest = rest_in[known] + rows_t[x, y] * cells.outer_face(x, y)
            smooths[place] = product_of_parts(rest, high_in[known], low_in[known])
        else:
            rest = cells.residual(rows_t, x, y)
            smooths[place] = product(rest, cells.inverse(x, y))
        rests[place] = rest
        rest_of[x, y], smooth_of[x, y] = rests.at[place], smooths.at[place]
    lateral, own = {}, {}
    for device, members in groups.items():
        for x, y in members:
            lon_target, lat_target = lateral_targets(x, y)
            for target, faces in ((lon_target, cells.lon_faces), (lat_target, cells.lat_faces)):
                lateral.setdefault(target, []).append(((x, y), faces(x, y)[1] * relax_weight))
            weight = cells.weight(x, y) * relax_weight
            factors = (
                cells.own_diag(x, y) * relax_weight,
                weight * cells.coef(x, y, UP),
                weight * cells.coef(x, y, DOWN),
            )
            own.setdefault(device, []).append(((x, y), factors))
    slots = {target: place for place, target in enumerate(stencil_offsets)}
    copies = []
    strip = levels // 4
    for target in target_order:
        for start in range(0, levels, strip):
            rows = slice(start, start + strip)
            total = None
            if target in first_targets:
                total = partial[first_targets.index(target), rows, :]
            for cell, factor in lateral.get(target, ()):
                term = smooth_of[cell][rows, :] * factor
                total = term if total is None else total + term
            parts = None
            for cell, factors in own.get(target, ()):
                smooth = smooth_of[cell][rows, :]
                terms = [smooth * factor for factor in factors]
                if cell in rest_of:
                    terms[0] = terms[0] - rest_of[cell][rows, :] * cells.weight(*cell)
                parts = plus(parts, tuple(terms))
            if parts is not None:
                total = total - parts[0] + left(parts[1]) + right(parts[2])
            blocks[slots[target], rows, :] = total
        place = slots[target]
        copies.append(pltpu.make_async_copy(blocks.at[place], out.at[place], sems.at[place]))
        copies[-1].start()
    for copy in copies:
        copy.wait()


def local(inverse, vert_diag, vert_coup, face_east, face_north, land_mask, aggregate):
    levels = inverse.shape[-1]
    size = 4 * COEF_ROWS
    args = (inverse, vert_diag, vert_coup, face_east, face_north, land_mask, aggregate)
    vmem = pl.BlockSpec(memory_space=pltpu.VMEM)
    params = pltpu.CompilerParams(vmem_limit_bytes=8 * 1024 * 1024)
    array = lambda count: jax.ShapeDtypeStruct((count, levels), jnp.float32)
    cost = lambda size: pl.CostEstimate(flops=size * 10**6, bytes_accessed=size * 10**3, transcendentals=0)
    shapes = [4 * levels + size] + [2 * levels + size] * 2
    both, to_near, to_far = pl.pallas_call(
        pack_kernel,
        out_shape=tuple(pltpu.VMEM((rows, levels), jnp.float32) for rows in shapes),
        in_specs=[pl.BlockSpec(memory_space=pltpu.HBM)] * 7,
        out_specs=(vmem,) * 3,
        scratch_shapes=[pltpu.VMEM(arg.shape, arg.dtype) for arg in args[:5]]
        + [pltpu.SMEM(arg.shape, arg.dtype) for arg in args[5:]]
        + [pltpu.SemaphoreType.DMA((7,))],
        compiler_params=pltpu.CompilerParams(vmem_limit_bytes=8 * 1024 * 1024),
    )(*(pltpu.with_memory_space_constraint(arg, pltpu.HBM) for arg in args))
    lon_near = lax.ppermute(to_near, "lon", pair_near("lon"))
    lon_far = lax.ppermute(to_far, "lon", pair_far_closed("lon"))
    lat_near = lax.ppermute(both, "lat", pair_near("lat"))
    lat_far = exchange_lat_far(both)

    def widened(facing_far, ring, spare, weight):
        return pl.pallas_call(
            functools.partial(wide_kernel, facing_far),
            out_shape=array(2 * (levels + COEF_ROWS) + spare),
            in_specs=[vmem] * 2,
            out_specs=vmem,
            cost_estimate=cost(weight),
            compiler_params=params,
        )(both, ring)

    wide_far = lax.ppermute(widened(False, lon_near, 8, 1000), "lon", pair_far_closed("lon"))
    wide_near = lax.ppermute(widened(True, lon_far, 0, 8000), "lon", pair_near("lon"))
    corner_rows = 2 * levels + CORNER_ROWS
    corner_to_near, corner_to_far = pl.pallas_call(
        corner_kernel,
        out_shape=(array(corner_rows), array(corner_rows)),
        in_specs=[vmem] * 4,
        out_specs=(vmem, vmem),
        compiler_params=params,
    )(lon_near, lon_far, lat_near, lat_far)
    corner_near = lax.ppermute(corner_to_near, "lat", pair_near("lat"))
    corner_far = exchange_lat_far(corner_to_far)
    blocks = lambda count: jax.ShapeDtypeStruct((count, levels, levels), jnp.float32)
    close = pl.pallas_call(
        close_kernel,
        out_shape=(
            *(blocks(len(cells)) for cells in (reach_cells, lat_far_cells, first_targets, near_cells)),
            *(jax.ShapeDtypeStruct((len(near_cells), levels, levels), jnp.bfloat16),) * 2,
        ),
        in_specs=[vmem] * 5,
        out_specs=(vmem,) * 6,
        cost_estimate=cost(1),
        compiler_params=params,
    )(both, lon_near, lon_far, lat_near, lat_far)
    near_args = (both, lon_near, lon_far, wide_near, wide_far, lat_near, lat_far)
    lon_smooth = pl.pallas_call(
        wide_products_kernel,
        out_shape=blocks(len(lon_far_cells)),
        in_specs=[vmem] * 8,
        out_specs=vmem,
        cost_estimate=cost(50000),
        compiler_params=params,
    )(*near_args, close[0])
    out = pl.pallas_call(
        coarse_kernel,
        out_shape=blocks(len(stencil_offsets)),
        in_specs=[vmem] * 16,
        out_specs=pl.BlockSpec(memory_space=pltpu.HBM),
        scratch_shapes=[
            pltpu.VMEM((len(stencil_offsets), levels, levels), jnp.float32),
            *(pltpu.VMEM((len(product_cells), levels, levels), jnp.float32),) * 2,
            pltpu.SemaphoreType.DMA((len(stencil_offsets),)),
        ],
        compiler_params=params,
    )(*near_args, corner_near, corner_far, *close, lon_smooth)
    return out[None, None]


def solution(mesh):
    return jax.shard_map(
        local,
        mesh=mesh,
        in_specs=(
            P("lon", "lat", None, None),
            P("lon", "lat", None),
            P("lon", "lat", None),
            P("lon", "lat", None),
            P("lon", "lat", None),
            P("lon", "lat"),
            P("lon", "lat"),
        ),
        out_specs=P("lon", "lat", None, None, None),
        check_vma=False,
    )
```

```python
import functools

import jax
import jax.numpy as jnp
from jax import lax
from jax.experimental import pallas as pl
from jax.experimental.pallas import tpu as pltpu
from jax.sharding import PartitionSpec as P

relax_weight = 0.6
stencil_offsets = [
    (-2, 0),
    (-1, -1),
    (-1, 0),
    (-1, 1),
    (0, -2),
    (0, -1),
    (0, 0),
    (0, 1),
    (0, 2),
    (1, -1),
    (1, 0),
    (1, 1),
    (2, 0),
]
DIAG, UP, DOWN, EAST, NORTH, OPEN, WEIGHT = range(7)
COEF_ROWS = 8
CORNER_ROWS = 2 * (COEF_ROWS + 2 * 4) + 2 * 4


def pair_near(axis):
    count = lax.axis_size(axis)
    return [(i, i ^ 1) for i in range(count) if i ^ 1 < count]


def pair_far_closed(axis):
    count = lax.axis_size(axis)
    return [(i, (i - 1 if i % 2 == 0 else i + 1) % count) for i in range(count)]


def exchange_lat_far(values):
    lon_count, lat_count = lax.axis_size("lon"), lax.axis_size("lat")
    pairs = []
    for i in range(lon_count):
        for j in range(lat_count):
            partner = j - 1 if j % 2 == 0 else j + 1
            if 0 <= partner < lat_count:
                pairs.append((i * lat_count + j, i * lat_count + partner))
            elif i ^ 2 < lon_count:
                pairs.append((i * lat_count + j, (i ^ 2) * lat_count + j))
    return lax.ppermute(values, ("lon", "lat"), pairs)


def pack_kernel(
    inverse_hbm,
    diag_hbm,
    coup_hbm,
    east_hbm,
    north_hbm,
    land_hbm,
    aggregate_hbm,
    both,
    to_near,
    to_far,
    inverse,
    vert_diag,
    vert_coup,
    face_east,
    face_north,
    land,
    aggregate,
    small_sems,
):
    lon = lax.rem(lax.axis_index("lon"), 2)
    levels = inverse.shape[-1]
    whole = pltpu.make_async_copy(inverse_hbm, inverse, small_sems.at[6])
    whole.start()
    small = [
        pltpu.make_async_copy(source, target, small_sems.at[place])
        for place, (source, target) in enumerate(
            (
                (land_hbm, land),
                (aggregate_hbm, aggregate),
                (coup_hbm, vert_coup),
                (diag_hbm, vert_diag),
                (east_hbm, face_east),
                (north_hbm, face_north),
            )
        )
    ]
    for copy in small:
        copy.start()
    for copy in small:
        copy.wait()
    lane = lax.broadcasted_iota(jnp.int32, (1, levels), 1)
    live = [
        jnp.where(jnp.full((1, levels), aggregate[q // 2, q % 2]) >= 0, 1.0, 0.0) for q in range(4)
    ]
    count = live[0] + live[1] + live[2] + live[3]
    scale = jnp.sqrt(jnp.maximum(count, 1.0))
    for q in range(4):
        x, y = q // 2, q % 2
        coupling = vert_coup[x, y : y + 1, :]
        up = jnp.where(lane < levels - 1, coupling, 0.0)
        down = jnp.where(lane > 0, pltpu.roll(coupling, 1, axis=1), 0.0)
        is_open = jnp.full((1, levels), land[x, y]).astype(jnp.float32)
        rows = [
            vert_diag[x, y : y + 1, :] + coupling + down,
            up,
            down,
            face_east[x, y : y + 1, :] * is_open,
            face_north[x, y : y + 1, :] * is_open,
            is_open,
            live[q] / scale,
            jnp.zeros((1, levels), jnp.float32),
        ]
        block = jnp.concatenate(rows, axis=0)
        for ref, base in ((both, 4 * levels), (to_near, 2 * levels), (to_far, 2 * levels)):
            ref[base + q * COEF_ROWS : base + (q + 1) * COEF_ROWS, :] = block
    whole.wait()
    even_lon = lon == 0
    for y in range(2):
        low, high = inverse[0, y], inverse[1, y]
        both[y * levels : (y + 1) * levels, :] = low
        both[(2 + y) * levels : (3 + y) * levels, :] = high
        to_near[y * levels : (y + 1) * levels, :] = jnp.where(even_lon, high, low)
        to_far[y * levels : (y + 1) * levels, :] = jnp.where(even_lon, low, high)


def parities():
    even_lon = lax.rem(lax.axis_index("lon"), 2) == 0
    even_lat = lax.rem(lax.axis_index("lat"), 2) == 0
    return even_lon, even_lat


def has_lat_far():
    index = lax.axis_index("lat")
    return index != jnp.where(lax.rem(index, 2) == 0, 0, lax.axis_size("lat") - 1)


def wide_kernel(facing_far, own, ring, wide):
    even_lon, _ = parities()
    levels = own.shape[1]
    high = jnp.logical_not(even_lon) if facing_far else even_lon
    for y in range(2):
        low_rows = own[y * levels : (y + 1) * levels, :]
        high_rows = own[(2 + y) * levels : (3 + y) * levels, :]
        wide[y * levels : (y + 1) * levels, :] = jnp.where(high, high_rows, low_rows)
    base = 2 * levels
    coef = [ring[base + q * COEF_ROWS : base + (q + 1) * COEF_ROWS, :] for q in range(4)]
    for y in range(2):
        beyond = jnp.where(high, coef[y], coef[2 + y])
        wide[base + y * COEF_ROWS : base + (y + 1) * COEF_ROWS, :] = beyond


def fill_corner(lon_near, lon_far, lat_near, lat_far, out, near):
    even_lon, even_lat = parities()
    levels = lon_near.shape[1]
    base = 2 * levels

    def block(values, q, first=0):
        return values[q * COEF_ROWS + first : q * COEF_ROWS + (WEIGHT + 1 if first else COEF_ROWS), :]

    def sides(rows):
        near, far = lon_near[rows, :], lon_far[rows, :]
        return jnp.where(even_lon, far, near), jnp.where(even_lon, near, far)

    low = sides(slice(0, levels))
    high = sides(slice(levels, base))
    coefs = sides(slice(base, lon_near.shape[0]))
    lat = slice(2 * base, lat_near.shape[0])
    lower = jnp.logical_not(even_lat) if near else even_lat
    other = jnp.where(has_lat_far(), lat_far[lat, :], 0.0) if near else lat_near[lat, :]
    rows = []
    for place, facing in enumerate((1, 0)):
        out[place * levels : (place + 1) * levels, :] = jnp.where(lower, low[place], high[place])
        choices = []
        for y in (0, 1):
            corner, beside, behind = 2 * facing + y, 2 * (1 - facing) + y, 2 * facing + 1 - y
            choices.append(
                [block(coefs[place], corner)]
                + [block(coefs[place], q, EAST) for q in (beside, behind)]
            )
        rows += [jnp.where(lower, *pair) for pair in zip(*choices)]
    for x in (0, 1):
        choices = (block(other, 2 * x + y, EAST) for y in (0, 1))
        rows.append(jnp.where(lower, *choices))
    out[base : base + CORNER_ROWS, :] = jnp.concatenate(rows, axis=0)


def corner_kernel(lon_near, lon_far, lat_near, lat_far, to_far):
    fill_corner(lon_near, lon_far, lat_near, lat_far, to_far, False)


def split(values):
    high = values.astype(jnp.bfloat16)
    return high, (values - high.astype(jnp.float32)).astype(jnp.bfloat16)


def product(left, right):
    return product_of_parts(left, *split(right))


def product_of_parts(left, right_high, right_low):
    left_high, left_low = split(left)
    return jnp.dot(
        jnp.concatenate([left_high, left_high, left_low], axis=1),
        jnp.concatenate([right_high, right_low, right_high], axis=0),
        preferred_element_type=jnp.float32,
    )


def left(values):
    return pltpu.roll(values, 1, axis=1)


def right(values):
    return pltpu.roll(values, values.shape[1] - 1, axis=1)


class Stencil:
    def __init__(self, own, lon_near, lon_far, wide_near, wide_far, lat_near, lat_far, corner_near=None, corner_far=None):
        even_lon, even_lat = parities()
        levels = own.shape[1]
        size = 4 * COEF_ROWS
        full = 4 * levels
        half = 2 * levels
        self.levels = levels
        self.wide = {3: (even_lon, wide_near, wide_far), -2: (even_lon, wide_far, wide_near)}
        sources = {
            (0, 0): (None, own, own, full),
            (1, 0): (even_lon, lon_near, lon_far, half),
            (-1, 0): (even_lon, lon_far, lon_near, half),
            (0, 1): (even_lat, lat_near, lat_far, full),
            (0, -1): (even_lat, lat_far, lat_near, full),
        }
        self.sources = sources
        self.coefs = {place: self.fetch(*source, size) for place, source in sources.items()}
        far = has_lat_far()
        keep = {1: jnp.logical_or(even_lat, far), -1: jnp.logical_or(jnp.logical_not(even_lat), far)}
        for place in sources:
            if place[1] != 0:
                inside = keep[1 if place[1] > 0 else -1]
                self.coefs[place] = jnp.where(inside, self.coefs[place], 0.0)
        self.parts = {}
        if corner_near is not None:
            self.corners = {1: (even_lat, corner_near, corner_far), -1: (even_lat, corner_far, corner_near)}
            for side, source in self.corners.items():
                rows = jnp.where(keep[side], self.fetch(*source, half, CORNER_ROWS), 0.0)
                facing, behind, beyond = (2, 3, 4) if side > 0 else (-1, -2, -3)
                start = 0
                for x, beside in ((-1, -2), (2, 3)):
                    self.parts[x, facing] = (rows, start)
                    self.parts[beside, facing] = (rows, start + COEF_ROWS - EAST)
                    self.parts[x, behind] = (rows, start + COEF_ROWS + 4 - EAST)
                    start += COEF_ROWS + 8
                for x in (0, 1):
                    self.parts[x, beyond] = (rows, start + 4 * x - EAST)
        pair = 2 * COEF_ROWS
        for x, source in self.wide.items() if wide_near is not None else ():
            beyond = self.fetch(*source, half, pair)
            self.coefs[2 if x > 0 else -2, 0] = jnp.concatenate([beyond, beyond], axis=0)
        self.east = functools.cache(self.east)
        self.north = functools.cache(self.north)
        self.main = functools.cache(self.main)

    def fetch(self, flag, first, other, start, count):
        if flag is None:
            return first[start : start + count, :]
        return jnp.where(flag, first[start : start + count, :], other[start : start + count, :])

    def coef(self, x, y, row):
        if (x, y) in self.parts:
            rows, start = self.parts[x, y]
            return rows[start + row : start + row + 1, :]
        at = (2 * (x % 2) + y % 2) * COEF_ROWS + row
        return self.coefs[x // 2, y // 2][at : at + 1, :]

    def weight(self, x, y):
        return self.coef(x, y, WEIGHT)

    def east(self, x, y):
        return self.coef(x, y, EAST) * self.coef(x + 1, y, OPEN)

    def north(self, x, y):
        return self.coef(x, y, NORTH) * self.coef(x, y + 1, OPEN)

    def main(self, x, y):
        lon = self.east(x, y) + self.east(x - 1, y)
        return self.coef(x, y, DIAG) + lon + self.north(x, y) + self.north(x, y - 1)

    def outer_face(self, x, y):
        if x in (0, 1):
            return self.east(x - 1, y) if x == 0 else self.east(x, y)
        return self.north(x, y - 1) if y == 0 else self.north(x, y)

    def inner_main(self, x, y):
        if x in (0, 1):
            inner = self.east(0, y) + self.north(x, y) + self.north(x, y - 1)
        else:
            inner = self.north(x, 0) + self.east(x, y) + self.east(x - 1, y)
        return self.coef(x, y, DIAG) + inner

    def lon_faces(self, x, y):
        above = self.east(x, y) * self.weight(x + 1, y)
        below = self.east(x - 1, y) * self.weight(x - 1, y)
        return (above, below) if x % 2 == 0 else (below, above)

    def lat_faces(self, x, y):
        above = self.north(x, y) * self.weight(x, y + 1)
        below = self.north(x, y - 1) * self.weight(x, y - 1)
        return (above, below) if y % 2 == 0 else (below, above)

    def own_diag(self, x, y):
        return (
            self.weight(x, y) * self.main(x, y) - self.lon_faces(x, y)[0] - self.lat_faces(x, y)[0]
        )

    def inverse(self, x, y):
        lon, lat = x // 2, y // 2
        levels = self.levels
        if x in self.wide:
            return self.fetch(*self.wide[x], y % 2 * levels, levels)
        if lon != 0 and lat != 0:
            return self.fetch(*self.corners[lat], 0 if lon < 0 else levels, levels)
        elif lon != 0:
            start = y % 2 * levels
        else:
            start = (2 * (x % 2) + y % 2) * levels
        return self.fetch(*self.sources[lon, lat][:3], start, levels)

    def residual(self, rows_t, x, y, main=None):
        total = None
        if (x, y) in rows_t:
            block = rows_t[x, y]
            total = (
                block * (self.main if main is None else main)(x, y)
                - left(block * self.coef(x, y, UP))
                - right(block * self.coef(x, y, DOWN))
            )
        for near, face in (
            ((x + 1, y), lambda: self.east(x, y)),
            ((x - 1, y), lambda: self.east(x - 1, y)),
            ((x, y + 1), lambda: self.north(x, y)),
            ((x, y - 1), lambda: self.north(x, y - 1)),
        ):
            if near in rows_t:
                term = rows_t[near] * face()
                total = -term if total is None else total - term
        return total


own_cells = [(x, y) for x in (0, 1) for y in (0, 1)]
lon_cells = [(x, y) for x in (-1, 2) for y in (0, 1)]
lat_cells = [(x, y) for x in (0, 1) for y in (-1, 2)]
near_cells = lon_cells + lat_cells
reach_cells = own_cells + near_cells
lon_far_cells = [(x, y) for x in (-2, 3) for y in (0, 1)]
lat_far_cells = [(x, y) for x in (0, 1) for y in (-2, 3)]
far_cells = lon_far_cells + lat_far_cells
corner_cells = [(2, 2), (2, -1), (-1, 2), (-1, -1)]
groups = {}
for cell in corner_cells + lon_far_cells + lon_cells + lat_far_cells + lat_cells:
    groups.setdefault((cell[0] // 2, cell[1] // 2), []).append(cell)
first_targets = [(0, 0), (1, 0), (-1, 0), (0, 1), (0, -1)]


class Sums:
    def __init__(self, out, targets, started=()):
        self.out = out
        self.slots = {target: place for place, target in enumerate(targets)}
        self.started = set(started)

    def add(self, target, term):
        place = self.slots[target]
        if target in self.started:
            self.out[place] += term
        else:
            self.out[place] = term
            self.started.add(target)


def lateral_targets(x, y):
    lon, lat = x // 2, y // 2
    return (lon + (-1 if x % 2 == 0 else 1), lat), (lon, lat + (-1 if y % 2 == 0 else 1))


def apply_columns(cells, sums, x, y, smooth):
    lon_target, lat_target = lateral_targets(x, y)
    sums.add(lon_target, smooth * cells.lon_faces(x, y)[1])
    sums.add(lat_target, smooth * cells.lat_faces(x, y)[1])
    weight = cells.weight(x, y)
    return (
        smooth * cells.own_diag(x, y),
        smooth * (weight * cells.coef(x, y, UP)),
        smooth * (weight * cells.coef(x, y, DOWN)),
    )


def plus(parts, more):
    return more if parts is None else tuple(a + b for a, b in zip(parts, more))


def close_kernel(own, lon_near, lon_far, lat_near, lat_far, rows_out, smooth_out, partial, rest_out, high_out, low_out, to_near):
    fill_corner(lon_near, lon_far, lat_near, lat_far, to_near, True)
    cells = Stencil(own, lon_near, lon_far, None, None, lat_near, lat_far)
    levels = cells.levels
    row = lax.broadcasted_iota(jnp.int32, (levels, levels), 0)
    lane = lax.broadcasted_iota(jnp.int32, (levels, levels), 1)
    rows_t = {}
    for x, y in own_cells:
        block = cells.inverse(x, y)
        weight = cells.weight(x, y)
        smoothed = (
            block * cells.own_diag(x, y)
            - left(block * (weight * cells.coef(x, y, UP)))
            - right(block * (weight * cells.coef(x, y, DOWN)))
        )
        rows_t[x, y] = (jnp.where(row == lane, weight, 0.0) - relax_weight * smoothed).T
    for x, y in lon_cells:
        rows_t[x, y] = (cells.inverse(x, y) * (relax_weight * cells.lon_faces(x, y)[1])).T
    for x, y in lat_cells:
        rows_t[x, y] = (cells.inverse(x, y) * (relax_weight * cells.lat_faces(x, y)[1])).T
    for place, cell in enumerate(reach_cells):
        rows_out[place] = rows_t[cell]
    sums = Sums(partial, first_targets)
    parts = None
    for x, y in own_cells:
        rest = cells.residual(rows_t, x, y)
        smooth = product(rest, cells.inverse(x, y)) * relax_weight
        terms = apply_columns(cells, sums, x, y, smooth)
        parts = plus(parts, (rest * cells.weight(x, y) - terms[0],) + terms[1:])
    sums.add((0, 0), parts[0] + left(parts[1]) + right(parts[2]))
    for x, y in far_cells:
        rest = cells.residual(rows_t, x, y)
        sums.add((x // 2, y // 2), rest * cells.weight(x, y))
        if (x, y) in lat_far_cells:
            smooth = product(rest, cells.inverse(x, y))
            smooth_out[lat_far_cells.index((x, y))] = smooth
    for place, (x, y) in enumerate(near_cells):
        rest_out[place] = cells.residual(rows_t, x, y, cells.inner_main)
        high_out[place], low_out[place] = split(cells.inverse(x, y))


def wide_products_kernel(own, lon_near, lon_far, wide_near, wide_far, lat_near, lat_far, rows_in, smooth_out):
    cells = Stencil(own, lon_near, lon_far, wide_near, wide_far, lat_near, lat_far)
    rows_t = {cell: rows_in[place] for place, cell in enumerate(reach_cells) if cell in lon_cells}
    for place, (x, y) in enumerate(lon_far_cells):
        rest = cells.residual(rows_t, x, y)
        smooth_out[place] = product(rest, cells.inverse(x, y))


product_cells = corner_cells + near_cells


target_order = [(-2, 0), (2, 0), (0, -2), (0, 2)] + [
    target for target in stencil_offsets if 2 not in target and -2 not in target
]


def coarse_kernel(*refs):
    cells = Stencil(*refs[:9])
    rows_in, lat_smooth, partial, rest_in, high_in, low_in, lon_smooth = refs[9:16]
    out, blocks, rests, smooths, sems = refs[16:]
    levels = cells.levels
    rows_t = {cell: rows_in[place] for place, cell in enumerate(reach_cells)}
    smooth_of, rest_of = {}, {}
    for place, cell in enumerate(lon_far_cells):
        smooth_of[cell] = lon_smooth.at[place]
    for place, cell in enumerate(lat_far_cells):
        smooth_of[cell] = lat_smooth.at[place]
    for place, (x, y) in enumerate(product_cells):
        if (x, y) in near_cells:
            known = near_cells.index((x, y))
            rest = rest_in[known] + rows_t[x, y] * cells.outer_face(x, y)
            smooths[place] = product_of_parts(rest, high_in[known], low_in[known])
        else:
            rest = cells.residual(rows_t, x, y)
            smooths[place] = product(rest, cells.inverse(x, y))
        rests[place] = rest
        rest_of[x, y], smooth_of[x, y] = rests.at[place], smooths.at[place]
    lateral, own = {}, {}
    for device, members in groups.items():
        for x, y in members:
            lon_target, lat_target = lateral_targets(x, y)
            for target, faces in ((lon_target, cells.lon_faces), (lat_target, cells.lat_faces)):
                lateral.setdefault(target, []).append(((x, y), faces(x, y)[1] * relax_weight))
            weight = cells.weight(x, y) * relax_weight
            factors = (
                cells.own_diag(x, y) * relax_weight,
                weight * cells.coef(x, y, UP),
                weight * cells.coef(x, y, DOWN),
            )
            own.setdefault(device, []).append(((x, y), factors))
    slots = {target: place for place, target in enumerate(stencil_offsets)}
    copies = []
    strip = levels // 4
    for target in target_order:
        for start in range(0, levels, strip):
            rows = slice(start, start + strip)
            total = None
            if target in first_targets:
                total = partial[first_targets.index(target), rows, :]
            for cell, factor in lateral.get(target, ()):
                term = smooth_of[cell][rows, :] * factor
                total = term if total is None else total + term
            parts = None
            for cell, factors in own.get(target, ()):
                smooth = smooth_of[cell][rows, :]
                terms = [smooth * factor for factor in factors]
                if cell in rest_of:
                    terms[0] = terms[0] - rest_of[cell][rows, :] * cells.weight(*cell)
                parts = plus(parts, tuple(terms))
            if parts is not None:
                total = total - parts[0] + left(parts[1]) + right(parts[2])
            blocks[slots[target], rows, :] = total
        place = slots[target]
        copies.append(pltpu.make_async_copy(blocks.at[place], out.at[place], sems.at[place]))
        copies[-1].start()
    for copy in copies:
        copy.wait()


def local(inverse, vert_diag, vert_coup, face_east, face_north, land_mask, aggregate):
    levels = inverse.shape[-1]
    size = 4 * COEF_ROWS
    args = (inverse, vert_diag, vert_coup, face_east, face_north, land_mask, aggregate)
    vmem = pl.BlockSpec(memory_space=pltpu.VMEM)
    params = pltpu.CompilerParams(vmem_limit_bytes=8 * 1024 * 1024)
    array = lambda count: jax.ShapeDtypeStruct((count, levels), jnp.float32)
    cost = lambda size: pl.CostEstimate(flops=size * 10**6, bytes_accessed=size * 10**3, transcendentals=0)
    shapes = [4 * levels + size] + [2 * levels + size] * 2
    both, to_near, to_far = pl.pallas_call(
        pack_kernel,
        out_shape=tuple(pltpu.VMEM((rows, levels), jnp.float32) for rows in shapes),
        in_specs=[pl.BlockSpec(memory_space=pltpu.HBM)] * 7,
        out_specs=(vmem,) * 3,
        scratch_shapes=[pltpu.VMEM(arg.shape, arg.dtype) for arg in args[:5]]
        + [pltpu.SMEM(arg.shape, arg.dtype) for arg in args[5:]]
        + [pltpu.SemaphoreType.DMA((7,))],
        compiler_params=pltpu.CompilerParams(vmem_limit_bytes=8 * 1024 * 1024),
    )(*(pltpu.with_memory_space_constraint(arg, pltpu.HBM) for arg in args))
    lon_near = lax.ppermute(to_near, "lon", pair_near("lon"))
    lon_far = lax.ppermute(to_far, "lon", pair_far_closed("lon"))
    lat_near = lax.ppermute(both, "lat", pair_near("lat"))
    lat_far = exchange_lat_far(both)

    def widened(facing_far, ring, spare, weight):
        return pl.pallas_call(
            functools.partial(wide_kernel, facing_far),
            out_shape=array(2 * (levels + COEF_ROWS) + spare),
            in_specs=[vmem] * 2,
            out_specs=vmem,
            cost_estimate=cost(weight),
            compiler_params=params,
        )(both, ring)

    wide_far = lax.ppermute(widened(False, lon_near, 8, 1000), "lon", pair_far_closed("lon"))
    wide_near = lax.ppermute(widened(True, lon_far, 0, 8000), "lon", pair_near("lon"))
    corner_rows = 2 * levels + CORNER_ROWS
    corner_to_far = pl.pallas_call(
        corner_kernel,
        out_shape=array(corner_rows),
        in_specs=[vmem] * 4,
        out_specs=vmem,
        compiler_params=params,
    )(lon_near, lon_far, lat_near, lat_far)
    corner_far = exchange_lat_far(corner_to_far)
    blocks = lambda count: jax.ShapeDtypeStruct((count, levels, levels), jnp.float32)
    *close, corner_to_near = pl.pallas_call(
        close_kernel,
        out_shape=(
            *(blocks(len(cells)) for cells in (reach_cells, lat_far_cells, first_targets, near_cells)),
            *(jax.ShapeDtypeStruct((len(near_cells), levels, levels), jnp.bfloat16),) * 2,
            array(corner_rows),
        ),
        in_specs=[vmem] * 5,
        out_specs=(vmem,) * 7,
        cost_estimate=cost(1),
        compiler_params=params,
    )(both, lon_near, lon_far, lat_near, lat_far)
    corner_near = lax.ppermute(corner_to_near, "lat", pair_near("lat"))
    near_args = (both, lon_near, lon_far, wide_near, wide_far, lat_near, lat_far)
    lon_smooth = pl.pallas_call(
        wide_products_kernel,
        out_shape=blocks(len(lon_far_cells)),
        in_specs=[vmem] * 8,
        out_specs=vmem,
        cost_estimate=cost(50000),
        compiler_params=params,
    )(*near_args, close[0])
    out = pl.pallas_call(
        coarse_kernel,
        out_shape=blocks(len(stencil_offsets)),
        in_specs=[vmem] * 16,
        out_specs=pl.BlockSpec(memory_space=pltpu.HBM),
        scratch_shapes=[
            pltpu.VMEM((len(stencil_offsets), levels, levels), jnp.float32),
            *(pltpu.VMEM((len(product_cells), levels, levels), jnp.float32),) * 2,
            pltpu.SemaphoreType.DMA((len(stencil_offsets),)),
        ],
        compiler_params=params,
    )(*near_args, corner_near, corner_far, *close, lon_smooth)
    return out[None, None]


def solution(mesh):
    return jax.shard_map(
        local,
        mesh=mesh,
        in_specs=(
            P("lon", "lat", None, None),
            P("lon", "lat", None),
            P("lon", "lat", None),
            P("lon", "lat", None),
            P("lon", "lat", None),
            P("lon", "lat"),
            P("lon", "lat"),
        ),
        out_specs=P("lon", "lat", None, None, None),
        check_vma=False,
    )
```

```python
import functools

import jax
import jax.numpy as jnp
from jax import lax
from jax.experimental import pallas as pl
from jax.experimental.pallas import tpu as pltpu
from jax.sharding import PartitionSpec as P

relax_weight = 0.6
stencil_offsets = [
    (-2, 0),
    (-1, -1),
    (-1, 0),
    (-1, 1),
    (0, -2),
    (0, -1),
    (0, 0),
    (0, 1),
    (0, 2),
    (1, -1),
    (1, 0),
    (1, 1),
    (2, 0),
]
DIAG, UP, DOWN, EAST, NORTH, OPEN, WEIGHT = range(7)
COEF_ROWS = 8
CORNER_ROWS = 2 * (COEF_ROWS + 2 * 4) + 2 * 4


def pair_near(axis):
    count = lax.axis_size(axis)
    return [(i, i ^ 1) for i in range(count) if i ^ 1 < count]


def pair_far_closed(axis):
    count = lax.axis_size(axis)
    return [(i, (i - 1 if i % 2 == 0 else i + 1) % count) for i in range(count)]


def exchange_lat_far(values):
    lon_count, lat_count = lax.axis_size("lon"), lax.axis_size("lat")
    pairs = []
    for i in range(lon_count):
        for j in range(lat_count):
            partner = j - 1 if j % 2 == 0 else j + 1
            if 0 <= partner < lat_count:
                pairs.append((i * lat_count + j, i * lat_count + partner))
            elif i ^ 2 < lon_count:
                pairs.append((i * lat_count + j, (i ^ 2) * lat_count + j))
    return lax.ppermute(values, ("lon", "lat"), pairs)


def pack_kernel(
    inverse_hbm,
    diag_hbm,
    coup_hbm,
    east_hbm,
    north_hbm,
    land_hbm,
    aggregate_hbm,
    both,
    to_near,
    to_far,
    inverse,
    vert_diag,
    vert_coup,
    face_east,
    face_north,
    land,
    aggregate,
    small_sems,
):
    lon = lax.rem(lax.axis_index("lon"), 2)
    levels = inverse.shape[-1]
    whole = pltpu.make_async_copy(inverse_hbm, inverse, small_sems.at[6])
    whole.start()
    small = [
        pltpu.make_async_copy(source, target, small_sems.at[place])
        for place, (source, target) in enumerate(
            (
                (land_hbm, land),
                (aggregate_hbm, aggregate),
                (coup_hbm, vert_coup),
                (diag_hbm, vert_diag),
                (east_hbm, face_east),
                (north_hbm, face_north),
            )
        )
    ]
    for copy in small:
        copy.start()
    for copy in small:
        copy.wait()
    lane = lax.broadcasted_iota(jnp.int32, (1, levels), 1)
    live = [
        jnp.where(jnp.full((1, levels), aggregate[q // 2, q % 2]) >= 0, 1.0, 0.0) for q in range(4)
    ]
    count = live[0] + live[1] + live[2] + live[3]
    scale = jnp.sqrt(jnp.maximum(count, 1.0))
    for q in range(4):
        x, y = q // 2, q % 2
        coupling = vert_coup[x, y : y + 1, :]
        up = jnp.where(lane < levels - 1, coupling, 0.0)
        down = jnp.where(lane > 0, pltpu.roll(coupling, 1, axis=1), 0.0)
        is_open = jnp.full((1, levels), land[x, y]).astype(jnp.float32)
        rows = [
            vert_diag[x, y : y + 1, :] + coupling + down,
            up,
            down,
            face_east[x, y : y + 1, :] * is_open,
            face_north[x, y : y + 1, :] * is_open,
            is_open,
            live[q] / scale,
            jnp.zeros((1, levels), jnp.float32),
        ]
        block = jnp.concatenate(rows, axis=0)
        for ref, base in ((both, 4 * levels), (to_near, 2 * levels), (to_far, 2 * levels)):
            ref[base + q * COEF_ROWS : base + (q + 1) * COEF_ROWS, :] = block
    whole.wait()
    even_lon = lon == 0
    for y in range(2):
        low, high = inverse[0, y], inverse[1, y]
        both[y * levels : (y + 1) * levels, :] = low
        both[(2 + y) * levels : (3 + y) * levels, :] = high
        to_near[y * levels : (y + 1) * levels, :] = jnp.where(even_lon, high, low)
        to_far[y * levels : (y + 1) * levels, :] = jnp.where(even_lon, low, high)


def parities():
    even_lon = lax.rem(lax.axis_index("lon"), 2) == 0
    even_lat = lax.rem(lax.axis_index("lat"), 2) == 0
    return even_lon, even_lat


def has_lat_far():
    index = lax.axis_index("lat")
    return index != jnp.where(lax.rem(index, 2) == 0, 0, lax.axis_size("lat") - 1)


def wide_kernel(facing_far, own, ring, wide):
    even_lon, _ = parities()
    levels = own.shape[1]
    high = jnp.logical_not(even_lon) if facing_far else even_lon
    for y in range(2):
        low_rows = own[y * levels : (y + 1) * levels, :]
        high_rows = own[(2 + y) * levels : (3 + y) * levels, :]
        wide[y * levels : (y + 1) * levels, :] = jnp.where(high, high_rows, low_rows)
    base = 2 * levels
    coef = [ring[base + q * COEF_ROWS : base + (q + 1) * COEF_ROWS, :] for q in range(4)]
    for y in range(2):
        beyond = jnp.where(high, coef[y], coef[2 + y])
        wide[base + y * COEF_ROWS : base + (y + 1) * COEF_ROWS, :] = beyond


def fill_corner(lon_near, lon_far, lat_near, lat_far, out, near):
    even_lon, even_lat = parities()
    levels = lon_near.shape[1]
    base = 2 * levels

    def block(values, q, first=0):
        return values[q * COEF_ROWS + first : q * COEF_ROWS + (WEIGHT + 1 if first else COEF_ROWS), :]

    def sides(rows):
        near, far = lon_near[rows, :], lon_far[rows, :]
        return jnp.where(even_lon, far, near), jnp.where(even_lon, near, far)

    low = sides(slice(0, levels))
    high = sides(slice(levels, base))
    coefs = sides(slice(base, lon_near.shape[0]))
    lat = slice(2 * base, lat_near.shape[0])
    lower = jnp.logical_not(even_lat) if near else even_lat
    other = jnp.where(has_lat_far(), lat_far[lat, :], 0.0) if near else lat_near[lat, :]
    rows = []
    for place, facing in enumerate((1, 0)):
        out[place * levels : (place + 1) * levels, :] = jnp.where(lower, low[place], high[place])
        choices = []
        for y in (0, 1):
            corner, beside, behind = 2 * facing + y, 2 * (1 - facing) + y, 2 * facing + 1 - y
            choices.append(
                [block(coefs[place], corner)]
                + [block(coefs[place], q, EAST) for q in (beside, behind)]
            )
        rows += [jnp.where(lower, *pair) for pair in zip(*choices)]
    for x in (0, 1):
        choices = (block(other, 2 * x + y, EAST) for y in (0, 1))
        rows.append(jnp.where(lower, *choices))
    out[base : base + CORNER_ROWS, :] = jnp.concatenate(rows, axis=0)


def corner_kernel(lon_near, lon_far, lat_near, lat_far, to_far):
    fill_corner(lon_near, lon_far, lat_near, lat_far, to_far, False)


def split(values):
    high = values.astype(jnp.bfloat16)
    return high, (values - high.astype(jnp.float32)).astype(jnp.bfloat16)


def product(left, right):
    return product_of_parts(left, *split(right))


def product_of_parts(left, right_high, right_low):
    left_high, left_low = split(left)
    return jnp.dot(
        jnp.concatenate([left_high, left_high, left_low], axis=1),
        jnp.concatenate([right_high, right_low, right_high], axis=0),
        preferred_element_type=jnp.float32,
    )


def left(values):
    return pltpu.roll(values, 1, axis=1)


def right(values):
    return pltpu.roll(values, values.shape[1] - 1, axis=1)


class Stencil:
    def __init__(self, own, lon_near, lon_far, wide_near, wide_far, lat_near, lat_far, corner_near=None, corner_far=None):
        even_lon, even_lat = parities()
        levels = own.shape[1]
        size = 4 * COEF_ROWS
        full = 4 * levels
        half = 2 * levels
        self.levels = levels
        self.wide = {3: (even_lon, wide_near, wide_far), -2: (even_lon, wide_far, wide_near)}
        sources = {
            (0, 0): (None, own, own, full),
            (1, 0): (even_lon, lon_near, lon_far, half),
            (-1, 0): (even_lon, lon_far, lon_near, half),
            (0, 1): (even_lat, lat_near, lat_far, full),
            (0, -1): (even_lat, lat_far, lat_near, full),
        }
        self.sources = sources
        self.coefs = {place: self.fetch(*source, size) for place, source in sources.items()}
        far = has_lat_far()
        keep = {1: jnp.logical_or(even_lat, far), -1: jnp.logical_or(jnp.logical_not(even_lat), far)}
        for place in sources:
            if place[1] != 0:
                inside = keep[1 if place[1] > 0 else -1]
                self.coefs[place] = jnp.where(inside, self.coefs[place], 0.0)
        self.parts = {}
        if corner_near is not None:
            self.corners = {1: (even_lat, corner_near, corner_far), -1: (even_lat, corner_far, corner_near)}
            for side, source in self.corners.items():
                rows = jnp.where(keep[side], self.fetch(*source, half, CORNER_ROWS), 0.0)
                facing, behind, beyond = (2, 3, 4) if side > 0 else (-1, -2, -3)
                start = 0
                for x, beside in ((-1, -2), (2, 3)):
                    self.parts[x, facing] = (rows, start)
                    self.parts[beside, facing] = (rows, start + COEF_ROWS - EAST)
                    self.parts[x, behind] = (rows, start + COEF_ROWS + 4 - EAST)
                    start += COEF_ROWS + 8
                for x in (0, 1):
                    self.parts[x, beyond] = (rows, start + 4 * x - EAST)
        pair = 2 * COEF_ROWS
        for x, source in self.wide.items() if wide_near is not None else ():
            beyond = self.fetch(*source, half, pair)
            self.coefs[2 if x > 0 else -2, 0] = jnp.concatenate([beyond, beyond], axis=0)
        self.east = functools.cache(self.east)
        self.north = functools.cache(self.north)
        self.main = functools.cache(self.main)

    def fetch(self, flag, first, other, start, count):
        if flag is None:
            return first[start : start + count, :]
        return jnp.where(flag, first[start : start + count, :], other[start : start + count, :])

    def coef(self, x, y, row):
        if (x, y) in self.parts:
            rows, start = self.parts[x, y]
            return rows[start + row : start + row + 1, :]
        at = (2 * (x % 2) + y % 2) * COEF_ROWS + row
        return self.coefs[x // 2, y // 2][at : at + 1, :]

    def weight(self, x, y):
        return self.coef(x, y, WEIGHT)

    def east(self, x, y):
        return self.coef(x, y, EAST) * self.coef(x + 1, y, OPEN)

    def north(self, x, y):
        return self.coef(x, y, NORTH) * self.coef(x, y + 1, OPEN)

    def main(self, x, y):
        lon = self.east(x, y) + self.east(x - 1, y)
        return self.coef(x, y, DIAG) + lon + self.north(x, y) + self.north(x, y - 1)

    def outer_face(self, x, y):
        if x in (0, 1):
            return self.east(x - 1, y) if x == 0 else self.east(x, y)
        return self.north(x, y - 1) if y == 0 else self.north(x, y)

    def inner_main(self, x, y):
        if x in (0, 1):
            inner = self.east(0, y) + self.north(x, y) + self.north(x, y - 1)
        else:
            inner = self.north(x, 0) + self.east(x, y) + self.east(x - 1, y)
        return self.coef(x, y, DIAG) + inner

    def lon_faces(self, x, y):
        above = self.east(x, y) * self.weight(x + 1, y)
        below = self.east(x - 1, y) * self.weight(x - 1, y)
        return (above, below) if x % 2 == 0 else (below, above)

    def lat_faces(self, x, y):
        above = self.north(x, y) * self.weight(x, y + 1)
        below = self.north(x, y - 1) * self.weight(x, y - 1)
        return (above, below) if y % 2 == 0 else (below, above)

    def own_diag(self, x, y):
        return (
            self.weight(x, y) * self.main(x, y) - self.lon_faces(x, y)[0] - self.lat_faces(x, y)[0]
        )

    def inverse(self, x, y):
        lon, lat = x // 2, y // 2
        levels = self.levels
        if x in self.wide:
            return self.fetch(*self.wide[x], y % 2 * levels, levels)
        if lon != 0 and lat != 0:
            return self.fetch(*self.corners[lat], 0 if lon < 0 else levels, levels)
        elif lon != 0:
            start = y % 2 * levels
        else:
            start = (2 * (x % 2) + y % 2) * levels
        return self.fetch(*self.sources[lon, lat][:3], start, levels)

    def residual(self, rows_t, x, y, main=None):
        total = None
        if (x, y) in rows_t:
            block = rows_t[x, y]
            total = (
                block * (self.main if main is None else main)(x, y)
                - left(block * self.coef(x, y, UP))
                - right(block * self.coef(x, y, DOWN))
            )
        for near, face in (
            ((x + 1, y), lambda: self.east(x, y)),
            ((x - 1, y), lambda: self.east(x - 1, y)),
            ((x, y + 1), lambda: self.north(x, y)),
            ((x, y - 1), lambda: self.north(x, y - 1)),
        ):
            if near in rows_t:
                term = rows_t[near] * face()
                total = -term if total is None else total - term
        return total


own_cells = [(x, y) for x in (0, 1) for y in (0, 1)]
lon_cells = [(x, y) for x in (-1, 2) for y in (0, 1)]
lat_cells = [(x, y) for x in (0, 1) for y in (-1, 2)]
near_cells = lon_cells + lat_cells
reach_cells = own_cells + near_cells
lon_far_cells = [(x, y) for x in (-2, 3) for y in (0, 1)]
lat_far_cells = [(x, y) for x in (0, 1) for y in (-2, 3)]
far_cells = lon_far_cells + lat_far_cells
corner_cells = [(2, 2), (2, -1), (-1, 2), (-1, -1)]
groups = {}
for cell in corner_cells + lon_far_cells + lon_cells + lat_far_cells + lat_cells:
    groups.setdefault((cell[0] // 2, cell[1] // 2), []).append(cell)
first_targets = [(0, 0), (1, 0), (-1, 0), (0, 1), (0, -1)]


class Sums:
    def __init__(self, out, targets, started=()):
        self.out = out
        self.slots = {target: place for place, target in enumerate(targets)}
        self.started = set(started)

    def add(self, target, term):
        place = self.slots[target]
        if target in self.started:
            self.out[place] += term
        else:
            self.out[place] = term
            self.started.add(target)


def lateral_targets(x, y):
    lon, lat = x // 2, y // 2
    return (lon + (-1 if x % 2 == 0 else 1), lat), (lon, lat + (-1 if y % 2 == 0 else 1))


def apply_columns(cells, sums, x, y, smooth):
    lon_target, lat_target = lateral_targets(x, y)
    sums.add(lon_target, smooth * cells.lon_faces(x, y)[1])
    sums.add(lat_target, smooth * cells.lat_faces(x, y)[1])
    weight = cells.weight(x, y)
    return (
        smooth * cells.own_diag(x, y),
        smooth * (weight * cells.coef(x, y, UP)),
        smooth * (weight * cells.coef(x, y, DOWN)),
    )


def plus(parts, more):
    return more if parts is None else tuple(a + b for a, b in zip(parts, more))


def close_kernel(own, lon_near, lon_far, lat_near, lat_far, rows_out, smooth_out, partial, rest_out, high_out, low_out, to_near):
    fill_corner(lon_near, lon_far, lat_near, lat_far, to_near, True)
    cells = Stencil(own, lon_near, lon_far, None, None, lat_near, lat_far)
    levels = cells.levels
    row = lax.broadcasted_iota(jnp.int32, (levels, levels), 0)
    lane = lax.broadcasted_iota(jnp.int32, (levels, levels), 1)
    rows_t = {}
    for x, y in own_cells:
        block = cells.inverse(x, y)
        weight = cells.weight(x, y)
        smoothed = (
            block * cells.own_diag(x, y)
            - left(block * (weight * cells.coef(x, y, UP)))
            - right(block * (weight * cells.coef(x, y, DOWN)))
        )
        rows_t[x, y] = (jnp.where(row == lane, weight, 0.0) - relax_weight * smoothed).T
    for x, y in lon_cells:
        rows_t[x, y] = (cells.inverse(x, y) * (relax_weight * cells.lon_faces(x, y)[1])).T
    for x, y in lat_cells:
        rows_t[x, y] = (cells.inverse(x, y) * (relax_weight * cells.lat_faces(x, y)[1])).T
    for place, cell in enumerate(reach_cells):
        rows_out[place] = rows_t[cell]
    sums = Sums(partial, first_targets)
    parts = None
    for x, y in own_cells:
        rest = cells.residual(rows_t, x, y)
        smooth = product(rest, cells.inverse(x, y)) * relax_weight
        terms = apply_columns(cells, sums, x, y, smooth)
        parts = plus(parts, (rest * cells.weight(x, y) - terms[0],) + terms[1:])
    sums.add((0, 0), parts[0] + left(parts[1]) + right(parts[2]))
    for x, y in far_cells:
        rest = cells.residual(rows_t, x, y)
        sums.add((x // 2, y // 2), rest * cells.weight(x, y))
        if (x, y) in lat_far_cells:
            smooth = product(rest, cells.inverse(x, y))
            smooth_out[lat_far_cells.index((x, y))] = smooth
    for place, (x, y) in enumerate(near_cells):
        rest_out[place] = cells.residual(rows_t, x, y, cells.inner_main)
        high_out[place], low_out[place] = split(cells.inverse(x, y))


def wide_products_kernel(own, lon_near, lon_far, wide_near, wide_far, lat_near, lat_far, rows_in, smooth_out):
    cells = Stencil(own, lon_near, lon_far, wide_near, wide_far, lat_near, lat_far)
    rows_t = {cell: rows_in[place] for place, cell in enumerate(reach_cells) if cell in lon_cells}
    for place, (x, y) in enumerate(lon_far_cells):
        rest = cells.residual(rows_t, x, y)
        smooth_out[place] = product(rest, cells.inverse(x, y))


product_cells = corner_cells + near_cells


target_order = [(-2, 0), (2, 0), (0, -2), (0, 2)] + [
    target for target in stencil_offsets if 2 not in target and -2 not in target
]


def coarse_kernel(*refs):
    cells = Stencil(*refs[:9])
    rows_in, lat_smooth, partial, rest_in, high_in, low_in, lon_smooth = refs[9:16]
    out, blocks, rests, smooths, sems = refs[16:]
    levels = cells.levels
    rows_t = {cell: rows_in[place] for place, cell in enumerate(reach_cells)}
    smooth_of, rest_of = {}, {}
    for place, cell in enumerate(lon_far_cells):
        smooth_of[cell] = lon_smooth.at[place]
    for place, cell in enumerate(lat_far_cells):
        smooth_of[cell] = lat_smooth.at[place]
    for place, (x, y) in enumerate(product_cells):
        if (x, y) in near_cells:
            known = near_cells.index((x, y))
            rest = rest_in[known] + rows_t[x, y] * cells.outer_face(x, y)
            smooths[place] = product_of_parts(rest, high_in[known], low_in[known])
        else:
            rest = cells.residual(rows_t, x, y)
            smooths[place] = product(rest, cells.inverse(x, y))
        rests[place] = rest
        rest_of[x, y], smooth_of[x, y] = rests.at[place], smooths.at[place]
    lateral, own = {}, {}
    for device, members in groups.items():
        for x, y in members:
            lon_target, lat_target = lateral_targets(x, y)
            for target, faces in ((lon_target, cells.lon_faces), (lat_target, cells.lat_faces)):
                lateral.setdefault(target, []).append(((x, y), faces(x, y)[1] * relax_weight))
            weight = cells.weight(x, y) * relax_weight
            factors = (
                cells.own_diag(x, y) * relax_weight,
                weight * cells.coef(x, y, UP),
                weight * cells.coef(x, y, DOWN),
            )
            own.setdefault(device, []).append(((x, y), factors))
    slots = {target: place for place, target in enumerate(stencil_offsets)}
    copies = []
    strip = levels // 4
    for target in target_order:
        for start in range(0, levels, strip):
            rows = slice(start, start + strip)
            total = None
            if target in first_targets:
                total = partial[first_targets.index(target), rows, :]
            for cell, factor in lateral.get(target, ()):
                term = smooth_of[cell][rows, :] * factor
                total = term if total is None else total + term
            parts = None
            for cell, factors in own.get(target, ()):
                smooth = smooth_of[cell][rows, :]
                terms = [smooth * factor for factor in factors]
                if cell in rest_of:
                    terms[0] = terms[0] - rest_of[cell][rows, :] * cells.weight(*cell)
                parts = plus(parts, tuple(terms))
            if parts is not None:
                total = total - parts[0] + left(parts[1]) + right(parts[2])
            blocks[slots[target], rows, :] = total
        place = slots[target]
        copies.append(pltpu.make_async_copy(blocks.at[place], out.at[place], sems.at[place]))
        copies[-1].start()
    for copy in copies:
        copy.wait()


def local(inverse, vert_diag, vert_coup, face_east, face_north, land_mask, aggregate):
    levels = inverse.shape[-1]
    size = 4 * COEF_ROWS
    args = (inverse, vert_diag, vert_coup, face_east, face_north, land_mask, aggregate)
    vmem = pl.BlockSpec(memory_space=pltpu.VMEM)
    params = pltpu.CompilerParams(vmem_limit_bytes=8 * 1024 * 1024)
    array = lambda count: jax.ShapeDtypeStruct((count, levels), jnp.float32)
    cost = lambda size: pl.CostEstimate(flops=size * 10**6, bytes_accessed=size * 10**3, transcendentals=0)
    shapes = [4 * levels + size] + [2 * levels + size] * 2
    both, to_near, to_far = pl.pallas_call(
        pack_kernel,
        out_shape=tuple(pltpu.VMEM((rows, levels), jnp.float32) for rows in shapes),
        in_specs=[pl.BlockSpec(memory_space=pltpu.HBM)] * 7,
        out_specs=(vmem,) * 3,
        scratch_shapes=[pltpu.VMEM(arg.shape, arg.dtype) for arg in args[:5]]
        + [pltpu.SMEM(arg.shape, arg.dtype) for arg in args[5:]]
        + [pltpu.SemaphoreType.DMA((7,))],
        compiler_params=pltpu.CompilerParams(vmem_limit_bytes=8 * 1024 * 1024),
    )(*(pltpu.with_memory_space_constraint(arg, pltpu.HBM) for arg in args))
    lon_near = lax.ppermute(to_near, "lon", pair_near("lon"))
    lon_far = lax.ppermute(to_far, "lon", pair_far_closed("lon"))
    lat_near = lax.ppermute(both, "lat", pair_near("lat"))
    lat_far = exchange_lat_far(both)

    def widened(facing_far, ring, spare, weight):
        return pl.pallas_call(
            functools.partial(wide_kernel, facing_far),
            out_shape=array(2 * (levels + COEF_ROWS) + spare),
            in_specs=[vmem] * 2,
            out_specs=vmem,
            cost_estimate=cost(weight),
            compiler_params=params,
        )(both, ring)

    wide_far = lax.ppermute(widened(False, lon_near, 0, 1000), "lon", pair_far_closed("lon"))
    wide_near = lax.ppermute(widened(True, lon_far, 0, 8000), "lon", pair_near("lon"))
    corner_rows = 2 * levels + CORNER_ROWS
    corner_to_far = pl.pallas_call(
        corner_kernel,
        out_shape=array(corner_rows),
        in_specs=[vmem] * 4,
        out_specs=vmem,
        compiler_params=params,
    )(lon_near, lon_far, lat_near, lat_far)
    corner_far = exchange_lat_far(corner_to_far)
    blocks = lambda count: jax.ShapeDtypeStruct((count, levels, levels), jnp.float32)
    *close, corner_to_near = pl.pallas_call(
        close_kernel,
        out_shape=(
            *(blocks(len(cells)) for cells in (reach_cells, lat_far_cells, first_targets, near_cells)),
            *(jax.ShapeDtypeStruct((len(near_cells), levels, levels), jnp.bfloat16),) * 2,
            array(corner_rows),
        ),
        in_specs=[vmem] * 5,
        out_specs=(vmem,) * 7,
        cost_estimate=cost(1),
        compiler_params=params,
    )(both, lon_near, lon_far, lat_near, lat_far)
    corner_near = lax.ppermute(corner_to_near, "lat", pair_near("lat"))
    near_args = (both, lon_near, lon_far, wide_near, wide_far, lat_near, lat_far)
    lon_smooth = pl.pallas_call(
        wide_products_kernel,
        out_shape=blocks(len(lon_far_cells)),
        in_specs=[vmem] * 8,
        out_specs=vmem,
        cost_estimate=cost(50000),
        compiler_params=params,
    )(*near_args, close[0])
    out = pl.pallas_call(
        coarse_kernel,
        out_shape=blocks(len(stencil_offsets)),
        in_specs=[vmem] * 16,
        out_specs=pl.BlockSpec(memory_space=pltpu.HBM),
        scratch_shapes=[
            pltpu.VMEM((len(stencil_offsets), levels, levels), jnp.float32),
            *(pltpu.VMEM((len(product_cells), levels, levels), jnp.float32),) * 2,
            pltpu.SemaphoreType.DMA((len(stencil_offsets),)),
        ],
        compiler_params=params,
    )(*near_args, corner_near, corner_far, *close, lon_smooth)
    return out[None, None]


def solution(mesh):
    return jax.shard_map(
        local,
        mesh=mesh,
        in_specs=(
            P("lon", "lat", None, None),
            P("lon", "lat", None),
            P("lon", "lat", None),
            P("lon", "lat", None),
            P("lon", "lat", None),
            P("lon", "lat"),
            P("lon", "lat"),
        ),
        out_specs=P("lon", "lat", None, None, None),
        check_vma=False,
    )
```

```python
import functools

import jax
import jax.numpy as jnp
from jax import lax
from jax.experimental import pallas as pl
from jax.experimental.pallas import tpu as pltpu
from jax.sharding import PartitionSpec as P

relax_weight = 0.6
stencil_offsets = [
    (-2, 0),
    (-1, -1),
    (-1, 0),
    (-1, 1),
    (0, -2),
    (0, -1),
    (0, 0),
    (0, 1),
    (0, 2),
    (1, -1),
    (1, 0),
    (1, 1),
    (2, 0),
]
DIAG, UP, DOWN, EAST, NORTH, OPEN, WEIGHT = range(7)
COEF_ROWS = 8
CORNER_ROWS = 2 * (COEF_ROWS + 2 * 4) + 2 * 4


def pair_near(axis):
    count = lax.axis_size(axis)
    return [(i, i ^ 1) for i in range(count) if i ^ 1 < count]


def pair_far_closed(axis):
    count = lax.axis_size(axis)
    return [(i, (i - 1 if i % 2 == 0 else i + 1) % count) for i in range(count)]


def exchange_lat_far(values):
    lon_count, lat_count = lax.axis_size("lon"), lax.axis_size("lat")
    pairs = []
    for i in range(lon_count):
        for j in range(lat_count):
            partner = j - 1 if j % 2 == 0 else j + 1
            if 0 <= partner < lat_count:
                pairs.append((i * lat_count + j, i * lat_count + partner))
            elif i ^ 2 < lon_count:
                pairs.append((i * lat_count + j, (i ^ 2) * lat_count + j))
    return lax.ppermute(values, ("lon", "lat"), pairs)


def pack_kernel(
    inverse_hbm,
    diag_hbm,
    coup_hbm,
    east_hbm,
    north_hbm,
    land_hbm,
    aggregate_hbm,
    both,
    to_near,
    to_far,
    inverse,
    vert_diag,
    vert_coup,
    face_east,
    face_north,
    land,
    aggregate,
    small_sems,
):
    lon = lax.rem(lax.axis_index("lon"), 2)
    levels = inverse.shape[-1]
    whole = pltpu.make_async_copy(inverse_hbm, inverse, small_sems.at[6])
    whole.start()
    small = [
        pltpu.make_async_copy(source, target, small_sems.at[place])
        for place, (source, target) in enumerate(
            (
                (land_hbm, land),
                (aggregate_hbm, aggregate),
                (coup_hbm, vert_coup),
                (diag_hbm, vert_diag),
                (east_hbm, face_east),
                (north_hbm, face_north),
            )
        )
    ]
    for copy in small:
        copy.start()
    for copy in small:
        copy.wait()
    lane = lax.broadcasted_iota(jnp.int32, (1, levels), 1)
    live = [
        jnp.where(jnp.full((1, levels), aggregate[q // 2, q % 2]) >= 0, 1.0, 0.0) for q in range(4)
    ]
    count = live[0] + live[1] + live[2] + live[3]
    scale = jnp.sqrt(jnp.maximum(count, 1.0))
    for q in range(4):
        x, y = q // 2, q % 2
        coupling = vert_coup[x, y : y + 1, :]
        up = jnp.where(lane < levels - 1, coupling, 0.0)
        down = jnp.where(lane > 0, pltpu.roll(coupling, 1, axis=1), 0.0)
        is_open = jnp.full((1, levels), land[x, y]).astype(jnp.float32)
        rows = [
            vert_diag[x, y : y + 1, :] + coupling + down,
            up,
            down,
            face_east[x, y : y + 1, :] * is_open,
            face_north[x, y : y + 1, :] * is_open,
            is_open,
            live[q] / scale,
            jnp.zeros((1, levels), jnp.float32),
        ]
        block = jnp.concatenate(rows, axis=0)
        for ref, base in ((both, 4 * levels), (to_near, 2 * levels), (to_far, 2 * levels)):
            ref[base + q * COEF_ROWS : base + (q + 1) * COEF_ROWS, :] = block
    whole.wait()
    even_lon = lon == 0
    for y in range(2):
        low, high = inverse[0, y], inverse[1, y]
        both[y * levels : (y + 1) * levels, :] = low
        both[(2 + y) * levels : (3 + y) * levels, :] = high
        to_near[y * levels : (y + 1) * levels, :] = jnp.where(even_lon, high, low)
        to_far[y * levels : (y + 1) * levels, :] = jnp.where(even_lon, low, high)


def parities():
    even_lon = lax.rem(lax.axis_index("lon"), 2) == 0
    even_lat = lax.rem(lax.axis_index("lat"), 2) == 0
    return even_lon, even_lat


def has_lat_far():
    index = lax.axis_index("lat")
    return index != jnp.where(lax.rem(index, 2) == 0, 0, lax.axis_size("lat") - 1)


def wide_kernel(facing_far, own, ring, wide):
    even_lon, _ = parities()
    levels = own.shape[1]
    high = jnp.logical_not(even_lon) if facing_far else even_lon
    for y in range(2):
        low_rows = own[y * levels : (y + 1) * levels, :]
        high_rows = own[(2 + y) * levels : (3 + y) * levels, :]
        wide[y * levels : (y + 1) * levels, :] = jnp.where(high, high_rows, low_rows)
    base = 2 * levels
    coef = [ring[base + q * COEF_ROWS : base + (q + 1) * COEF_ROWS, :] for q in range(4)]
    for y in range(2):
        beyond = jnp.where(high, coef[y], coef[2 + y])
        wide[base + y * COEF_ROWS : base + (y + 1) * COEF_ROWS, :] = beyond


def fill_corner(lon_near, lon_far, lat_near, lat_far, out, near):
    even_lon, even_lat = parities()
    levels = lon_near.shape[1]
    base = 2 * levels

    def block(values, q, first=0):
        return values[q * COEF_ROWS + first : q * COEF_ROWS + (WEIGHT + 1 if first else COEF_ROWS), :]

    def sides(rows):
        near, far = lon_near[rows, :], lon_far[rows, :]
        return jnp.where(even_lon, far, near), jnp.where(even_lon, near, far)

    low = sides(slice(0, levels))
    high = sides(slice(levels, base))
    coefs = sides(slice(base, lon_near.shape[0]))
    lat = slice(2 * base, lat_near.shape[0])
    lower = jnp.logical_not(even_lat) if near else even_lat
    other = jnp.where(has_lat_far(), lat_far[lat, :], 0.0) if near else lat_near[lat, :]
    rows = []
    for place, facing in enumerate((1, 0)):
        out[place * levels : (place + 1) * levels, :] = jnp.where(lower, low[place], high[place])
        choices = []
        for y in (0, 1):
            corner, beside, behind = 2 * facing + y, 2 * (1 - facing) + y, 2 * facing + 1 - y
            choices.append(
                [block(coefs[place], corner)]
                + [block(coefs[place], q, EAST) for q in (beside, behind)]
            )
        rows += [jnp.where(lower, *pair) for pair in zip(*choices)]
    for x in (0, 1):
        choices = (block(other, 2 * x + y, EAST) for y in (0, 1))
        rows.append(jnp.where(lower, *choices))
    out[base : base + CORNER_ROWS, :] = jnp.concatenate(rows, axis=0)


def corner_kernel(lon_near, lon_far, lat_near, lat_far, to_far):
    fill_corner(lon_near, lon_far, lat_near, lat_far, to_far, False)


def split(values):
    high = values.astype(jnp.bfloat16)
    return high, (values - high.astype(jnp.float32)).astype(jnp.bfloat16)


def product(left, right):
    return product_of_parts(left, *split(right))


def product_of_parts(left, right_high, right_low):
    left_high, left_low = split(left)
    return jnp.dot(
        jnp.concatenate([left_high, left_high, left_low], axis=1),
        jnp.concatenate([right_high, right_low, right_high], axis=0),
        preferred_element_type=jnp.float32,
    )


def left(values):
    return pltpu.roll(values, 1, axis=1)


def right(values):
    return pltpu.roll(values, values.shape[1] - 1, axis=1)


class Stencil:
    def __init__(self, own, lon_near, lon_far, wide_near, wide_far, lat_near, lat_far, corner_near=None, corner_far=None):
        even_lon, even_lat = parities()
        levels = own.shape[1]
        size = 4 * COEF_ROWS
        full = 4 * levels
        half = 2 * levels
        self.levels = levels
        self.wide = {3: (even_lon, wide_near, wide_far), -2: (even_lon, wide_far, wide_near)}
        sources = {
            (0, 0): (None, own, own, full),
            (1, 0): (even_lon, lon_near, lon_far, half),
            (-1, 0): (even_lon, lon_far, lon_near, half),
            (0, 1): (even_lat, lat_near, lat_far, full),
            (0, -1): (even_lat, lat_far, lat_near, full),
        }
        self.sources = sources
        self.coefs = {place: self.fetch(*source, size) for place, source in sources.items()}
        far = has_lat_far()
        keep = {1: jnp.logical_or(even_lat, far), -1: jnp.logical_or(jnp.logical_not(even_lat), far)}
        for place in sources:
            if place[1] != 0:
                inside = keep[1 if place[1] > 0 else -1]
                self.coefs[place] = jnp.where(inside, self.coefs[place], 0.0)
        self.parts = {}
        if corner_near is not None:
            self.corners = {1: (even_lat, corner_near, corner_far), -1: (even_lat, corner_far, corner_near)}
            for side, source in self.corners.items():
                rows = jnp.where(keep[side], self.fetch(*source, half, CORNER_ROWS), 0.0)
                facing, behind, beyond = (2, 3, 4) if side > 0 else (-1, -2, -3)
                start = 0
                for x, beside in ((-1, -2), (2, 3)):
                    self.parts[x, facing] = (rows, start)
                    self.parts[beside, facing] = (rows, start + COEF_ROWS - EAST)
                    self.parts[x, behind] = (rows, start + COEF_ROWS + 4 - EAST)
                    start += COEF_ROWS + 8
                for x in (0, 1):
                    self.parts[x, beyond] = (rows, start + 4 * x - EAST)
        pair = 2 * COEF_ROWS
        for x, source in self.wide.items() if wide_near is not None else ():
            beyond = self.fetch(*source, half, pair)
            self.coefs[2 if x > 0 else -2, 0] = jnp.concatenate([beyond, beyond], axis=0)
        self.east = functools.cache(self.east)
        self.north = functools.cache(self.north)
        self.main = functools.cache(self.main)

    def fetch(self, flag, first, other, start, count):
        if flag is None:
            return first[start : start + count, :]
        return jnp.where(flag, first[start : start + count, :], other[start : start + count, :])

    def coef(self, x, y, row):
        if (x, y) in self.parts:
            rows, start = self.parts[x, y]
            return rows[start + row : start + row + 1, :]
        at = (2 * (x % 2) + y % 2) * COEF_ROWS + row
        return self.coefs[x // 2, y // 2][at : at + 1, :]

    def weight(self, x, y):
        return self.coef(x, y, WEIGHT)

    def east(self, x, y):
        return self.coef(x, y, EAST) * self.coef(x + 1, y, OPEN)

    def north(self, x, y):
        return self.coef(x, y, NORTH) * self.coef(x, y + 1, OPEN)

    def main(self, x, y):
        lon = self.east(x, y) + self.east(x - 1, y)
        return self.coef(x, y, DIAG) + lon + self.north(x, y) + self.north(x, y - 1)

    def outer_face(self, x, y):
        if x in (0, 1):
            return self.east(x - 1, y) if x == 0 else self.east(x, y)
        return self.north(x, y - 1) if y == 0 else self.north(x, y)

    def inner_main(self, x, y):
        if x in (0, 1):
            inner = self.east(0, y) + self.north(x, y) + self.north(x, y - 1)
        else:
            inner = self.north(x, 0) + self.east(x, y) + self.east(x - 1, y)
        return self.coef(x, y, DIAG) + inner

    def lon_faces(self, x, y):
        above = self.east(x, y) * self.weight(x + 1, y)
        below = self.east(x - 1, y) * self.weight(x - 1, y)
        return (above, below) if x % 2 == 0 else (below, above)

    def lat_faces(self, x, y):
        above = self.north(x, y) * self.weight(x, y + 1)
        below = self.north(x, y - 1) * self.weight(x, y - 1)
        return (above, below) if y % 2 == 0 else (below, above)

    def own_diag(self, x, y):
        return (
            self.weight(x, y) * self.main(x, y) - self.lon_faces(x, y)[0] - self.lat_faces(x, y)[0]
        )

    def inverse(self, x, y):
        lon, lat = x // 2, y // 2
        levels = self.levels
        if x in self.wide:
            return self.fetch(*self.wide[x], y % 2 * levels, levels)
        if lon != 0 and lat != 0:
            return self.fetch(*self.corners[lat], 0 if lon < 0 else levels, levels)
        elif lon != 0:
            start = y % 2 * levels
        else:
            start = (2 * (x % 2) + y % 2) * levels
        return self.fetch(*self.sources[lon, lat][:3], start, levels)

    def residual(self, rows_t, x, y, main=None):
        total = None
        if (x, y) in rows_t:
            block = rows_t[x, y]
            total = (
                block * (self.main if main is None else main)(x, y)
                - left(block * self.coef(x, y, UP))
                - right(block * self.coef(x, y, DOWN))
            )
        for near, face in (
            ((x + 1, y), lambda: self.east(x, y)),
            ((x - 1, y), lambda: self.east(x - 1, y)),
            ((x, y + 1), lambda: self.north(x, y)),
            ((x, y - 1), lambda: self.north(x, y - 1)),
        ):
            if near in rows_t:
                term = rows_t[near] * face()
                total = -term if total is None else total - term
        return total


own_cells = [(x, y) for x in (0, 1) for y in (0, 1)]
lon_cells = [(x, y) for x in (-1, 2) for y in (0, 1)]
lat_cells = [(x, y) for x in (0, 1) for y in (-1, 2)]
near_cells = lon_cells + lat_cells
reach_cells = own_cells + near_cells
lon_far_cells = [(x, y) for x in (-2, 3) for y in (0, 1)]
lat_far_cells = [(x, y) for x in (0, 1) for y in (-2, 3)]
far_cells = lon_far_cells + lat_far_cells
corner_cells = [(2, 2), (2, -1), (-1, 2), (-1, -1)]
groups = {}
for cell in corner_cells + lon_far_cells + lon_cells + lat_far_cells + lat_cells:
    groups.setdefault((cell[0] // 2, cell[1] // 2), []).append(cell)
first_targets = [(0, 0), (1, 0), (-1, 0), (0, 1), (0, -1)]


class Sums:
    def __init__(self, out, targets, started=()):
        self.out = out
        self.slots = {target: place for place, target in enumerate(targets)}
        self.started = set(started)

    def add(self, target, term):
        place = self.slots[target]
        if target in self.started:
            self.out[place] += term
        else:
            self.out[place] = term
            self.started.add(target)


def lateral_targets(x, y):
    lon, lat = x // 2, y // 2
    return (lon + (-1 if x % 2 == 0 else 1), lat), (lon, lat + (-1 if y % 2 == 0 else 1))


def apply_columns(cells, sums, x, y, smooth):
    lon_target, lat_target = lateral_targets(x, y)
    sums.add(lon_target, smooth * cells.lon_faces(x, y)[1])
    sums.add(lat_target, smooth * cells.lat_faces(x, y)[1])
    weight = cells.weight(x, y)
    return (
        smooth * cells.own_diag(x, y),
        smooth * (weight * cells.coef(x, y, UP)),
        smooth * (weight * cells.coef(x, y, DOWN)),
    )


def plus(parts, more):
    return more if parts is None else tuple(a + b for a, b in zip(parts, more))


def close_kernel(own, lon_near, lon_far, lat_near, lat_far, rows_out, smooth_out, partial, rest_out, high_out, low_out, to_near):
    fill_corner(lon_near, lon_far, lat_near, lat_far, to_near, True)
    cells = Stencil(own, lon_near, lon_far, None, None, lat_near, lat_far)
    levels = cells.levels
    row = lax.broadcasted_iota(jnp.int32, (levels, levels), 0)
    lane = lax.broadcasted_iota(jnp.int32, (levels, levels), 1)
    rows_t = {}
    for x, y in own_cells:
        block = cells.inverse(x, y)
        weight = cells.weight(x, y)
        smoothed = (
            block * cells.own_diag(x, y)
            - left(block * (weight * cells.coef(x, y, UP)))
            - right(block * (weight * cells.coef(x, y, DOWN)))
        )
        rows_t[x, y] = (jnp.where(row == lane, weight, 0.0) - relax_weight * smoothed).T
    for x, y in lon_cells:
        rows_t[x, y] = (cells.inverse(x, y) * (relax_weight * cells.lon_faces(x, y)[1])).T
    for x, y in lat_cells:
        rows_t[x, y] = (cells.inverse(x, y) * (relax_weight * cells.lat_faces(x, y)[1])).T
    for place, cell in enumerate(reach_cells):
        rows_out[place] = rows_t[cell]
    sums = Sums(partial, first_targets)
    parts = None
    for x, y in own_cells:
        rest = cells.residual(rows_t, x, y)
        smooth = product(rest, cells.inverse(x, y)) * relax_weight
        terms = apply_columns(cells, sums, x, y, smooth)
        parts = plus(parts, (rest * cells.weight(x, y) - terms[0],) + terms[1:])
    sums.add((0, 0), parts[0] + left(parts[1]) + right(parts[2]))
    for x, y in far_cells:
        rest = cells.residual(rows_t, x, y)
        sums.add((x // 2, y // 2), rest * cells.weight(x, y))
        if (x, y) in lat_far_cells:
            smooth = product(rest, cells.inverse(x, y))
            smooth_out[lat_far_cells.index((x, y))] = smooth
    for place, (x, y) in enumerate(near_cells):
        rest_out[place] = cells.residual(rows_t, x, y, cells.inner_main)
        high_out[place], low_out[place] = split(cells.inverse(x, y))


def wide_products_kernel(own, lon_near, lon_far, wide_near, wide_far, lat_near, lat_far, rows_in, smooth_out):
    cells = Stencil(own, lon_near, lon_far, wide_near, wide_far, lat_near, lat_far)
    rows_t = {cell: rows_in[place] for place, cell in enumerate(reach_cells) if cell in lon_cells}
    for place, (x, y) in enumerate(lon_far_cells):
        rest = cells.residual(rows_t, x, y)
        smooth_out[place] = product(rest, cells.inverse(x, y))


product_cells = corner_cells + near_cells


target_order = [(-2, 0), (2, 0), (0, -2), (0, 2)] + [
    target for target in stencil_offsets if 2 not in target and -2 not in target
]


def coarse_kernel(*refs):
    cells = Stencil(*refs[:9])
    rows_in, lat_smooth, partial, rest_in, high_in, low_in, lon_smooth = refs[9:16]
    out, blocks, rests, smooths, sems = refs[16:]
    levels = cells.levels
    rows_t = {cell: rows_in[place] for place, cell in enumerate(reach_cells)}
    smooth_of, rest_of = {}, {}
    for place, cell in enumerate(lon_far_cells):
        smooth_of[cell] = lon_smooth.at[place]
    for place, cell in enumerate(lat_far_cells):
        smooth_of[cell] = lat_smooth.at[place]
    lateral, own = {}, {}
    for device, members in groups.items():
        for x, y in members:
            lon_target, lat_target = lateral_targets(x, y)
            for target, faces in ((lon_target, cells.lon_faces), (lat_target, cells.lat_faces)):
                lateral.setdefault(target, []).append(((x, y), faces(x, y)[1] * relax_weight))
            weight = cells.weight(x, y) * relax_weight
            factors = (
                cells.own_diag(x, y) * relax_weight,
                weight * cells.coef(x, y, UP),
                weight * cells.coef(x, y, DOWN),
            )
            own.setdefault(device, []).append(((x, y), factors))
    slots = {target: place for place, target in enumerate(stencil_offsets)}
    copies = []
    strip = levels // 4
    for turn, target in enumerate(target_order):
        if turn == 4:
            for place, (x, y) in enumerate(product_cells):
                if (x, y) in near_cells:
                    known = near_cells.index((x, y))
                    rest = rest_in[known] + rows_t[x, y] * cells.outer_face(x, y)
                    smooths[place] = product_of_parts(rest, high_in[known], low_in[known])
                else:
                    rest = cells.residual(rows_t, x, y)
                    smooths[place] = product(rest, cells.inverse(x, y))
                rests[place] = rest
                rest_of[x, y], smooth_of[x, y] = rests.at[place], smooths.at[place]
        for start in range(0, levels, strip):
            rows = slice(start, start + strip)
            total = None
            if target in first_targets:
                total = partial[first_targets.index(target), rows, :]
            for cell, factor in lateral.get(target, ()):
                term = smooth_of[cell][rows, :] * factor
                total = term if total is None else total + term
            parts = None
            for cell, factors in own.get(target, ()):
                smooth = smooth_of[cell][rows, :]
                terms = [smooth * factor for factor in factors]
                if cell in rest_of:
                    terms[0] = terms[0] - rest_of[cell][rows, :] * cells.weight(*cell)
                parts = plus(parts, tuple(terms))
            if parts is not None:
                total = total - parts[0] + left(parts[1]) + right(parts[2])
            blocks[slots[target], rows, :] = total
        place = slots[target]
        copies.append(pltpu.make_async_copy(blocks.at[place], out.at[place], sems.at[place]))
        copies[-1].start()
    for copy in copies:
        copy.wait()


def local(inverse, vert_diag, vert_coup, face_east, face_north, land_mask, aggregate):
    levels = inverse.shape[-1]
    size = 4 * COEF_ROWS
    args = (inverse, vert_diag, vert_coup, face_east, face_north, land_mask, aggregate)
    vmem = pl.BlockSpec(memory_space=pltpu.VMEM)
    params = pltpu.CompilerParams(vmem_limit_bytes=8 * 1024 * 1024)
    array = lambda count: jax.ShapeDtypeStruct((count, levels), jnp.float32)
    cost = lambda size: pl.CostEstimate(flops=size * 10**6, bytes_accessed=size * 10**3, transcendentals=0)
    shapes = [4 * levels + size] + [2 * levels + size] * 2
    both, to_near, to_far = pl.pallas_call(
        pack_kernel,
        out_shape=tuple(pltpu.VMEM((rows, levels), jnp.float32) for rows in shapes),
        in_specs=[pl.BlockSpec(memory_space=pltpu.HBM)] * 7,
        out_specs=(vmem,) * 3,
        scratch_shapes=[pltpu.VMEM(arg.shape, arg.dtype) for arg in args[:5]]
        + [pltpu.SMEM(arg.shape, arg.dtype) for arg in args[5:]]
        + [pltpu.SemaphoreType.DMA((7,))],
        compiler_params=pltpu.CompilerParams(vmem_limit_bytes=8 * 1024 * 1024),
    )(*(pltpu.with_memory_space_constraint(arg, pltpu.HBM) for arg in args))
    lon_near = lax.ppermute(to_near, "lon", pair_near("lon"))
    lon_far = lax.ppermute(to_far, "lon", pair_far_closed("lon"))
    lat_near = lax.ppermute(both, "lat", pair_near("lat"))
    lat_far = exchange_lat_far(both)

    def widened(facing_far, ring, spare, weight):
        return pl.pallas_call(
            functools.partial(wide_kernel, facing_far),
            out_shape=array(2 * (levels + COEF_ROWS) + spare),
            in_specs=[vmem] * 2,
            out_specs=vmem,
            cost_estimate=cost(weight),
            compiler_params=params,
        )(both, ring)

    wide_far = lax.ppermute(widened(False, lon_near, 0, 1000), "lon", pair_far_closed("lon"))
    wide_near = lax.ppermute(widened(True, lon_far, 0, 8000), "lon", pair_near("lon"))
    corner_rows = 2 * levels + CORNER_ROWS
    corner_to_far = pl.pallas_call(
        corner_kernel,
        out_shape=array(corner_rows),
        in_specs=[vmem] * 4,
        out_specs=vmem,
        compiler_params=params,
    )(lon_near, lon_far, lat_near, lat_far)
    corner_far = exchange_lat_far(corner_to_far)
    blocks = lambda count: jax.ShapeDtypeStruct((count, levels, levels), jnp.float32)
    *close, corner_to_near = pl.pallas_call(
        close_kernel,
        out_shape=(
            *(blocks(len(cells)) for cells in (reach_cells, lat_far_cells, first_targets, near_cells)),
            *(jax.ShapeDtypeStruct((len(near_cells), levels, levels), jnp.bfloat16),) * 2,
            array(corner_rows),
        ),
        in_specs=[vmem] * 5,
        out_specs=(vmem,) * 7,
        cost_estimate=cost(1),
        compiler_params=params,
    )(both, lon_near, lon_far, lat_near, lat_far)
    corner_near = lax.ppermute(corner_to_near, "lat", pair_near("lat"))
    near_args = (both, lon_near, lon_far, wide_near, wide_far, lat_near, lat_far)
    lon_smooth = pl.pallas_call(
        wide_products_kernel,
        out_shape=blocks(len(lon_far_cells)),
        in_specs=[vmem] * 8,
        out_specs=vmem,
        cost_estimate=cost(50000),
        compiler_params=params,
    )(*near_args, close[0])
    out = pl.pallas_call(
        coarse_kernel,
        out_shape=blocks(len(stencil_offsets)),
        in_specs=[vmem] * 16,
        out_specs=pl.BlockSpec(memory_space=pltpu.HBM),
        scratch_shapes=[
            pltpu.VMEM((len(stencil_offsets), levels, levels), jnp.float32),
            *(pltpu.VMEM((len(product_cells), levels, levels), jnp.float32),) * 2,
            pltpu.SemaphoreType.DMA((len(stencil_offsets),)),
        ],
        compiler_params=params,
    )(*near_args, corner_near, corner_far, *close, lon_smooth)
    return out[None, None]


def solution(mesh):
    return jax.shard_map(
        local,
        mesh=mesh,
        in_specs=(
            P("lon", "lat", None, None),
            P("lon", "lat", None),
            P("lon", "lat", None),
            P("lon", "lat", None),
            P("lon", "lat", None),
            P("lon", "lat"),
            P("lon", "lat"),
        ),
        out_specs=P("lon", "lat", None, None, None),
        check_vma=False,
    )
```
